32 devices in a mesh: groups: 2 (over y), gx: 4 (over x, core), gy: 4 (over z).
Axes of the slice: x: 2, y: 2, z: 4, core: 2. Of those that a mesh axis runs over, the one named last changes fastest.
Arguments:
- tokens: bfloat16 [1024, 8192], P(('groups', 'gy'), 'gx'), parts along dimension 0, may hold values from -120 to 120
- gate_matrix: bfloat16 [8192, 26624], P('gx', 'gy'), may hold values from -0.0625 to 0.0625
- up_matrix: bfloat16 [8192, 26624], P('gx', 'gy'), may hold values from -0.0625 to 0.0625
- down_matrix: bfloat16 [26624, 8192], P('gy', 'gx'), may hold values from -0.0390625 to 0.0390625
Outputs:
- mixed: bfloat16 [1024, 8192], P(('groups', 'gy'), 'gx'), parts along dimension 0
The draws below stay inside these ranges and needn't reach their ends.
There are 2 independent parts, one for each index of `groups`. The reference program is written for one: setup_inputs(seed, part) draws one part's arguments, and reference() takes and returns one part's arrays. A program takes and returns all parts, laid end to end along the dimension named above; an argument that names none is the same for every part. Nothing has to cross between parts.
All inputs are finite; a program needn't handle non-finite values.
Results may differ from the reference program's by a relative error of at most 0.019.
Values may be sent and summed in bfloat16 or wider, within the bound.
No kernel may reach another device: no remote copies, remote signals or barrier semaphores. Data moves between devices by JAX's collectives and lax.ppermute only.
A program may use at most 256 MiB of HBM per device.

```python
import jax
import jax.numpy as jnp
from jax import lax

D = 8192
FF = 26624
BATCH = 512
N_GX = 4


def draw_tokens(key, part):
    key = jax.random.fold_in(key, 11)
    key_noise, key_rows = jax.random.split(key)
    column = jnp.arange(D, dtype=jnp.float32) / D
    column_scale = jnp.exp(jnp.log(3.0) * column)[None, :]
    row_scale = jnp.exp(jax.random.uniform(key_rows, (BATCH, 1), jnp.float32, 0.0, jnp.log(10.0)))
    noise = jnp.clip(jax.random.normal(key_noise, (BATCH, D), jnp.float32), -4.0, 4.0)
    return (noise * column_scale * row_scale).astype(jnp.bfloat16)


def steps_of(stream_key, extent, pieces, smallest, top_value):
    loudness, own = 1.0, jax.random.fold_in(stream_key, 6)
    for position, shards_of in pieces:
        steps = jnp.exp(jax.random.uniform(jax.random.fold_in(own, position), (shards_of,), jnp.float32, smallest / len(pieces), top_value / len(pieces)))
        loudness = loudness * jnp.repeat(steps, extent[position] // shards_of).reshape([-1 if axis == position else 1 for axis in range(len(extent))])
    return loudness


def bell_draw(own_key, shape, deviation, most, cuts=(), held_as=jnp.bfloat16):
    drawn = jax.random.normal(own_key, shape, jnp.float32) * deviation
    if len(cuts) > 0:
        drawn = steps_of(own_key, shape, cuts, -0.22, 0.18) * drawn
    return jnp.clip(drawn, min=-most, max=most).astype(held_as)


def setup_inputs(seed: int = 0, part: int = 0) -> dict:
    streams_of = jax.random.split(jax.random.key(seed), 5)
    own_keys = jax.random.split(jax.random.fold_in(streams_of[4], part), 5)
    return {
        "tokens": draw_tokens(jax.random.fold_in(jax.random.fold_in(streams_of[4], part), 71), part),
        "gate_matrix": bell_draw(streams_of[1], (D, FF), D ** -0.5, 0.0625, ((0, 4), (1, 4))),
        "up_matrix": bell_draw(streams_of[2], (D, FF), D ** -0.5, 0.0625, ((0, 4), (1, 4))),
        "down_matrix": bell_draw(streams_of[3], (FF, D), FF ** -0.5, 0.0390625, ((0, 4), (1, 4))),
    }


def reference(tokens, gate_matrix, up_matrix, down_matrix):
    values = tokens.astype(jnp.float32)
    meansq = lax.optimization_barrier(jnp.mean(values * values, axis=1, keepdims=True))
    normed = (values * lax.rsqrt(meansq + 1e-05)).astype(jnp.bfloat16)
    block = D // N_GX

    def add_block(index, carry):
        gate_total, up_total = carry
        start = index * block
        rows = lax.dynamic_slice_in_dim(normed, start, block, 1)
        gate_rows = lax.dynamic_slice_in_dim(gate_matrix, start, block, 0)
        up_rows = lax.dynamic_slice_in_dim(up_matrix, start, block, 0)
        gate_piece = jnp.dot(rows, gate_rows, preferred_element_type=jnp.float32).astype(jnp.bfloat16)
        up_piece = jnp.dot(rows, up_rows, preferred_element_type=jnp.float32).astype(jnp.bfloat16)
        gate_piece, up_piece = lax.optimization_barrier((gate_piece, up_piece))
        return (gate_total + gate_piece.astype(jnp.float32), up_total + up_piece.astype(jnp.float32))
    empty = jnp.zeros((tokens.shape[0], FF), jnp.float32)
    gate, up_sum = lax.fori_loop(0, N_GX, add_block, (empty, empty))
    hidden = (jax.nn.silu(gate) * up_sum).astype(jnp.bfloat16)
    return jnp.dot(hidden, down_matrix, preferred_element_type=jnp.float32).astype(jnp.bfloat16)
```

```python
import functools

import jax
import jax.numpy as jnp
from jax import lax
from jax.experimental import pallas as pl
from jax.experimental.pallas import tpu as pltpu
from jax.sharding import PartitionSpec as P

D = 8192
EPS = 1e-05
LANES = 128
GU_TILE = 256
OUT_TILE = 512
VMEM_LIMIT = 64 * 1024 * 1024 - 64 * 1024
ANY = pl.BlockSpec(memory_space=pl.ANY)
SMEM = pl.BlockSpec(memory_space=pltpu.SMEM)
VMEM = pl.BlockSpec(memory_space=pltpu.VMEM)


def swap(value, axis, size, mask):
    return lax.ppermute(value, axis, [(i, i ^ mask) for i in range(size)])


def silu_product(gate, up, scale):
    gate = gate * scale
    return gate / (1.0 + jnp.exp(-gate)) * (up * scale)


def gu_kernel(n_tok, n_recv, width, with_hidden, start_ref, *refs):
    toks = refs[:n_tok]
    gate_ref, up_ref = refs[n_tok : n_tok + 2]
    recvs = refs[n_tok + 2 : n_tok + 2 + n_recv]
    at = n_tok + 2 + n_recv
    scale_ref = refs[at] if with_hidden else None
    at += 1 if with_hidden else 0
    out_ref, xbuf, wbuf, rbuf, obuf, xsem, wsem, rsem, osem = refs[at + 1 :]
    full, rest = divmod(width, GU_TILE)
    base = pl.multiple_of(start_ref[0], LANES)

    def weights(j, n):
        columns = pl.ds(pl.multiple_of(base + j * GU_TILE, LANES), n)
        return (
            pltpu.make_async_copy(gate_ref.at[:, columns], wbuf.at[j, :, pl.ds(0, n)], wsem.at[0, j]),
            pltpu.make_async_copy(up_ref.at[:, columns], wbuf.at[j, :, pl.ds(n, n)], wsem.at[1, j]),
        )

    def receive(r, j, n):
        columns = pl.ds(pl.multiple_of(j * GU_TILE, LANES), n)
        return pltpu.make_async_copy(recvs[r].at[:, :, columns], rbuf.at[r, j, :, :, pl.ds(0, n)], rsem.at[r, j])

    def write(j, n):
        columns = pl.ds(pl.multiple_of(j * GU_TILE, LANES), n)
        if with_hidden:
            return pltpu.make_async_copy(obuf.at[j, 0, :, pl.ds(0, n)], out_ref.at[:, columns], osem.at[j])
        return pltpu.make_async_copy(obuf.at[j, :, :, pl.ds(0, n)], out_ref.at[:, :, columns], osem.at[j])

    copies, row = [], 0
    for i, tok in enumerate(toks):
        copies.append(pltpu.make_async_copy(tok, xbuf.at[pl.ds(row, tok.shape[0])], xsem.at[i]))
        row += tok.shape[0]
    for copy in copies:
        copy.start()

    def begin(j, n):
        for copy in weights(j, n):
            copy.start()
        for r in range(n_recv):
            receive(r, j, n).start()

    def over_tiles(step):
        if full:
            @pl.loop(0, full)
            def _(j):
                step(j, GU_TILE)
        if rest:
            step(full, rest)

    def multiply(j, n):
        for copy in weights(j, n):
            copy.wait()
        both = jnp.dot(xbuf[...], wbuf[j, :, pl.ds(0, 2 * n)], preferred_element_type=jnp.float32)
        gate, up = both[:, :n], both[:, n:]
        for r in range(n_recv):
            receive(r, j, n).wait()
            gate = gate + rbuf[r, j, 0, :, pl.ds(0, n)].astype(jnp.float32)
            up = up + rbuf[r, j, 1, :, pl.ds(0, n)].astype(jnp.float32)
        if with_hidden:
            obuf[j, 0, :, pl.ds(0, n)] = silu_product(gate, up, scale_ref[...]).astype(jnp.bfloat16)
        else:
            obuf[j, 0, :, pl.ds(0, n)] = gate.astype(jnp.bfloat16)
            obuf[j, 1, :, pl.ds(0, n)] = up.astype(jnp.bfloat16)
        write(j, n).start()

    over_tiles(begin)
    for copy in copies:
        copy.wait()
    over_tiles(multiply)
    over_tiles(lambda j, n: write(j, n).wait())


def gate_up(toks, gate_matrix, up_matrix, start, width, recvs, scale, dep):
    rows, depth = sum(t.shape[0] for t in toks), gate_matrix.shape[0]
    with_hidden = scale is not None
    if width % LANES:
        tok = jnp.concatenate(toks, axis=0)
        gate, up = (
            jnp.dot(tok, lax.dynamic_slice_in_dim(m, start, width, 1), preferred_element_type=jnp.float32)
            for m in (gate_matrix, up_matrix)
        )
        for r in recvs:
            gate, up = gate + r[0].astype(jnp.float32), up + r[1].astype(jnp.float32)
        if with_hidden:
            return silu_product(gate, up, scale).astype(jnp.bfloat16)
        return jnp.stack([gate, up]).astype(jnp.bfloat16)
    tiles = pl.cdiv(width, GU_TILE)
    kernel = functools.partial(gu_kernel, len(toks), len(recvs), width, with_hidden)
    shape = (rows, width) if with_hidden else (2, rows, width)
    n_recv = max(len(recvs), 1)
    return pl.pallas_call(
        kernel,
        out_shape=jax.ShapeDtypeStruct(shape, jnp.bfloat16),
        in_specs=[SMEM] + [ANY] * (len(toks) + 2 + len(recvs)) + [VMEM] * with_hidden + [ANY],
        out_specs=ANY,
        scratch_shapes=[
            pltpu.VMEM((rows, depth), jnp.bfloat16),
            pltpu.VMEM((tiles, depth, 2 * GU_TILE), jnp.bfloat16),
            pltpu.VMEM((n_recv, tiles if recvs else 1, 2, rows if recvs else 16, GU_TILE), jnp.bfloat16),
            pltpu.VMEM((tiles, 1 if with_hidden else 2, rows, GU_TILE), jnp.bfloat16),
            pltpu.SemaphoreType.DMA((len(toks),)),
            pltpu.SemaphoreType.DMA((2, tiles)),
            pltpu.SemaphoreType.DMA((n_recv, tiles)),
            pltpu.SemaphoreType.DMA((tiles,)),
        ],
        compiler_params=pltpu.CompilerParams(vmem_limit_bytes=VMEM_LIMIT),
        cost_estimate=pl.CostEstimate(
            flops=4 * rows * depth * width,
            bytes_accessed=4 * depth * width + 2 * rows * depth + 4 * rows * width * (1 + len(recvs)),
            transcendentals=0,
        ),
        name="gate_up",
    )(
        start.astype(jnp.int32).reshape(1), *toks, gate_matrix, up_matrix, *recvs,
        *([scale] if with_hidden else []), dep,
    )


def down_kernel(n_pieces, with_total, starts_ref, *refs):
    pieces, down_ref = refs[:n_pieces], refs[n_pieces]
    at = n_pieces + 1
    total_ref = refs[at] if with_total else None
    at += 1 if with_total else 0
    out_ref = refs[at + 1]
    at += 2
    hbufs, dbufs = refs[at : at + n_pieces], refs[at + n_pieces : at + 2 * n_pieces]
    tbuf, obuf, hsem, dsem, tsem, osem = refs[at + 2 * n_pieces :]
    tiles, tile = obuf.shape[0], obuf.shape[2]

    def columns(j):
        return pl.ds(pl.multiple_of(j * tile, LANES), tile)

    def weights(p, j):
        rows = pl.ds(pl.multiple_of(starts_ref[p], LANES), dbufs[p].shape[1])
        return pltpu.make_async_copy(down_ref.at[rows, columns(j)], dbufs[p].at[j], dsem.at[p, j])

    def total(j):
        return pltpu.make_async_copy(total_ref.at[:, columns(j)], tbuf.at[j], tsem.at[j])

    def write(j):
        return pltpu.make_async_copy(obuf.at[j], out_ref.at[:, columns(j)], osem.at[j])

    copies = [pltpu.make_async_copy(pieces[p], hbufs[p], hsem.at[p]) for p in range(n_pieces)]
    for copy in copies:
        copy.start()

    @pl.loop(0, tiles)
    def _(j):
        for p in range(n_pieces):
            weights(p, j).start()
        if with_total:
            total(j).start()

    for copy in copies:
        copy.wait()

    @pl.loop(0, tiles)
    def _(j):
        result = None
        for p in range(n_pieces):
            weights(p, j).wait()
            term = jnp.dot(hbufs[p][...], dbufs[p][j], preferred_element_type=jnp.float32)
            result = term if result is None else result + term
        if with_total:
            total(j).wait()
            result = result + tbuf[j]
        obuf[j] = result.astype(obuf.dtype)
        write(j).start()

    @pl.loop(0, tiles)
    def _(j):
        write(j).wait()


def down_product(pieces, starts, down_matrix, total, out_dtype, dep):
    rows, columns = pieces[0].shape[0], down_matrix.shape[1]
    if any(p.shape[1] % LANES for p in pieces) or columns % LANES:
        result = sum(
            jnp.dot(p, lax.dynamic_slice_in_dim(down_matrix, s, p.shape[1], 0), preferred_element_type=jnp.float32)
            for p, s in zip(pieces, starts)
        )
        return (result if total is None else result + total).astype(out_dtype)
    tile = OUT_TILE if columns % OUT_TILE == 0 else LANES
    tiles = columns // tile
    with_total = total is not None
    depth = sum(p.shape[1] for p in pieces)
    return pl.pallas_call(
        functools.partial(down_kernel, len(pieces), with_total),
        out_shape=jax.ShapeDtypeStruct((rows, columns), out_dtype),
        in_specs=[SMEM] + [ANY] * (len(pieces) + 2 + with_total),
        out_specs=ANY,
        scratch_shapes=[pltpu.VMEM(p.shape, jnp.bfloat16) for p in pieces]
        + [pltpu.VMEM((tiles, p.shape[1], tile), jnp.bfloat16) for p in pieces]
        + [
            pltpu.VMEM((tiles, rows, tile) if with_total else (1, 8, LANES), jnp.float32),
            pltpu.VMEM((tiles, rows, tile), out_dtype),
            pltpu.SemaphoreType.DMA((len(pieces),)),
            pltpu.SemaphoreType.DMA((len(pieces), tiles)),
            pltpu.SemaphoreType.DMA((tiles,)),
            pltpu.SemaphoreType.DMA((tiles,)),
        ],
        compiler_params=pltpu.CompilerParams(vmem_limit_bytes=VMEM_LIMIT),
        cost_estimate=pl.CostEstimate(
            flops=2 * rows * depth * columns,
            bytes_accessed=2 * depth * columns + 2 * rows * (depth + 2 * columns),
            transcendentals=0,
        ),
        name="down",
    )(jnp.stack(starts).astype(jnp.int32), *pieces, down_matrix, *([total] if with_total else []), dep)


def on_device(n_gx, n_gy, tokens, gate_matrix, up_matrix, down_matrix):
    features = tokens.shape[1] * n_gx
    width = gate_matrix.shape[1] // n_gx
    me = lax.axis_index("gx")
    far = [2 * k for k in range(1, n_gx // 2)]

    def core(value):
        return swap(value, "gx", n_gx, 1)

    def summed_squares(toks):
        values = jnp.concatenate(toks, axis=0).astype(jnp.float32)
        total = jnp.sum(values * values, axis=1)
        mask = 1
        while mask < n_gx:
            total = total + swap(total, "gx", n_gx, mask)
            mask *= 2
        return lax.rsqrt(total / features + EPS)[:, None]

    blocks = {0: tokens}
    mask = n_gy // 2
    while mask:
        for j in list(blocks):
            blocks[j ^ mask] = swap(blocks[j], "gy", n_gy, mask)
        mask //= 2

    half = (width // LANES + 1) // 2 * LANES if width % LANES == 0 else width // 2
    groups = [[0], list(range(2, n_gy)), [1]]
    scales = [summed_squares([blocks[j] for j in group]) for group in groups]
    jobs = [(0, 0, width), (1, 0, half), (1, half, width - half), (2, 0, width)]
    state = [dict() for _ in jobs]
    chain = [tokens]

    def product(job, piece, recvs, scale=None):
        group, low, n = jobs[job]
        toks = [blocks[j] for j in groups[group]]
        result = gate_up(toks, gate_matrix, up_matrix, piece * width + low, n, recvs, scale, chain[0])
        chain[0] = result
        return result

    def front(job):
        st = state[job]
        lent = [core(product(job, (me ^ k) ^ 1, [])) for k in far]
        st["lent"] = core(product(job, me ^ 1, []))
        st["far"] = [
            swap(product(job, me ^ k, [r]), "gx", n_gx, k) for k, r in zip(far, lent)
        ]

    def own(job):
        st = state[job]
        st["own"] = product(job, me, [st["lent"]])

    def finish(job, fused):
        st = state[job]
        scale = scales[jobs[job][0]]
        if fused:
            hidden = product(job, me, [st["lent"], *st["far"]], scale)
        else:
            both = [r.astype(jnp.float32) for r in [st["own"], *st["far"]]]
            gate, up = sum(b[0] for b in both), sum(b[1] for b in both)
            hidden = silu_product(gate, up, scale).astype(jnp.bfloat16)
        st["near"] = [(hidden, me), (core(hidden), me ^ 1)]
        over = [(swap(hidden, "gx", n_gx, k), me ^ k) for k in far]
        st["over"] = over + [(core(h), q ^ 1) for h, q in over]

    def down(job, pieces, total, dtype):
        low = jobs[job][1]
        result = down_product(
            [h for h, _ in pieces], [q * width + low for _, q in pieces], down_matrix, total, dtype, chain[0]
        )
        chain[0] = result
        return result

    def down_all(job, total, dtype):
        return down(job, state[job]["near"] + state[job]["over"], total, dtype)

    front(0)
    own(0)
    front(1)
    finish(0, False)
    front(2)
    finish(1, True)
    result = down_all(0, None, jnp.float32)
    front(3)
    finish(2, True)
    part = down_all(1, None, jnp.float32)
    own(3)
    part = down_all(2, part, jnp.bfloat16)
    finish(3, False)

    rows = tokens.shape[0]
    parts = {j: part[i * rows : (i + 1) * rows] for i, j in enumerate(groups[1])}
    parts[0] = result
    mask = 1
    while mask < n_gy:
        for j in [j for j in parts if j & mask]:
            arrived = swap(parts.pop(j), "gy", n_gy, mask).astype(jnp.float32)
            total = parts[j ^ mask].astype(jnp.float32) + arrived
            parts[j ^ mask] = total if j == mask else total.astype(jnp.bfloat16)
        mask *= 2

    last = down(3, state[3]["near"], None, jnp.float32)
    last = down(3, state[3]["over"], last, jnp.bfloat16)
    last = swap(last, "gy", n_gy, 1).astype(jnp.float32)
    return (parts[0] + last).astype(jnp.bfloat16)


def solution(mesh):
    n_gx, n_gy = mesh.shape["gx"], mesh.shape["gy"]
    placed = (P(("groups", "gy"), "gx"), P("gx", "gy"), P("gx", "gy"), P("gy", "gx"))
    return jax.shard_map(
        functools.partial(on_device, n_gx, n_gy),
        mesh=mesh,
        in_specs=placed,
        out_specs=P(("groups", "gy"), "gx"),
        check_vma=False,
    )
```

```python
import functools

import jax
import jax.numpy as jnp
from jax import lax
from jax.experimental import pallas as pl
from jax.experimental.pallas import tpu as pltpu
from jax.sharding import PartitionSpec as P

EPS = 1e-05
LANES = 128
GU_TILE = 256
OUT_TILE = 256
AHEAD = 3
SLOTS = AHEAD + 1
VMEM_LIMIT = 64 * 1024 * 1024 - 64 * 1024
ANY = pl.BlockSpec(memory_space=pl.ANY)
SMEM = pl.BlockSpec(memory_space=pltpu.SMEM)
VMEM = pl.BlockSpec(memory_space=pltpu.VMEM)


def swap(value, axis, size, mask):
    return lax.ppermute(value, axis, [(i, i ^ mask) for i in range(size)])


def silu_product(gate, up, scale):
    gate = gate * scale
    return gate / (1.0 + jnp.exp(-gate)) * (up * scale)


class GateUp:
    def __init__(self, toks, block, starts, width, recvs=(), scale=None):
        self.toks, self.block, self.width, self.recvs, self.scale = toks, block, width, list(recvs), scale
        self.columns, self.starts = starts, [*starts, *[row for _, row in toks]]
        self.rows = block * len(toks)
        shape = (self.rows, width * len(starts))
        self.outs = [jax.ShapeDtypeStruct(shape if scale is not None else (2, *shape), jnp.bfloat16)]

    def plain(self, gate_matrix, up_matrix, down_matrix):
        tok = jnp.concatenate([lax.dynamic_slice_in_dim(t, row, self.block, 0) for t, row in self.toks], axis=0)
        gate, up = (
            jnp.dot(
                tok,
                jnp.concatenate([lax.dynamic_slice_in_dim(m, s, self.width, 1) for s in self.columns], axis=1),
                preferred_element_type=jnp.float32,
            )
            for m in (gate_matrix, up_matrix)
        )
        for r, low in self.recvs:
            r = r[:, :, low : low + self.width].astype(jnp.float32)
            gate, up = gate + r[0], up + r[1]
        if self.scale is not None:
            return [silu_product(gate, up, self.scale).astype(jnp.bfloat16)]
        return [jnp.stack([gate, up]).astype(jnp.bfloat16)]

    def fits(self, down_matrix):
        return self.width % LANES == 0 and self.block % 16 == 0

    def arrays(self):
        return [*[t for t, _ in self.toks], *[r for r, _ in self.recvs]]

    def scratch(self, depth):
        pieces, tiles = len(self.columns), pl.cdiv(self.width, GU_TILE)
        return [
            pltpu.VMEM((self.rows, depth), jnp.bfloat16),
            pltpu.VMEM((max(len(self.recvs), 1), tiles, 2, self.rows if self.recvs else 16, GU_TILE), jnp.bfloat16),
            pltpu.VMEM((pieces * tiles, 2 if self.scale is None else 1, self.rows, GU_TILE), jnp.bfloat16),
            pltpu.SemaphoreType.DMA((len(self.toks),)),
            pltpu.SemaphoreType.DMA((max(len(self.recvs), 1), tiles)),
            pltpu.SemaphoreType.DMA((pieces * tiles,)),
        ]

    def bind(self, ctx, arrays, scale_ref, starts, outs, scratch):
        gate_ref, up_ref, wbuf, wsem, base = ctx["gate"], ctx["up"], ctx["wbuf"], ctx["wsem"], ctx["tiles"]
        xbuf, rbuf, obuf, xsem, rsem, osem = scratch
        toks, recvs = arrays[: len(self.toks)], arrays[len(self.toks) :]
        lows, width, pieces, hidden = [low for _, low in self.recvs], self.width, len(self.columns), self.scale is not None
        out_ref = outs[0]
        full, rest = divmod(width, GU_TILE)
        tiles = full + (rest > 0)
        ctx["tiles"] += pieces * tiles

        def weights(p, j, n):
            slot = (base + p * tiles + j) % SLOTS
            columns = pl.ds(pl.multiple_of(starts(p) + j * GU_TILE, LANES), n)
            return (
                pltpu.make_async_copy(gate_ref.at[:, columns], wbuf.at[slot, :, pl.ds(0, n)], wsem.at[0, slot]),
                pltpu.make_async_copy(up_ref.at[:, columns], wbuf.at[slot, :, pl.ds(n, n)], wsem.at[1, slot]),
            )

        def receive(r, j, n):
            columns = pl.ds(pl.multiple_of(lows[r] + j * GU_TILE, LANES), n)
            return pltpu.make_async_copy(recvs[r].at[:, :, columns], rbuf.at[r, j, :, :, pl.ds(0, n)], rsem.at[r, j])

        def write(p, j, n):
            t = p * tiles + j
            columns = pl.ds(pl.multiple_of(p * width + j * GU_TILE, LANES), n)
            if hidden:
                return pltpu.make_async_copy(obuf.at[t, 0, :, pl.ds(0, n)], out_ref.at[:, columns], osem.at[t])
            return pltpu.make_async_copy(obuf.at[t, :, :, pl.ds(0, n)], out_ref.at[:, :, columns], osem.at[t])

        def begin(p, j, n):
            for copy in weights(p, j, n):
                copy.start()
            for r in range(len(recvs)):
                receive(r, j, n).start()

        def begin_tile(t):
            if isinstance(t, int):
                if t < pieces * tiles:
                    begin(t // tiles, t % tiles, GU_TILE if t % tiles < full else rest)
                return
            p, j = t // tiles, t % tiles

            if full:
                @pl.when((p < pieces) & (j < full))
                def _():
                    begin(p, j, GU_TILE)

            if rest:
                @pl.when((p < pieces) & (j == full))
                def _():
                    begin(p, full, rest)

        block, copies = self.block, []
        for i, tok in enumerate(toks):
            rows = pl.ds(pl.multiple_of(starts(pieces + i), 16), block)
            copies.append(pltpu.make_async_copy(tok.at[rows], xbuf.at[pl.ds(i * block, block)], xsem.at[i]))

        def prefetch():
            for copy in copies:
                copy.start()
            for t in range(AHEAD):
                begin_tile(t)

        def multiply(p, j, n):
            slot = (base + p * tiles + j) % SLOTS
            for copy in weights(p, j, n):
                copy.wait()
            both = jnp.dot(xbuf[...], wbuf[slot, :, pl.ds(0, 2 * n)], preferred_element_type=jnp.float32)
            begin_tile(p * tiles + j + AHEAD)
            gate, up = both[:, :n], both[:, n:]
            for r in range(len(recvs)):
                receive(r, j, n).wait()
                gate = gate + rbuf[r, j, 0, :, pl.ds(0, n)].astype(jnp.float32)
                up = up + rbuf[r, j, 1, :, pl.ds(0, n)].astype(jnp.float32)
            t = p * tiles + j
            if hidden:
                obuf[t, 0, :, pl.ds(0, n)] = silu_product(gate, up, scale_ref[...]).astype(jnp.bfloat16)
            else:
                obuf[t, 0, :, pl.ds(0, n)] = gate.astype(jnp.bfloat16)
                obuf[t, 1, :, pl.ds(0, n)] = up.astype(jnp.bfloat16)
            write(p, j, n).start()

        def compute(then):
            for copy in copies:
                copy.wait()
            for p in range(pieces):
                last = p == pieces - 1
                looped = full - 1 if last and not rest else full
                if looped:
                    @pl.loop(0, looped)
                    def _(j):
                        multiply(p, j, GU_TILE)
                if last:
                    then()
                if last and not rest:
                    multiply(p, full - 1, GU_TILE)
                elif rest:
                    multiply(p, full, rest)

        def drain():
            for p in range(pieces):
                if full:
                    @pl.loop(0, full)
                    def _(j):
                        write(p, j, GU_TILE).wait()
                if rest:
                    write(p, full, rest).wait()

        return prefetch, compute, drain


class Down:
    def __init__(self, pieces, starts, total, block, columns, dtype):
        self.pieces, self.starts, self.total, self.block, self.dtype = pieces, starts, total, block, dtype
        self.rows, self.columns, self.scale = pieces[0].shape[0], columns, None
        self.outs = [jax.ShapeDtypeStruct((block, columns), dtype) for _ in range(self.rows // block)]

    def plain(self, gate_matrix, up_matrix, down_matrix):
        result = sum(
            jnp.dot(p, lax.dynamic_slice_in_dim(down_matrix, s, p.shape[1], 0), preferred_element_type=jnp.float32)
            for p, s in zip(self.pieces, self.starts)
        )
        if self.total is not None:
            result = result + jnp.concatenate(self.total, axis=0)
        return jnp.split(result.astype(self.dtype), len(self.outs))

    def fits(self, down_matrix):
        return all(p.shape[1] % LANES == 0 for p in self.pieces) and self.columns % OUT_TILE == 0

    def arrays(self):
        return [*self.pieces, *(self.total or [])]

    def scratch(self, depth):
        tiles, n = self.columns // OUT_TILE, len(self.pieces)
        return [
            *[pltpu.VMEM(p.shape, jnp.bfloat16) for p in self.pieces],
            *[pltpu.VMEM((SLOTS, p.shape[1], OUT_TILE), jnp.bfloat16) for p in self.pieces],
            pltpu.VMEM((SLOTS, self.rows, OUT_TILE) if self.total else (1, 8, LANES), jnp.float32),
            pltpu.VMEM((tiles, self.rows, OUT_TILE), self.dtype),
            pltpu.SemaphoreType.DMA((n,)),
            pltpu.SemaphoreType.DMA((n, SLOTS)),
            pltpu.SemaphoreType.DMA((len(self.outs), SLOTS)),
            pltpu.SemaphoreType.DMA((len(self.outs), tiles)),
        ]

    def bind(self, ctx, arrays, scale_ref, starts, outs, scratch):
        n, tiles, block = len(self.pieces), self.columns // OUT_TILE, self.block
        pieces, totals = arrays[:n], arrays[n:]
        hbufs, dbufs = scratch[:n], scratch[n : 2 * n]
        tbuf, obuf, hsem, dsem, tsem, osem = scratch[2 * n :]
        down_ref = ctx["down"]

        def columns(j):
            return pl.ds(pl.multiple_of(j * OUT_TILE, LANES), OUT_TILE)

        def weights(p, j):
            rows = pl.ds(pl.multiple_of(starts(p), LANES), dbufs[p].shape[1])
            return pltpu.make_async_copy(down_ref.at[rows, columns(j)], dbufs[p].at[j % SLOTS], dsem.at[p, j % SLOTS])

        def total(i, j):
            slot = j % SLOTS
            return pltpu.make_async_copy(
                totals[i].at[:, columns(j)], tbuf.at[slot, pl.ds(i * block, block)], tsem.at[i, slot]
            )

        def write(i, j):
            return pltpu.make_async_copy(
                obuf.at[j, pl.ds(i * block, block)], outs[i].at[:, columns(j)], osem.at[i, j]
            )

        def begin(j):
            for p in range(n):
                weights(p, j).start()
            for i in range(len(totals)):
                total(i, j).start()

        copies = [pltpu.make_async_copy(pieces[p], hbufs[p], hsem.at[p]) for p in range(n)]

        def prefetch():
            for copy in copies:
                copy.start()
            for j in range(min(AHEAD, tiles)):
                begin(j)

        def multiply(j):
            result = None
            for p in range(n):
                weights(p, j).wait()
                term = jnp.dot(hbufs[p][...], dbufs[p][j % SLOTS], preferred_element_type=jnp.float32)
                result = term if result is None else result + term
            if isinstance(j, int):
                if j + AHEAD < tiles:
                    begin(j + AHEAD)
            else:
                @pl.when(j + AHEAD < tiles)
                def _():
                    begin(j + AHEAD)
            for i in range(len(totals)):
                total(i, j).wait()
            if totals:
                result = result + tbuf[j % SLOTS]
            obuf[j] = result.astype(obuf.dtype)
            for i in range(len(outs)):
                write(i, j).start()

        def compute(then):
            for copy in copies:
                copy.wait()

            @pl.loop(0, tiles - 1)
            def _(j):
                multiply(j)

            then()
            multiply(tiles - 1)

        def drain():
            @pl.loop(0, tiles)
            def _(j):
                for i in range(len(outs)):
                    write(i, j).wait()

        return prefetch, compute, drain


def run(phases, gate_matrix, up_matrix, down_matrix, dep):
    if not all(p.fits(down_matrix) for p in phases):
        return [p.plain(gate_matrix, up_matrix, down_matrix) for p in phases]
    depth = gate_matrix.shape[0]
    operands = [gate_matrix, up_matrix, down_matrix]

    def index(array):
        for i, known in enumerate(operands):
            if known is array:
                return i
        operands.append(array)
        return len(operands) - 1

    where = [[index(a) for a in p.arrays()] for p in phases]
    index(dep)
    scales = [p.scale for p in phases if p.scale is not None]
    starts = [s for p in phases for s in p.starts]
    outs = [o for p in phases for o in p.outs]
    scratch = [p.scratch(depth) for p in phases]
    any_gate_up = any(isinstance(p, GateUp) for p in phases)

    def kernel(starts_ref, *refs):
        refs = list(refs)
        arrays = [refs.pop(0) for _ in operands]
        scale_refs = [refs.pop(0) for _ in scales]
        out_refs = [refs.pop(0) for _ in outs]
        ctx = {"gate": arrays[0], "up": arrays[1], "down": arrays[2], "tiles": 0}
        ctx["wbuf"], ctx["wsem"] = refs.pop(0), refs.pop(0)
        bound, first = [], 0
        for p, places, buffers in zip(phases, where, scratch):
            scale_ref = scale_refs.pop(0) if p.scale is not None else None
            mine = [out_refs.pop(0) for _ in p.outs]
            held = [refs.pop(0) for _ in buffers]
            start = functools.partial(lambda low, i: starts_ref[low + i], first)
            first += len(p.starts)
            bound.append(p.bind(ctx, [arrays[i] for i in places], scale_ref, start, mine, held))
        bound[0][0]()
        for i, (_, compute, _) in enumerate(bound):
            compute(bound[i + 1][0] if i + 1 < len(bound) else lambda: None)
        for _, _, drain in bound:
            drain()

    results = pl.pallas_call(
        kernel,
        out_shape=outs,
        in_specs=[SMEM] + [ANY] * len(operands) + [VMEM] * len(scales),
        out_specs=[ANY] * len(outs),
        scratch_shapes=[
            pltpu.VMEM((SLOTS, depth, 2 * GU_TILE) if any_gate_up else (1, 16, LANES), jnp.bfloat16),
            pltpu.SemaphoreType.DMA((2, SLOTS)),
            *[buffer for buffers in scratch for buffer in buffers],
        ],
        compiler_params=pltpu.CompilerParams(vmem_limit_bytes=VMEM_LIMIT),
        cost_estimate=pl.CostEstimate(flops=WORK, bytes_accessed=1024, transcendentals=0),
        name="step_" + "".join("g" if isinstance(p, GateUp) else "d" for p in phases),
    )(jnp.stack(starts).astype(jnp.int32), *operands, *scales)
    results, split = list(results), []
    for p in phases:
        split.append([results.pop(0) for _ in p.outs])
    return split


WORK = 10**3
STEPS = (
    "s0",
    "s1",
    "x0",
    "x1",
    "h0",
    "h1",
    "r0 s2",
    "r1 s3",
    "x2",
    "x3 s4 s5 d0 d1",
    "h2",
    "h3",
    "r2 x4 x5",
    "r3 d2 d3",
    "h4",
    "h5",
    "r4 d4",
    "r5 d5",
)


def cut(width, part, parts):
    unit = LANES if width % LANES == 0 else 1
    return width // unit * part // parts * unit


def on_device(n_gx, n_gy, tokens, gate_matrix, up_matrix, down_matrix):
    features = tokens.shape[1] * n_gx
    width = gate_matrix.shape[1] // n_gx
    block, columns = tokens.shape[0], down_matrix.shape[1]
    me = lax.axis_index("gx")
    far = [2 * k for k in range(1, n_gx // 2)]

    def core(value):
        return swap(value, "gx", n_gx, 1)

    values = tokens.astype(jnp.float32)
    squares = jnp.sum(values * values, axis=1)
    mask = 1
    while mask < n_gx:
        squares = squares + swap(squares, "gx", n_gx, mask)
        mask *= 2

    gathered = lax.all_gather(tokens, "gy", axis=0, tiled=True)
    here = lax.axis_index("gy")
    blocks = {j: (gathered, (here ^ j) * block) if j else (tokens, jnp.int32(0)) for j in range(n_gy)}
    factors = {0: lax.rsqrt(squares / features + EPS)}
    mask = n_gy // 2
    while mask:
        names = list(factors)
        arrived = swap(jnp.concatenate([factors[j] for j in names]), "gy", n_gy, mask)
        factors.update({j ^ mask: part for j, part in zip(names, jnp.split(arrived, len(names)))})
        mask //= 2

    groups = [[0], list(range(2, n_gy)), [1]]
    first, half = cut(width, 7, 13), cut(width, 7, 13)
    jobs = [(0, 0, first), (0, first, width), (1, 0, half), (1, half, width), (2, 0, half), (2, half, width)]
    jobs = [(group, low, high - low) for group, low, high in jobs]
    state = [dict() for _ in jobs]
    totals = {}
    chain = tokens

    def phase(kind, job):
        group, low, n = jobs[job]
        toks, st = [blocks[j] for j in groups[group]], state[job]
        start = lambda q: q * width + low
        if kind == "s":
            return [GateUp(toks, block, [start(me ^ k ^ 1)], n) for k in [*far, 0]]
        if kind == "x":
            return [GateUp(toks, block, [start(me ^ k)], n, [(st["lent"][i], 0)]) for i, k in enumerate(far)]
        if kind == "h":
            recvs = [(st["lent"][-1], 0)] + [(r, 0) for r in st["far"]]
            scale = jnp.concatenate([factors[j] for j in groups[group]])[:, None]
            return [GateUp(toks, block, [start(me)], n, recvs, scale)]
        last = all(g != group for g, _, _ in jobs[job + 1 :])
        dtype = jnp.bfloat16 if last and group else jnp.float32
        pieces = [(st["hidden"], me), (st["sibling"], me ^ 1)] + st["over"]
        return [Down([h for h, _ in pieces], [start(q) for _, q in pieces], totals.get(group), block, columns, dtype)]

    def deliver(kind, job, outs):
        group, st = jobs[job][0], state[job]
        if kind == "s":
            st["lent"] = [core(o[0]) for o in outs]
        elif kind == "x":
            st["far"] = [swap(o[0], "gx", n_gx, k) for o, k in zip(outs, far)]
        elif kind == "h":
            st["hidden"], st["sibling"] = outs[0][0], core(outs[0][0])
            st["crossed"] = [swap(outs[0][0], "gx", n_gx, k) for k in far]
        else:
            totals[group] = outs[0]

    def tied(values):
        nonlocal chain
        values, chain = lax.optimization_barrier((values, chain))
        return values

    def forward(job):
        crossed = tied(state[job]["crossed"])
        state[job]["over"] = [(h, me ^ k) for h, k in zip(crossed, far)]
        state[job]["over"] += [(core(h), me ^ k ^ 1) for h, k in zip(crossed, far)]

    for names in STEPS:
        items = []
        for name in names.split():
            if name[0] == "r":
                forward(int(name[1:]))
            else:
                items.append((name[0], int(name[1:])))
        waiting = [(kind, job, phase(kind, job)) for kind, job in items if kind != "d"]
        downs = [job for kind, job in items if kind == "d"]
        merged = []
        for job in downs:
            found = phase("d", job)[0]
            if merged and jobs[merged[-1][1]][0] == jobs[job][0]:
                before = merged[-1][2][0]
                both = Down(
                    before.pieces + found.pieces, before.starts + found.starts, before.total, block, columns, found.dtype
                )
                merged[-1] = ("d", job, [both])
            else:
                merged.append(("d", job, [found]))
        waiting += merged
        results = run([p for _, _, ps in waiting for p in ps], gate_matrix, up_matrix, down_matrix, chain)
        chain = results[0][0]
        for kind, job, ps in waiting:
            deliver(kind, job, [results.pop(0) for _ in ps])

    parts = dict(zip(groups[1], totals[1]))
    parts[0] = totals[0][0]
    mask = 1
    while mask < n_gy:
        for j in [j for j in parts if j & mask]:
            arrived = swap(parts.pop(j), "gy", n_gy, mask).astype(jnp.float32)
            total = parts[j ^ mask].astype(jnp.float32) + arrived
            parts[j ^ mask] = total if j == mask else total.astype(jnp.bfloat16)
        mask *= 2
    last = swap(totals[2][0], "gy", n_gy, 1).astype(jnp.float32)
    return (parts[0] + last).astype(jnp.bfloat16)


def solution(mesh):
    n_gx, n_gy = mesh.shape["gx"], mesh.shape["gy"]
    placed = (P(("groups", "gy"), "gx"), P("gx", "gy"), P("gx", "gy"), P("gy", "gx"))
    return jax.shard_map(
        functools.partial(on_device, n_gx, n_gy),
        mesh=mesh,
        in_specs=placed,
        out_specs=P(("groups", "gy"), "gx"),
        check_vma=False,
    )
```

```python
import functools

import jax
import jax.numpy as jnp
from jax import lax
from jax.experimental import pallas as pl
from jax.experimental.pallas import tpu as pltpu
from jax.sharding import PartitionSpec as P

EPS = 1e-05
LANES = 128
DEPTH = 512
BREADTH = 2048
UNIT = 128
AHEAD = 4
SLOTS = AHEAD + 1
COST = pl.CostEstimate(flops=1000, bytes_accessed=1000, transcendentals=0)
VMEM_LIMIT = 64 * 1024 * 1024 - 64 * 1024
ANY = pl.BlockSpec(memory_space=pl.ANY)
SMEM = pl.BlockSpec(memory_space=pltpu.SMEM)


def swap(value, axis, size, mask):
    return lax.ppermute(value, axis, [(i, i ^ mask) for i in range(size)])


def silu_product(gate, up, scale):
    gate = gate * scale
    return gate / (1.0 + jnp.exp(-gate)) * (up * scale)


def multiple(value, of):
    return value if isinstance(value, int) else pl.multiple_of(value, of)


class Group:
    def __init__(self, toks, block):
        self.toks, self.block, self.rows = toks, block, block * len(toks)

    def plain(self, table):
        return jnp.concatenate([lax.dynamic_slice_in_dim(t, table[i], self.block, 0) for t, i in self.toks], axis=0)


class GateUp:
    def __init__(self, group, place, low, width, recvs=(), squares=(), finish=False, emit=False, features=1):
        self.group, self.place, self.low, self.width, self.recvs = group, place, low, width, list(recvs)
        self.squares, self.finish, self.emit, self.features = list(squares), finish, emit, features
        rows = group.rows
        self.outs = [jax.ShapeDtypeStruct((rows, width) if finish else (2, rows, width), jnp.bfloat16)]
        if emit:
            self.outs.append(jax.ShapeDtypeStruct((rows, LANES), jnp.float32))

    def fits(self, depth, columns):
        return self.width % LANES == 0 and 2 * self.width <= BREADTH and depth % DEPTH == 0 and self.group.block % 16 == 0

    def arrays(self):
        return [*self.recvs, *[s for s in self.squares if s is not None]]

    def plain(self, table, gate_matrix, up_matrix, down_matrix):
        tok = self.group.plain(table)
        gate, up = (
            jnp.dot(
                tok,
                lax.dynamic_slice_in_dim(m, table[self.place] + self.low, self.width, 1),
                preferred_element_type=jnp.float32,
            )
            for m in (gate_matrix, up_matrix)
        )
        for r in self.recvs:
            gate, up = gate + r[0].astype(jnp.float32), up + r[1].astype(jnp.float32)
        values = tok.astype(jnp.float32)
        own = jnp.broadcast_to(jnp.sum(values * values, axis=1, keepdims=True), (tok.shape[0], LANES))
        squares = sum(own if s is None else s for s in self.squares)
        if self.finish:
            scale = lax.rsqrt(squares[:, :1] / self.features + EPS)
            return [silu_product(gate, up, scale).astype(jnp.bfloat16)]
        return [jnp.stack([gate, up]).astype(jnp.bfloat16)] + ([squares] if self.emit else [])

    def scratch(self):
        rows, n, s = self.group.rows, self.width, len(self.arrays()) - len(self.recvs)
        return [
            pltpu.VMEM((max(len(self.recvs), 1), 2, rows, n) if self.recvs else (1, 2, 16, LANES), jnp.bfloat16),
            pltpu.VMEM((max(s, 1), rows, LANES), jnp.float32),
            pltpu.VMEM((1 if self.finish else 2, rows, n), jnp.bfloat16),
            pltpu.VMEM((rows, LANES), jnp.float32),
            pltpu.SemaphoreType.DMA((len(self.recvs) + s + 1,)),
            pltpu.SemaphoreType.DMA((2,)),
        ]

    def bind(self, refs, table, arrays, outs, scratch):
        rbuf, sbuf, obuf, qbuf, rsem, osem = scratch
        n, rows, n_recv = self.width, self.group.rows, len(self.recvs)
        xbuf, acc = refs["x"][id(self.group)], refs["acc"]
        self.count = xbuf.shape[1] // DEPTH
        columns = pl.ds(pl.multiple_of(table[self.place] + self.low, LANES), n)

        def weights(k, slot):
            part = pl.ds(multiple(k * DEPTH, DEPTH), DEPTH)
            return [
                pltpu.make_async_copy(m.at[part, columns], refs["w"].at[slot, :, pl.ds(i * n, n)], refs["wsem"].at[slot, i])
                for i, m in enumerate((refs["gate"], refs["up"]))
            ]

        copies = [pltpu.make_async_copy(a, rbuf.at[i], rsem.at[i]) for i, a in enumerate(arrays[:n_recv])]
        copies += [pltpu.make_async_copy(a, sbuf.at[i], rsem.at[n_recv + i]) for i, a in enumerate(arrays[n_recv:])]
        writes = [pltpu.make_async_copy(obuf.at[0] if self.finish else obuf, outs[0], osem.at[0])]
        if self.emit:
            writes.append(pltpu.make_async_copy(qbuf, outs[1], osem.at[1]))

        def multiply(k, slot):
            part = pl.ds(multiple(k * DEPTH, LANES), DEPTH)
            acc[:rows, : 2 * n] += jnp.dot(
                xbuf[:, part], refs["w"][slot, :, : 2 * n], preferred_element_type=jnp.float32
            )

        def sums():
            held, total = 0, None
            for s in self.squares:
                if s is None:
                    values = xbuf[...].astype(jnp.float32)
                    term = jnp.broadcast_to(jnp.sum(values * values, axis=1, keepdims=True), (rows, LANES))
                else:
                    term, held = sbuf[held], held + 1
                total = term if total is None else total + term
            return total

        def end():
            for copy in copies:
                copy.wait()
            if self.emit:
                qbuf[...] = sums()
            if self.finish:
                scale = lax.rsqrt(sums()[:, :1] / self.features + EPS)
            for low in range(0, n, LANES):
                gate, up = acc[:rows, low : low + LANES], acc[:rows, n + low : n + low + LANES]
                for r in range(n_recv):
                    gate = gate + rbuf[r, 0, :, low : low + LANES].astype(jnp.float32)
                    up = up + rbuf[r, 1, :, low : low + LANES].astype(jnp.float32)
                if self.finish:
                    obuf[0, :, low : low + LANES] = silu_product(gate, up, scale).astype(jnp.bfloat16)
                else:
                    obuf[0, :, low : low + LANES] = gate.astype(jnp.bfloat16)
                    obuf[1, :, low : low + LANES] = up.astype(jnp.bfloat16)
            for copy in writes:
                copy.start()

        self.weights, self.copies, self.multiply, self.end, self.writes = weights, copies, multiply, end, writes

    def clear(self, acc):
        acc[: self.group.rows, : 2 * self.width] = jnp.zeros((self.group.rows, 2 * self.width), jnp.float32)


class Down:
    def __init__(self, pieces, places, lows, total, block, columns, dtype):
        self.pieces, self.places, self.lows, self.total, self.block, self.dtype = pieces, places, lows, total, block, dtype
        self.rows, self.columns, self.group = pieces[0].shape[0], columns, None
        self.outs = [jax.ShapeDtypeStruct((block, columns), dtype) for _ in range(self.rows // block)]

    def fits(self, depth, columns):
        whole = sum(p.shape[1] for p in self.pieces) % DEPTH == 0
        return all(p.shape[1] % UNIT == 0 for p in self.pieces) and whole and columns <= BREADTH and columns % LANES == 0

    def arrays(self):
        return [*self.pieces, *(self.total or [])]

    def plain(self, table, gate_matrix, up_matrix, down_matrix):
        result = sum(
            jnp.dot(
                p, lax.dynamic_slice_in_dim(down_matrix, table[i] + low, p.shape[1], 0), preferred_element_type=jnp.float32
            )
            for p, i, low in zip(self.pieces, self.places, self.lows)
        )
        if self.total is not None:
            result = result + jnp.concatenate(self.total, axis=0)
        return jnp.split(result.astype(self.dtype), len(self.outs))

    def scratch(self):
        return [
            pltpu.VMEM((self.rows, sum(p.shape[1] for p in self.pieces)), jnp.bfloat16),
            pltpu.VMEM((self.rows if self.total else 8, self.columns), jnp.float32),
            pltpu.VMEM((self.rows, self.columns), self.dtype),
            pltpu.SemaphoreType.DMA((len(self.pieces) + len(self.outs),)),
            pltpu.SemaphoreType.DMA((len(self.outs),)),
        ]

    def bind(self, refs, table, arrays, outs, scratch):
        hbuf, tbuf, obuf, hsem, osem = scratch
        n, rows, block, columns, acc = len(self.pieces), self.rows, self.block, self.columns, refs["acc"]
        sizes = [p.shape[1] for p in self.pieces]
        self.count = sum(sizes) // DEPTH
        firsts = [sum(sizes[:p]) // UNIT for p in range(n)]
        starts = [table[i] + low for i, low in zip(self.places, self.lows)]

        def weights(k, slot):
            copies = []
            for i in range(DEPTH // UNIT):
                unit = k * (DEPTH // UNIT) + i
                row = starts[0] + unit * UNIT
                for p in range(1, n):
                    row = jnp.where(unit >= firsts[p], starts[p] + (unit - firsts[p]) * UNIT, row)
                copies.append(
                    pltpu.make_async_copy(
                        refs["down"].at[pl.ds(pl.multiple_of(row, UNIT), UNIT)],
                        refs["w"].at[slot, pl.ds(i * UNIT, UNIT), pl.ds(0, columns)],
                        refs["wsem"].at[slot, i],
                    )
                )
            return copies

        copies = [
            pltpu.make_async_copy(a, hbuf.at[:, pl.ds(first * UNIT, size)], hsem.at[i])
            for i, (a, first, size) in enumerate(zip(arrays, firsts, sizes))
        ]
        copies += [
            pltpu.make_async_copy(a, tbuf.at[pl.ds(i * block, block)], hsem.at[n + i]) for i, a in enumerate(arrays[n:])
        ]
        writes = [
            pltpu.make_async_copy(obuf.at[pl.ds(i * block, block)], out, osem.at[i]) for i, out in enumerate(outs)
        ]

        def multiply(k, slot):
            part = pl.ds(multiple(k * DEPTH, LANES), DEPTH)
            acc[:rows, :columns] += jnp.dot(
                hbuf[:, part], refs["w"][slot, :, :columns], preferred_element_type=jnp.float32
            )

        def end():
            obuf[...] = acc[:rows, :columns].astype(obuf.dtype)
            for copy in writes:
                copy.start()

        self.tbuf = tbuf
        self.weights, self.copies, self.multiply, self.end, self.writes = weights, copies, multiply, end, writes

    def clear(self, acc):
        acc[: self.rows, : self.columns] = (
            self.tbuf[...] if self.total else jnp.zeros((self.rows, self.columns), jnp.float32)
        )


def run(phases, table, gate_matrix, up_matrix, down_matrix, dep):
    depth, columns = gate_matrix.shape[0], down_matrix.shape[1]
    if not all(p.fits(depth, columns) for p in phases):
        return [p.plain(table, gate_matrix, up_matrix, down_matrix) for p in phases]
    operands = [gate_matrix, up_matrix, down_matrix]

    def index(array):
        for i, known in enumerate(operands):
            if known is array:
                return i
        operands.append(array)
        return len(operands) - 1

    groups = []
    for p in phases:
        if p.group is not None and all(p.group is not g for g in groups):
            groups.append(p.group)
    tok_places = [[index(t) for t, _ in g.toks] for g in groups]
    where = [[index(a) for a in p.arrays()] for p in phases]
    index(dep)
    outs = [o for p in phases for o in p.outs]
    scratch = [p.scratch() for p in phases]
    rows = max(p.group.rows if p.group is not None else p.rows for p in phases)

    def kernel(table_ref, *args):
        args = list(args)
        arrays = [args.pop(0) for _ in operands]
        out_refs = [args.pop(0) for _ in outs]
        refs = {"gate": arrays[0], "up": arrays[1], "down": arrays[2], "x": {}}
        refs["w"], refs["wsem"], refs["acc"] = args.pop(0), args.pop(0), args.pop(0)
        ready = {}
        for g, places in zip(groups, tok_places):
            xbuf, xsem = args.pop(0), args.pop(0)
            refs["x"][id(g)] = xbuf
            ready[id(g)] = [
                pltpu.make_async_copy(
                    arrays[place].at[pl.ds(pl.multiple_of(table_ref[i], 16), g.block)],
                    xbuf.at[pl.ds(j * g.block, g.block)],
                    xsem.at[j],
                )
                for j, (place, (_, i)) in enumerate(zip(places, g.toks))
            ]
        for p, places, buffers in zip(phases, where, scratch):
            mine = [out_refs.pop(0) for _ in p.outs]
            held = [args.pop(0) for _ in buffers]
            p.bind(refs, table_ref, [arrays[i] for i in places], mine, held)

        def begin(i, k, slot):
            for copy in phases[i].weights(k, slot):
                copy.start()

        offsets = [sum(q.count for q in phases[:i]) for i in range(len(phases) + 1)]
        for g in groups[:1]:
            for copy in ready[id(g)]:
                copy.start()
        for t in range(min(AHEAD, offsets[-1])):
            i = max(j for j in range(len(phases)) if offsets[j] <= t)
            begin(i, t - offsets[i], t % SLOTS)
        for g in groups[1:]:
            for copy in ready[id(g)]:
                copy.start()
        for p in phases:
            for copy in p.copies:
                copy.start()
        for i, p in enumerate(phases):
            if p.group is not None:
                for copy in ready.pop(id(p.group), []):
                    copy.wait()
            else:
                for copy in p.copies:
                    copy.wait()
            p.clear(refs["acc"])

            @pl.loop(0, p.count)
            def _(k):
                t = offsets[i] + k
                slot = lax.rem(t, SLOTS)
                for copy in p.weights(k, slot):
                    copy.wait()
                later = lax.rem(t + AHEAD, SLOTS)
                for j in range(i, len(phases)):
                    if offsets[j] < offsets[i + 1] + AHEAD:
                        @pl.when((t + AHEAD >= offsets[j]) & (t + AHEAD < offsets[j + 1]))
                        def _():
                            begin(j, t + AHEAD - offsets[j], later)
                p.multiply(k, slot)

            p.end()
        for p in phases:
            for copy in p.writes:
                copy.wait()

    results = list(
        pl.pallas_call(
            kernel,
            out_shape=outs,
            in_specs=[SMEM] + [ANY] * len(operands),
            out_specs=[ANY] * len(outs),
            scratch_shapes=[
                pltpu.VMEM((SLOTS, DEPTH, BREADTH), jnp.bfloat16),
                pltpu.SemaphoreType.DMA((SLOTS, DEPTH // UNIT)),
                pltpu.VMEM((rows, BREADTH), jnp.float32),
                *[
                    buffer
                    for g in groups
                    for buffer in (pltpu.VMEM((g.rows, depth), jnp.bfloat16), pltpu.SemaphoreType.DMA((len(g.toks),)))
                ],
                *[buffer for buffers in scratch for buffer in buffers],
            ],
            compiler_params=pltpu.CompilerParams(vmem_limit_bytes=VMEM_LIMIT),
            cost_estimate=COST,
            name="step_" + "".join("g" if p.group is not None else "d" for p in phases),
        )(table, *operands)
    )
    return [[results.pop(0) for _ in p.outs] for p in phases]


STEPS = (
    ("s0", "s1"),
    ("x0",),
    ("x1",),
    ("h0",),
    ("h1",),
    ("r0", "s2"),
    ("r1", "s3"),
    ("x2",),
    ("x3", "s4", "s5", "d0", "d1"),
    ("h2",),
    ("h3",),
    ("r2", "x4", "x5"),
    ("r3", "d2", "d3"),
    ("h4",),
    ("h5",),
    ("r4", "d4"),
    ("r5", "d5"),
)


def cut(width, part, parts):
    unit = LANES if width % LANES == 0 else 1
    return width // unit * part // parts * unit


def on_device(n_gx, n_gy, tokens, gate_matrix, up_matrix, down_matrix):
    features = tokens.shape[1] * n_gx
    width = gate_matrix.shape[1] // n_gx
    block, columns = tokens.shape[0], down_matrix.shape[1]
    far = [2 * k for k in range(1, n_gx // 2)]

    def core(value):
        return swap(value, "gx", n_gx, 1)

    gathered = lax.all_gather(tokens, "gy", axis=0, tiled=True)
    table = jnp.concatenate(
        [
            (lax.axis_index("gx") ^ jnp.arange(n_gx, dtype=jnp.int32)) * width,
            (lax.axis_index("gy") ^ jnp.arange(n_gy, dtype=jnp.int32)) * block,
            jnp.zeros((1,), jnp.int32),
        ]
    )
    sets = [[0], list(range(2, n_gy)), [1]]
    groups = [Group([(gathered, n_gx + j) if j else (tokens, n_gx + n_gy) for j in js], block) for js in sets]
    squares = [None] * len(groups)
    half = cut(width, 7, 13)
    jobs = [(g, low, high - low) for g in range(len(groups)) for low, high in ((0, half), (half, width))]
    state = [dict() for _ in jobs]
    totals = {}
    chain = tokens

    def phases_of(kind, job):
        g, low, n = jobs[job]
        group, st, first = groups[g], state[job], low == 0
        if kind == "s":
            return [
                GateUp(group, k ^ 1, low, n, squares=[None], emit=first and k == 0) for k in [*far, 0]
            ]
        if kind == "x":
            return [
                GateUp(group, k, low, n, [st["lent"][i]], squares=[None, squares[g]] if first else [], emit=first and i == 0)
                for i, k in enumerate(far)
            ]
        if kind == "h":
            return [GateUp(group, 0, low, n, [st["lent"][-1], *st["far"]], squares[g], finish=True, features=features)]
        pieces = [(st["hidden"], 0), (st["sibling"], 1)] + st["over"]
        return [
            Down(
                [h for h, _ in pieces], [q for _, q in pieces], [low] * len(pieces), totals.get(g), block, columns,
                jnp.bfloat16 if not first and g else jnp.float32,
            )
        ]

    def deliver(kind, job, outs):
        g, st = jobs[job][0], state[job]
        if kind == "s":
            st["lent"] = [core(o[0]) for o in outs]
            if jobs[job][1] == 0:
                squares[g] = core(outs[-1][1])
        elif kind == "x":
            st["far"] = [swap(o[0], "gx", n_gx, k) for o, k in zip(outs, far)]
            if jobs[job][1] == 0:
                squares[g] = [outs[0][1], *[swap(outs[0][1], "gx", n_gx, k) for k in far]]
        elif kind == "h":
            st["hidden"], st["sibling"] = outs[0][0], core(outs[0][0])
            st["crossed"] = [swap(outs[0][0], "gx", n_gx, k) for k in far]
        else:
            totals[g] = outs[0]

    def forward(job):
        nonlocal chain
        crossed, chain = lax.optimization_barrier((state[job]["crossed"], chain))
        state[job]["over"] = [(h, k) for h, k in zip(crossed, far)]
        state[job]["over"] += [(core(h), k ^ 1) for h, k in zip(crossed, far)]

    for names in STEPS:
        items = []
        for kind, job in [(name[0], int(name[1:])) for name in names]:
            if kind == "r":
                forward(job)
                continue
            found = phases_of(kind, job)
            if kind == "d" and items and items[-1][0] == "d" and jobs[items[-1][1]][0] == jobs[job][0]:
                before, after = items.pop()[2][0], found[0]
                found = [
                    Down(
                        before.pieces + after.pieces, before.places + after.places, before.lows + after.lows, before.total,
                        block, columns, after.dtype,
                    )
                ]
            items.append((kind, job, found))
        results = run([p for _, _, ps in items for p in ps], table, gate_matrix, up_matrix, down_matrix, chain)
        chain = results[0][0]
        for kind, job, ps in items:
            deliver(kind, job, [results.pop(0) for _ in ps])

    parts = dict(zip(sets[1], totals[1]))
    parts[0] = totals[0][0]
    mask = 1
    while mask < n_gy:
        for j in [j for j in parts if j & mask]:
            arrived = swap(parts.pop(j), "gy", n_gy, mask).astype(jnp.float32)
            total = parts[j ^ mask].astype(jnp.float32) + arrived
            parts[j ^ mask] = total if j == mask else total.astype(jnp.bfloat16)
        mask *= 2
    last = swap(totals[2][0], "gy", n_gy, 1).astype(jnp.float32)
    return (parts[0] + last).astype(jnp.bfloat16)


def solution(mesh):
    n_gx, n_gy = mesh.shape["gx"], mesh.shape["gy"]
    placed = (P(("groups", "gy"), "gx"), P("gx", "gy"), P("gx", "gy"), P("gy", "gx"))
    return jax.shard_map(
        functools.partial(on_device, n_gx, n_gy),
        mesh=mesh,
        in_specs=placed,
        out_specs=P(("groups", "gy"), "gx"),
        check_vma=False,
    )
```

```python
import functools

import jax
import jax.numpy as jnp
from jax import lax
from jax.experimental import pallas as pl
from jax.experimental.pallas import tpu as pltpu
from jax.sharding import PartitionSpec as P

EPS = 1e-05
LANES = 128
DEPTH = 256
UNIT = 128
AHEAD = 5
SLOTS = AHEAD + 1
COST = pl.CostEstimate(flops=1000, bytes_accessed=1000, transcendentals=0)
VMEM_LIMIT = 64 * 1024 * 1024 - 64 * 1024
ANY = pl.BlockSpec(memory_space=pl.ANY)
SMEM = pl.BlockSpec(memory_space=pltpu.SMEM)


def swap(value, axis, size, mask):
    return lax.ppermute(value, axis, [(i, i ^ mask) for i in range(size)])


def silu_product(gate, up, scale):
    gate = gate * scale
    return gate / (1.0 + jnp.exp(-gate)) * (up * scale)


def multiple(value, of):
    return value if isinstance(value, int) else pl.multiple_of(value, of)


class Group:
    def __init__(self, toks, block):
        self.toks, self.block, self.rows = toks, block, block * len(toks)

    def plain(self, table):
        return jnp.concatenate([lax.dynamic_slice_in_dim(t, table[i], self.block, 0) for t, i in self.toks], axis=0)


class GateUp:
    def __init__(self, group, place, low, width, recvs=(), squares=(), emit=False, features=1):
        self.group, self.place, self.low, self.width, self.recvs = group, place, low, width, list(recvs)
        self.squares, self.finish, self.emit, self.features = list(squares), bool(squares), emit, features
        rows = group.rows
        self.outs = [jax.ShapeDtypeStruct((rows, width) if self.finish else (2, rows, width), jnp.bfloat16)]
        if emit:
            self.outs.append(jax.ShapeDtypeStruct((rows, LANES), jnp.float32))

    def fits(self, depth, columns):
        return self.width % LANES == 0 and depth % DEPTH == 0 and self.group.block % 16 == 0

    def arrays(self):
        return [*self.recvs, *[s for s, _ in self.squares]]

    def plain(self, table, gate_matrix, up_matrix, down_matrix):
        tok = self.group.plain(table)
        gate, up = (
            jnp.dot(
                tok,
                lax.dynamic_slice_in_dim(m, table[self.place] + self.low, self.width, 1),
                preferred_element_type=jnp.float32,
            )
            for m in (gate_matrix, up_matrix)
        )
        for r in self.recvs:
            gate, up = gate + r[0].astype(jnp.float32), up + r[1].astype(jnp.float32)
        if self.finish:
            squares = Group(self.squares, self.group.block).plain(table)
            scale = lax.rsqrt(squares[:, :1] / self.features + EPS)
            return [silu_product(gate, up, scale).astype(jnp.bfloat16)]
        values = tok.astype(jnp.float32)
        own = jnp.broadcast_to(jnp.sum(values * values, axis=1, keepdims=True), (tok.shape[0], LANES))
        return [jnp.stack([gate, up]).astype(jnp.bfloat16)] + ([own] if self.emit else [])

    def scratch(self):
        rows, n, s = self.group.rows, self.width, len(self.squares)
        return [
            pltpu.VMEM((max(len(self.recvs), 1), 2, rows, n) if self.recvs else (1, 2, 16, LANES), jnp.bfloat16),
            pltpu.VMEM((rows if s else 8, LANES), jnp.float32),
            pltpu.VMEM((1 if self.finish else 2, rows, n), jnp.bfloat16),
            pltpu.VMEM((rows, LANES), jnp.float32),
            pltpu.SemaphoreType.DMA((len(self.recvs) + s + 1,)),
            pltpu.SemaphoreType.DMA((2,)),
        ]

    def bind(self, refs, table, arrays, outs, scratch):
        rbuf, sbuf, obuf, qbuf, rsem, osem = scratch
        n, rows, n_recv = self.width, self.group.rows, len(self.recvs)
        xbuf, acc = refs["x"][id(self.group)], refs["acc"]
        self.count = xbuf.shape[1] // DEPTH
        columns = pl.ds(pl.multiple_of(table[self.place] + self.low, LANES), n)

        def weights(k, slot):
            part = pl.ds(multiple(k * DEPTH, DEPTH), DEPTH)
            return [
                pltpu.make_async_copy(m.at[part, columns], refs["w"].at[slot, :, pl.ds(i * n, n)], refs["wsem"].at[slot, i])
                for i, m in enumerate((refs["gate"], refs["up"]))
            ]

        copies = [pltpu.make_async_copy(a, rbuf.at[i], rsem.at[i]) for i, a in enumerate(arrays[:n_recv])]
        block = self.group.block
        copies += [
            pltpu.make_async_copy(
                a.at[pl.ds(pl.multiple_of(table[place], 16), block)], sbuf.at[pl.ds(i * block, block)], rsem.at[n_recv + i]
            )
            for i, (a, (_, place)) in enumerate(zip(arrays[n_recv:], self.squares))
        ]
        writes = [pltpu.make_async_copy(obuf.at[0] if self.finish else obuf, outs[0], osem.at[0])]
        if self.emit:
            writes.append(pltpu.make_async_copy(qbuf, outs[1], osem.at[1]))

        def multiply(k, slot):
            part = pl.ds(multiple(k * DEPTH, LANES), DEPTH)
            acc[:rows, : 2 * n] += jnp.dot(
                xbuf[:, part], refs["w"][slot, :, : 2 * n], preferred_element_type=jnp.float32
            )

        def end():
            for copy in copies:
                copy.wait()
            if self.emit:
                values = xbuf[...].astype(jnp.float32)
                qbuf[...] = jnp.broadcast_to(jnp.sum(values * values, axis=1, keepdims=True), (rows, LANES))
            if self.finish:
                scale = lax.rsqrt(sbuf[:, :1] / self.features + EPS)
            for low in range(0, n, LANES):
                gate, up = acc[:rows, low : low + LANES], acc[:rows, n + low : n + low + LANES]
                for r in range(n_recv):
                    gate = gate + rbuf[r, 0, :, low : low + LANES].astype(jnp.float32)
                    up = up + rbuf[r, 1, :, low : low + LANES].astype(jnp.float32)
                if self.finish:
                    obuf[0, :, low : low + LANES] = silu_product(gate, up, scale).astype(jnp.bfloat16)
                else:
                    obuf[0, :, low : low + LANES] = gate.astype(jnp.bfloat16)
                    obuf[1, :, low : low + LANES] = up.astype(jnp.bfloat16)
            for copy in writes:
                copy.start()

        self.weights, self.copies, self.multiply, self.end, self.writes = weights, copies, multiply, end, writes

    def clear(self, acc):
        acc[: self.group.rows, : 2 * self.width] = jnp.zeros((self.group.rows, 2 * self.width), jnp.float32)


class Down:
    def __init__(self, pieces, places, lows, total, block, columns, dtype):
        self.pieces, self.places, self.lows, self.total, self.block, self.dtype = pieces, places, lows, total, block, dtype
        self.rows, self.columns, self.group = pieces[0].shape[0], columns, None
        self.outs = [jax.ShapeDtypeStruct((block, columns), dtype) for _ in range(self.rows // block)]

    def fits(self, depth, columns):
        whole = sum(p.shape[1] for p in self.pieces) % DEPTH == 0
        return all(p.shape[1] % UNIT == 0 for p in self.pieces) and whole and columns % LANES == 0

    def arrays(self):
        return [*self.pieces, *(self.total or [])]

    def plain(self, table, gate_matrix, up_matrix, down_matrix):
        result = sum(
            jnp.dot(
                p, lax.dynamic_slice_in_dim(down_matrix, table[i] + low, p.shape[1], 0), preferred_element_type=jnp.float32
            )
            for p, i, low in zip(self.pieces, self.places, self.lows)
        )
        if self.total is not None:
            result = result + jnp.concatenate(self.total, axis=0).astype(jnp.float32)
        return jnp.split(result.astype(self.dtype), len(self.outs))

    def scratch(self):
        return [
            pltpu.VMEM((self.rows, sum(p.shape[1] for p in self.pieces)), jnp.bfloat16),
            pltpu.VMEM((self.rows if self.total else 16, self.columns), self.total[0].dtype if self.total else jnp.float32),
            pltpu.VMEM((self.rows, self.columns), self.dtype),
            pltpu.SemaphoreType.DMA((len(self.pieces) + len(self.outs),)),
            pltpu.SemaphoreType.DMA((len(self.outs),)),
        ]

    def bind(self, refs, table, arrays, outs, scratch):
        hbuf, tbuf, obuf, hsem, osem = scratch
        n, rows, block, columns, acc = len(self.pieces), self.rows, self.block, self.columns, refs["acc"]
        sizes = [p.shape[1] for p in self.pieces]
        self.count = sum(sizes) // DEPTH
        firsts = [sum(sizes[:p]) // UNIT for p in range(n)]
        starts = [table[i] + low for i, low in zip(self.places, self.lows)]

        def weights(k, slot):
            copies = []
            for i in range(DEPTH // UNIT):
                unit = k * (DEPTH // UNIT) + i
                row = starts[0] + unit * UNIT
                for p in range(1, n):
                    row = jnp.where(unit >= firsts[p], starts[p] + (unit - firsts[p]) * UNIT, row)
                copies.append(
                    pltpu.make_async_copy(
                        refs["down"].at[pl.ds(pl.multiple_of(row, UNIT), UNIT)],
                        refs["w"].at[slot, pl.ds(i * UNIT, UNIT), pl.ds(0, columns)],
                        refs["wsem"].at[slot, i],
                    )
                )
            return copies

        copies = [
            pltpu.make_async_copy(a, hbuf.at[:, pl.ds(first * UNIT, size)], hsem.at[i])
            for i, (a, first, size) in enumerate(zip(arrays, firsts, sizes))
        ]
        copies += [
            pltpu.make_async_copy(a, tbuf.at[pl.ds(i * block, block)], hsem.at[n + i]) for i, a in enumerate(arrays[n:])
        ]
        writes = [
            pltpu.make_async_copy(obuf.at[pl.ds(i * block, block)], out, osem.at[i]) for i, out in enumerate(outs)
        ]

        def multiply(k, slot):
            part = pl.ds(multiple(k * DEPTH, LANES), DEPTH)
            acc[:rows, :columns] += jnp.dot(
                hbuf[:, part], refs["w"][slot, :, :columns], preferred_element_type=jnp.float32
            )

        def end():
            obuf[...] = acc[:rows, :columns].astype(obuf.dtype)
            for copy in writes:
                copy.start()

        self.tbuf = tbuf
        self.weights, self.copies, self.multiply, self.end, self.writes = weights, copies, multiply, end, writes

    def clear(self, acc):
        acc[: self.rows, : self.columns] = (
            self.tbuf[...].astype(jnp.float32) if self.total else jnp.zeros((self.rows, self.columns), jnp.float32)
        )


def run(phases, table, gate_matrix, up_matrix, down_matrix, dep):
    depth, columns = gate_matrix.shape[0], down_matrix.shape[1]
    if not all(p.fits(depth, columns) for p in phases):
        return [p.plain(table, gate_matrix, up_matrix, down_matrix) for p in phases]
    operands = [gate_matrix, up_matrix, down_matrix]

    def index(array):
        for i, known in enumerate(operands):
            if known is array:
                return i
        operands.append(array)
        return len(operands) - 1

    groups = []
    for p in phases:
        if p.group is not None and all(p.group is not g for g in groups):
            groups.append(p.group)
    tok_places = [[index(t) for t, _ in g.toks] for g in groups]
    where = [[index(a) for a in p.arrays()] for p in phases]
    index(dep)
    outs = [o for p in phases for o in p.outs]
    scratch = [p.scratch() for p in phases]
    rows = max(p.group.rows if p.group is not None else p.rows for p in phases)
    breadth = max(2 * p.width if p.group is not None else columns for p in phases)

    def kernel(table_ref, *args):
        args = list(args)
        arrays = [args.pop(0) for _ in operands]
        out_refs = [args.pop(0) for _ in outs]
        refs = {"gate": arrays[0], "up": arrays[1], "down": arrays[2], "x": {}}
        refs["w"], refs["wsem"], refs["acc"] = args.pop(0), args.pop(0), args.pop(0)
        ready = {}
        for g, places in zip(groups, tok_places):
            xbuf, xsem = args.pop(0), args.pop(0)
            refs["x"][id(g)] = xbuf
            ready[id(g)] = [
                pltpu.make_async_copy(
                    arrays[place].at[pl.ds(pl.multiple_of(table_ref[i], 16), g.block)],
                    xbuf.at[pl.ds(j * g.block, g.block)],
                    xsem.at[j],
                )
                for j, (place, (_, i)) in enumerate(zip(places, g.toks))
            ]
        for p, places, buffers in zip(phases, where, scratch):
            mine = [out_refs.pop(0) for _ in p.outs]
            held = [args.pop(0) for _ in buffers]
            p.bind(refs, table_ref, [arrays[i] for i in places], mine, held)

        def begin(i, k, slot):
            for copy in phases[i].weights(k, slot):
                copy.start()

        offsets = [sum(q.count for q in phases[:i]) for i in range(len(phases) + 1)]
        for g in groups[:1]:
            for copy in ready[id(g)]:
                copy.start()
        for t in range(min(AHEAD, offsets[-1])):
            i = max(j for j in range(len(phases)) if offsets[j] <= t)
            begin(i, t - offsets[i], t % SLOTS)
        for g in groups[1:]:
            for copy in ready[id(g)]:
                copy.start()
        for p in phases:
            for copy in p.copies:
                copy.start()
        for i, p in enumerate(phases):
            if p.group is not None:
                for copy in ready.pop(id(p.group), []):
                    copy.wait()
            else:
                for copy in p.copies:
                    copy.wait()
            p.clear(refs["acc"])

            @pl.loop(0, p.count)
            def _(k):
                t = offsets[i] + k
                slot = lax.rem(t, SLOTS)
                for copy in p.weights(k, slot):
                    copy.wait()
                later = lax.rem(t + AHEAD, SLOTS)
                for j in range(i, len(phases)):
                    if offsets[j] < offsets[i + 1] + AHEAD:
                        @pl.when((t + AHEAD >= offsets[j]) & (t + AHEAD < offsets[j + 1]))
                        def _():
                            begin(j, t + AHEAD - offsets[j], later)
                p.multiply(k, slot)

            p.end()
        for p in phases:
            for copy in p.writes:
                copy.wait()

    results = list(
        pl.pallas_call(
            kernel,
            out_shape=outs,
            in_specs=[SMEM] + [ANY] * len(operands),
            out_specs=[ANY] * len(outs),
            scratch_shapes=[
                pltpu.VMEM((SLOTS, DEPTH, breadth), jnp.bfloat16),
                pltpu.SemaphoreType.DMA((SLOTS, DEPTH // UNIT)),
                pltpu.VMEM((rows, breadth), jnp.float32),
                *[
                    buffer
                    for g in groups
                    for buffer in (pltpu.VMEM((g.rows, depth), jnp.bfloat16), pltpu.SemaphoreType.DMA((len(g.toks),)))
                ],
                *[buffer for buffers in scratch for buffer in buffers],
            ],
            compiler_params=pltpu.CompilerParams(vmem_limit_bytes=VMEM_LIMIT),
            cost_estimate=COST,
            name="step_" + "".join("g" if p.group is not None else "d" for p in phases),
        )(table, *operands)
    )
    return [[results.pop(0) for _ in p.outs] for p in phases]


STEPS = (
    ("s0", "s1"),
    ("q", "x0", "x1"),
    ("h0",),
    ("h1",),
    ("r0", "r1", "s2", "s3"),
    ("x2",),
    ("x3",),
    ("h2",),
    ("s4",),
    ("h3",),
    ("x4",),
    ("r2", "r3", "d2", "d3"),
    ("h4",),
    ("z", "d0", "d1"),
    ("r4", "d4"),
)


def cut(width, part, parts):
    unit = LANES if width % LANES == 0 else 1
    return width // unit * part // parts * unit


def on_device(n_gx, n_gy, tokens, gate_matrix, up_matrix, down_matrix):
    features = tokens.shape[1] * n_gx
    width = gate_matrix.shape[1] // n_gx
    block, columns = tokens.shape[0], down_matrix.shape[1]
    far = [2 * k for k in range(1, n_gx // 2)]

    def core(value):
        return swap(value, "gx", n_gx, 1)

    gathered = lax.all_gather(tokens, "gy", axis=0, tiled=True)
    table = jnp.concatenate(
        [
            (lax.axis_index("gx") ^ jnp.arange(n_gx, dtype=jnp.int32)) * width,
            (lax.axis_index("gy") ^ jnp.arange(n_gy, dtype=jnp.int32)) * block,
            jnp.zeros((1,), jnp.int32),
        ]
    )
    sets = [[0], list(range(2, n_gy)), [1]]
    groups = [Group([(gathered, n_gx + j) if j else (tokens, n_gx + n_gy) for j in js], block) for js in sets]
    squares = gathered_squares = None
    half = cut(width, 7, 13)
    jobs = [(0, 0, half), (0, half, width - half), (1, 0, half), (1, half, width - half), (2, 0, width)]
    state = [dict() for _ in jobs]
    totals = {}
    chain = tokens

    def phases_of(kind, job):
        g, low, n = jobs[job]
        group, st, first = groups[g], state[job], low == 0
        if kind == "s":
            return [
                GateUp(group, k ^ 1, low, n, emit=job == 0 and k == 0) for k in [*far, 0]
            ]
        if kind == "x":
            return [GateUp(group, k, low, n, [st["lent"][i]]) for i, k in enumerate(far)]
        if kind == "h":
            known = [(gathered_squares, n_gx + j) if j else (squares, n_gx + n_gy) for j in sets[g]]
            return [GateUp(group, 0, low, n, [st["lent"][-1], *st["far"]], known, features=features)]
        pieces = [(st["hidden"], 0), (st["sibling"], 1)] + st["over"]
        return [
            Down(
                [h for h, _ in pieces], [q for _, q in pieces], [low] * len(pieces), totals.get(g), block, columns,
                jnp.bfloat16 if g and low + n == width else jnp.float32,
            )
        ]

    def deliver(kind, job, outs):
        nonlocal squares
        g, st = jobs[job][0], state[job]
        if kind == "s":
            st["lent"] = [core(o[0]) for o in outs]
            if job == 0:
                squares = [outs[-1][1], *[swap(outs[-1][1], "gx", n_gx, k) for k in range(1, n_gx)]]
        elif kind == "x":
            st["far"] = [swap(o[0], "gx", n_gx, k) for o, k in zip(outs, far)]
        elif kind == "h":
            st["hidden"], st["sibling"] = outs[0][0], core(outs[0][0])
            st["crossed"] = [swap(outs[0][0], "gx", n_gx, k) for k in far]
        else:
            totals[g] = outs[0]

    def tied(values):
        nonlocal chain
        values, chain = lax.optimization_barrier((values, chain))
        return values

    def forward(job):
        crossed = tied(state[job]["crossed"])
        state[job]["over"] = [(h, k) for h, k in zip(crossed, far)]
        state[job]["over"] += [(core(h), k ^ 1) for h, k in zip(crossed, far)]

    def reduce_over_gy():
        parts = dict(zip(sets[1], totals[1]))
        mask = 1
        while mask < n_gy:
            for j in [j for j in parts if j & mask]:
                arrived = swap(parts.pop(j), "gy", n_gy, mask)
                if j == mask:
                    landed.append(arrived)
                    continue
                arrived = tied(arrived).astype(jnp.float32)
                parts[j ^ mask] = (parts[j ^ mask].astype(jnp.float32) + arrived).astype(jnp.bfloat16)
            mask *= 2

    landed = []
    for names in STEPS:
        items = []
        for name in names:
            kind, job = name[0], int(name[1:] or 0)
            if kind == "r":
                forward(job)
                continue
            if kind == "q":
                squares = sum(tied(squares))
                gathered_squares = lax.all_gather(squares, "gy", axis=0, tiled=True)
                continue
            if kind == "z":
                reduce_over_gy()
                continue
            if kind == "e":
                totals[0] = [landed.pop(0)]
                continue
            found = phases_of(kind, job)
            if kind == "d" and items and items[-1][0] == "d" and jobs[items[-1][1]][0] == jobs[job][0]:
                before, after = items.pop()[2][0], found[0]
                found = [
                    Down(
                        before.pieces + after.pieces, before.places + after.places, before.lows + after.lows, before.total,
                        block, columns, after.dtype,
                    )
                ]
            items.append((kind, job, found))
        results = run([p for _, _, ps in items for p in ps], table, gate_matrix, up_matrix, down_matrix, chain)
        chain = results[0][0]
        for kind, job, ps in items:
            deliver(kind, job, [results.pop(0) for _ in ps])

    landed.append(swap(totals[2][0], "gy", n_gy, 1))
    return sum((part.astype(jnp.float32) for part in landed), totals[0][0]).astype(jnp.bfloat16)


def solution(mesh):
    n_gx, n_gy = mesh.shape["gx"], mesh.shape["gy"]
    placed = (P(("groups", "gy"), "gx"), P("gx", "gy"), P("gx", "gy"), P("gy", "gx"))
    return jax.shard_map(
        functools.partial(on_device, n_gx, n_gy),
        mesh=mesh,
        in_specs=placed,
        out_specs=P(("groups", "gy"), "gx"),
        check_vma=False,
    )
```

```python
import functools

import jax
import jax.numpy as jnp
from jax import lax
from jax.experimental import pallas as pl
from jax.experimental.pallas import tpu as pltpu
from jax.sharding import PartitionSpec as P

EPS = 1e-05
LANES = 128
GU_TILE = 256
OUT_TILE = 512
COST = pl.CostEstimate(flops=1000, bytes_accessed=1000, transcendentals=0)
VMEM_LIMIT = 64 * 1024 * 1024 - 64 * 1024
ANY = pl.BlockSpec(memory_space=pl.ANY)
SMEM = pl.BlockSpec(memory_space=pltpu.SMEM)


def swap(value, axis, size, mask):
    return lax.ppermute(value, axis, [(i, i ^ mask) for i in range(size)])


def silu_product(gate, up, scale):
    gate = gate * scale
    return gate / (1.0 + jnp.exp(-gate)) * (up * scale)


class Group:
    def __init__(self, toks, block):
        self.toks, self.block, self.rows = toks, block, block * len(toks)

    def plain(self, table):
        return jnp.concatenate([lax.dynamic_slice_in_dim(t, table[i], self.block, 0) for t, i in self.toks], axis=0)


class GateUp:
    def __init__(self, group, place, low, width, recvs=(), carry=False, emit=False, squares=None, at=0, features=1):
        self.group, self.place, self.low, self.width, self.recvs = group, place, low, width, list(recvs)
        self.carry, self.emit, self.squares, self.at, self.features = carry, emit, squares, at, features
        rows, wide = group.rows, width + (LANES if carry else 0)
        self.outs = [jax.ShapeDtypeStruct((2, rows, wide) if squares is None else (rows, width), jnp.bfloat16)]
        if emit:
            self.outs.append(jax.ShapeDtypeStruct((rows, LANES), jnp.float32))

    def fits(self, depth, columns):
        return self.width % LANES == 0 and depth % LANES == 0 and self.group.block % 16 == 0

    def arrays(self):
        return [*self.recvs, *([self.squares[0], *self.squares[1]] if self.squares else [])]

    def plain(self, table, gate_matrix, up_matrix, down_matrix):
        tok, n = self.group.plain(table), self.width
        gate, up = (
            jnp.dot(
                tok, lax.dynamic_slice_in_dim(m, table[self.place] + self.low, n, 1), preferred_element_type=jnp.float32
            )
            for m in (gate_matrix, up_matrix)
        )
        for r in self.recvs:
            gate, up = gate + r[0, :, :n].astype(jnp.float32), up + r[1, :, :n].astype(jnp.float32)
        if self.squares:
            total = self.squares[0]
            for part in self.squares[1]:
                part = part[:, :, self.at : self.at + LANES].astype(jnp.float32)
                total = total + part[0] + part[1]
            return [silu_product(gate, up, lax.rsqrt(total[:, :1] / self.features + EPS)).astype(jnp.bfloat16)]
        if not self.carry:
            return [jnp.stack([gate, up]).astype(jnp.bfloat16)]
        values = tok.astype(jnp.float32)
        total = jnp.broadcast_to(jnp.sum(values * values, axis=1, keepdims=True), (tok.shape[0], LANES))
        for r in self.recvs:
            part = r[:, :, n : n + LANES].astype(jnp.float32)
            total = total + part[0] + part[1]
        high = total.astype(jnp.bfloat16).astype(jnp.float32)
        both = jnp.stack([jnp.concatenate([gate, high], axis=1), jnp.concatenate([up, total - high], axis=1)])
        return [both.astype(jnp.bfloat16)] + ([total] if self.emit else [])

    def scratch(self, depth):
        rows, n, tiles, n_recv = self.group.rows, self.width, pl.cdiv(self.width, GU_TILE), len(self.recvs)
        extra = len(self.squares[1]) if self.squares else n_recv if self.carry else 0
        return [
            pltpu.VMEM((tiles, depth, 2 * GU_TILE), jnp.bfloat16),
            pltpu.VMEM((n_recv, 2, rows, n) if n_recv else (1, 2, 16, LANES), jnp.bfloat16),
            pltpu.VMEM((extra, 2, rows, LANES) if extra else (1, 2, 16, LANES), jnp.bfloat16),
            pltpu.VMEM((rows, LANES) if self.squares or self.emit else (8, LANES), jnp.float32),
            pltpu.VMEM((tiles, 1 if self.squares else 2, rows, GU_TILE), jnp.bfloat16),
            pltpu.VMEM((2, rows, LANES) if self.carry else (2, 16, LANES), jnp.bfloat16),
            pltpu.SemaphoreType.DMA((2, tiles)),
            pltpu.SemaphoreType.DMA((n_recv + extra + 1,)),
            pltpu.SemaphoreType.DMA((tiles + 2,)),
        ]

    def bind(self, refs, table, arrays, outs, scratch):
        wbuf, rbuf, ebuf, qbuf, obuf, cbuf, wsem, rsem, osem = scratch
        n, rows, n_recv = self.width, self.group.rows, len(self.recvs)
        xbuf, hidden = refs["x"][id(self.group)], self.squares is not None
        full, rest = divmod(n, GU_TILE)
        tiles = full + (rest > 0)
        start = table[self.place] + self.low

        def weights(j, m):
            columns = pl.ds(pl.multiple_of(start + j * GU_TILE, LANES), m)
            return [
                pltpu.make_async_copy(refs[name].at[:, columns], wbuf.at[j, :, pl.ds(i * m, m)], wsem.at[i, j])
                for i, name in enumerate(("gate", "up"))
            ]

        def write(j, m):
            columns = pl.ds(pl.multiple_of(j * GU_TILE, LANES), m)
            if hidden:
                return pltpu.make_async_copy(obuf.at[j, 0, :, pl.ds(0, m)], outs[0].at[:, columns], osem.at[j])
            return pltpu.make_async_copy(obuf.at[j, :, :, pl.ds(0, m)], outs[0].at[:, :, columns], osem.at[j])

        def over_tiles(step):
            if full:
                @pl.loop(0, full)
                def _(j):
                    step(j, GU_TILE)
            if rest:
                step(full, rest)

        copies = [
            pltpu.make_async_copy(a.at[:, :, pl.ds(0, n)], rbuf.at[i], rsem.at[i]) for i, a in enumerate(arrays[:n_recv])
        ]
        extras = arrays[n_recv + 1 :] if hidden else arrays[:n_recv] if self.carry else []
        copies += [
            pltpu.make_async_copy(a.at[:, :, pl.ds(self.at if hidden else n, LANES)], ebuf.at[i], rsem.at[n_recv + i])
            for i, a in enumerate(extras)
        ]
        if hidden:
            copies.append(pltpu.make_async_copy(arrays[n_recv], qbuf, rsem.at[n_recv + len(extras)]))
        writes = []
        if self.carry:
            writes.append(pltpu.make_async_copy(cbuf, outs[0].at[:, :, pl.ds(n, LANES)], osem.at[tiles]))
        if self.emit:
            writes.append(pltpu.make_async_copy(qbuf, outs[1], osem.at[tiles + 1]))

        def begin():
            def step(j, m):
                for copy in weights(j, m):
                    copy.start()

            over_tiles(step)

        def compute():
            for copy in copies:
                copy.wait()
            extra = None
            for i in range(len(extras)):
                term = ebuf[i, 0].astype(jnp.float32) + ebuf[i, 1].astype(jnp.float32)
                extra = term if extra is None else extra + term
            if self.carry:
                values = xbuf[...].astype(jnp.float32)
                total = jnp.broadcast_to(jnp.sum(values * values, axis=1, keepdims=True), (rows, LANES))
                total = total if extra is None else total + extra
                high = total.astype(jnp.bfloat16)
                cbuf[0] = high
                cbuf[1] = (total - high.astype(jnp.float32)).astype(jnp.bfloat16)
                if self.emit:
                    qbuf[...] = total
                for copy in writes:
                    copy.start()
            if hidden:
                total = qbuf[...] if extra is None else qbuf[...] + extra
                qbuf[...] = lax.rsqrt(total / self.features + EPS)

            def step(j, m):
                for copy in weights(j, m):
                    copy.wait()
                both = jnp.dot(xbuf[...], wbuf[j, :, pl.ds(0, 2 * m)], preferred_element_type=jnp.float32)
                gate, up = both[:, :m], both[:, m:]
                columns = pl.ds(pl.multiple_of(j * GU_TILE, LANES), m)
                for r in range(n_recv):
                    gate = gate + rbuf[r, 0, :, columns].astype(jnp.float32)
                    up = up + rbuf[r, 1, :, columns].astype(jnp.float32)
                if hidden:
                    obuf[j, 0, :, pl.ds(0, m)] = silu_product(gate, up, qbuf[:, :1]).astype(jnp.bfloat16)
                else:
                    obuf[j, 0, :, pl.ds(0, m)] = gate.astype(jnp.bfloat16)
                    obuf[j, 1, :, pl.ds(0, m)] = up.astype(jnp.bfloat16)
                write(j, m).start()

            over_tiles(step)

        def drain():
            over_tiles(lambda j, m: write(j, m).wait())
            for copy in writes:
                copy.wait()

        return copies, begin, compute, drain


class Down:
    def __init__(self, pieces, places, lows, total, block, columns, dtype):
        self.pieces, self.places, self.lows, self.total, self.block, self.dtype = pieces, places, lows, total, block, dtype
        self.rows, self.columns, self.group = pieces[0].shape[0], columns, None
        self.outs = [jax.ShapeDtypeStruct((block, columns), dtype) for _ in range(self.rows // block)]

    def fits(self, depth, columns):
        return all(p.shape[1] % LANES == 0 for p in self.pieces) and columns % OUT_TILE == 0 and self.block % 16 == 0

    def arrays(self):
        return [*self.pieces, *(self.total or [])]

    def plain(self, table, gate_matrix, up_matrix, down_matrix):
        result = sum(
            jnp.dot(
                p, lax.dynamic_slice_in_dim(down_matrix, table[i] + low, p.shape[1], 0), preferred_element_type=jnp.float32
            )
            for p, i, low in zip(self.pieces, self.places, self.lows)
        )
        if self.total is not None:
            result = result + jnp.concatenate(self.total, axis=0).astype(jnp.float32)
        return jnp.split(result.astype(self.dtype), len(self.outs))

    def scratch(self, depth):
        tiles, whole = self.columns // OUT_TILE, sum(p.shape[1] for p in self.pieces)
        return [
            pltpu.VMEM((self.rows, whole), jnp.bfloat16),
            pltpu.VMEM((tiles, whole, OUT_TILE), jnp.bfloat16),
            pltpu.VMEM(
                (self.rows if self.total else 16, self.columns), self.total[0].dtype if self.total else jnp.float32
            ),
            pltpu.VMEM((tiles, self.rows, OUT_TILE), self.dtype),
            pltpu.SemaphoreType.DMA((len(self.pieces) + len(self.outs),)),
            pltpu.SemaphoreType.DMA((len(self.pieces), tiles)),
            pltpu.SemaphoreType.DMA((len(self.outs), tiles)),
        ]

    def bind(self, refs, table, arrays, outs, scratch):
        hbuf, dbuf, tbuf, obuf, hsem, dsem, osem = scratch
        n, block, tiles = len(self.pieces), self.block, self.columns // OUT_TILE
        sizes = [p.shape[1] for p in self.pieces]
        firsts = [sum(sizes[:p]) for p in range(n)]
        starts = [table[i] + low for i, low in zip(self.places, self.lows)]

        def columns(j):
            return pl.ds(pl.multiple_of(j * OUT_TILE, LANES), OUT_TILE)

        def weights(p, j):
            return pltpu.make_async_copy(
                refs["down"].at[pl.ds(pl.multiple_of(starts[p], LANES), sizes[p]), columns(j)],
                dbuf.at[j, pl.ds(firsts[p], sizes[p])],
                dsem.at[p, j],
            )

        def write(i, j):
            return pltpu.make_async_copy(
                obuf.at[j, pl.ds(i * block, block)], outs[i].at[:, columns(j)], osem.at[i, j]
            )

        copies = [
            pltpu.make_async_copy(a, hbuf.at[:, pl.ds(firsts[i], sizes[i])], hsem.at[i]) for i, a in enumerate(arrays[:n])
        ]
        copies += [
            pltpu.make_async_copy(a, tbuf.at[pl.ds(i * block, block)], hsem.at[n + i]) for i, a in enumerate(arrays[n:])
        ]

        def begin():
            @pl.loop(0, tiles)
            def _(j):
                for p in range(n):
                    weights(p, j).start()

        def compute():
            for copy in copies:
                copy.wait()

            @pl.loop(0, tiles)
            def _(j):
                for p in range(n):
                    weights(p, j).wait()
                result = jnp.dot(hbuf[...], dbuf[j], preferred_element_type=jnp.float32)
                if self.total:
                    result = result + tbuf[:, columns(j)].astype(jnp.float32)
                obuf[j] = result.astype(obuf.dtype)
                for i in range(len(outs)):
                    write(i, j).start()

        def drain():
            @pl.loop(0, tiles)
            def _(j):
                for i in range(len(outs)):
                    write(i, j).wait()

        return copies, begin, compute, drain


def run(phases, table, gate_matrix, up_matrix, down_matrix, dep):
    depth, columns = gate_matrix.shape[0], down_matrix.shape[1]
    if not all(p.fits(depth, columns) for p in phases):
        return [p.plain(table, gate_matrix, up_matrix, down_matrix) for p in phases]
    operands = [gate_matrix, up_matrix, down_matrix]

    def index(array):
        for i, known in enumerate(operands):
            if known is array:
                return i
        operands.append(array)
        return len(operands) - 1

    groups = []
    for p in phases:
        if p.group is not None and all(p.group is not g for g in groups):
            groups.append(p.group)
    tok_places = [[index(t) for t, _ in g.toks] for g in groups]
    where = [[index(a) for a in p.arrays()] for p in phases]
    index(dep)
    outs = [o for p in phases for o in p.outs]
    scratch = [p.scratch(depth) for p in phases]

    def kernel(table_ref, *args):
        args = list(args)
        arrays = [args.pop(0) for _ in operands]
        out_refs = [args.pop(0) for _ in outs]
        refs = {"gate": arrays[0], "up": arrays[1], "down": arrays[2], "x": {}}
        ready = {}
        for g, places in zip(groups, tok_places):
            xbuf, xsem = args.pop(0), args.pop(0)
            refs["x"][id(g)] = xbuf
            ready[id(g)] = [
                pltpu.make_async_copy(
                    arrays[place].at[pl.ds(pl.multiple_of(table_ref[i], 16), g.block)],
                    xbuf.at[pl.ds(j * g.block, g.block)],
                    xsem.at[j],
                )
                for j, (place, (_, i)) in enumerate(zip(places, g.toks))
            ]
        bound = []
        for p, places, buffers in zip(phases, where, scratch):
            mine = [out_refs.pop(0) for _ in p.outs]
            held = [args.pop(0) for _ in buffers]
            bound.append(p.bind(refs, table_ref, [arrays[i] for i in places], mine, held))
        for copies in ready.values():
            for copy in copies:
                copy.start()
        for copies, begin, _, _ in bound:
            for copy in copies:
                copy.start()
            begin()
        for p, (_, _, compute, _) in zip(phases, bound):
            for copy in ready.pop(id(p.group), []):
                copy.wait()
            compute()
        for _, _, _, drain in bound:
            drain()

    results = list(
        pl.pallas_call(
            kernel,
            out_shape=outs,
            in_specs=[SMEM] + [ANY] * len(operands),
            out_specs=[ANY] * len(outs),
            scratch_shapes=[
                *[
                    buffer
                    for g in groups
                    for buffer in (pltpu.VMEM((g.rows, depth), jnp.bfloat16), pltpu.SemaphoreType.DMA((len(g.toks),)))
                ],
                *[buffer for buffers in scratch for buffer in buffers],
            ],
            compiler_params=pltpu.CompilerParams(vmem_limit_bytes=VMEM_LIMIT),
            cost_estimate=COST,
            name="step_" + "".join("g" if p.group is not None else "d" for p in phases),
        )(table, *operands)
    )
    return [[results.pop(0) for _ in p.outs] for p in phases]


STEPS = (
    ("s0", "s1"),
    ("x0", "x1"),
    ("h0",),
    ("h1",),
    ("r0", "r1", "s2", "s3"),
    ("x2",),
    ("x3",),
    ("s4",),
    ("h2",),
    ("h3",),
    ("x4",),
    ("r2", "r3", "d2", "d3"),
    ("h4",),
    ("z", "d0", "d1"),
    ("r4", "d4"),
)


def cut(width, part, parts):
    unit = LANES if width % LANES == 0 else 1
    return width // unit * part // parts * unit


def on_device(n_gx, n_gy, tokens, gate_matrix, up_matrix, down_matrix):
    features = tokens.shape[1] * n_gx
    width = gate_matrix.shape[1] // n_gx
    block, columns = tokens.shape[0], down_matrix.shape[1]
    far = [2 * k for k in range(1, n_gx // 2)]

    def core(value):
        return swap(value, "gx", n_gx, 1)

    gathered = lax.all_gather(tokens, "gy", axis=0, tiled=True)
    table = jnp.concatenate(
        [
            (lax.axis_index("gx") ^ jnp.arange(n_gx, dtype=jnp.int32)) * width,
            (lax.axis_index("gy") ^ jnp.arange(n_gy, dtype=jnp.int32)) * block,
            jnp.zeros((1,), jnp.int32),
        ]
    )
    sets = [[0], list(range(2, n_gy)), [1]]
    groups = [Group([(gathered, n_gx + j) if j else (tokens, n_gx + n_gy) for j in js], block) for js in sets]
    squares = {}
    half = cut(width, 7, 13)
    jobs = [(0, 0, half), (0, half, width - half), (1, 0, half), (1, half, width - half), (2, 0, width)]
    firsts = [min(i for i, job in enumerate(jobs) if job[0] == g) for g in range(len(groups))]
    state = [dict() for _ in jobs]
    totals = {}
    chain = tokens

    def phases_of(kind, job):
        g, low, n = jobs[job]
        group, st, first = groups[g], state[job], low == 0
        if kind == "s":
            return [GateUp(group, k ^ 1, low, n, carry=first and k > 0) for k in [*far, 0]]
        if kind == "x":
            return [
                GateUp(group, k, low, n, [st["lent"][i]], carry=first, emit=first and i == 0)
                for i, k in enumerate(far)
            ]
        if kind == "h":
            recvs = [st["lent"][-1], *st["far"]]
            return [GateUp(group, 0, low, n, recvs, squares=squares[g], at=jobs[firsts[g]][2], features=features)]
        pieces = [(st["hidden"], 0), (st["sibling"], 1)] + st["over"]
        return [
            Down(
                [h for h, _ in pieces], [q for _, q in pieces], [low] * len(pieces), totals.get(g), block, columns,
                jnp.bfloat16 if g and low + n == width else jnp.float32,
            )
        ]

    def deliver(kind, job, outs):
        g, st = jobs[job][0], state[job]
        if kind == "s":
            st["lent"] = [core(o[0]) for o in outs]
        elif kind == "x":
            st["far"] = [swap(o[0], "gx", n_gx, k) for o, k in zip(outs, far)]
            if job == firsts[g]:
                squares[g] = (outs[0][1], st["far"])
        elif kind == "h":
            st["hidden"], st["sibling"] = outs[0][0], core(outs[0][0])
            st["crossed"] = [swap(outs[0][0], "gx", n_gx, k) for k in far]
        else:
            totals[g] = outs[0]

    def tied(values):
        nonlocal chain
        values, chain = lax.optimization_barrier((values, chain))
        return values

    def forward(job):
        crossed = tied(state[job]["crossed"])
        state[job]["over"] = [(h, k) for h, k in zip(crossed, far)]
        state[job]["over"] += [(core(h), k ^ 1) for h, k in zip(crossed, far)]

    def reduce_over_gy():
        parts = dict(zip(sets[1], totals[1]))
        mask = 1
        while mask < n_gy:
            for j in [j for j in parts if j & mask]:
                arrived = swap(parts.pop(j), "gy", n_gy, mask)
                if j == mask:
                    landed.append(arrived)
                    continue
                arrived = tied(arrived).astype(jnp.float32)
                parts[j ^ mask] = (parts[j ^ mask].astype(jnp.float32) + arrived).astype(jnp.bfloat16)
            mask *= 2

    landed = []
    for names in STEPS:
        items = []
        for name in names:
            kind, job = name[0], int(name[1:] or 0)
            if kind == "r":
                forward(job)
                continue
            if kind == "z":
                reduce_over_gy()
                continue
            found = phases_of(kind, job)
            if kind == "d" and items and items[-1][0] == "d" and jobs[items[-1][1]][0] == jobs[job][0]:
                before, after = items.pop()[2][0], found[0]
                found = [
                    Down(
                        before.pieces + after.pieces, before.places + after.places, before.lows + after.lows, before.total,
                        block, columns, after.dtype,
                    )
                ]
            items.append((kind, job, found))
        results = run([p for _, _, ps in items for p in ps], table, gate_matrix, up_matrix, down_matrix, chain)
        chain = results[0][0]
        for kind, job, ps in items:
            deliver(kind, job, [results.pop(0) for _ in ps])

    landed.append(swap(totals[2][0], "gy", n_gy, 1))
    return sum((part.astype(jnp.float32) for part in landed), totals[0][0]).astype(jnp.bfloat16)


def solution(mesh):
    n_gx, n_gy = mesh.shape["gx"], mesh.shape["gy"]
    placed = (P(("groups", "gy"), "gx"), P("gx", "gy"), P("gx", "gy"), P("gy", "gx"))
    return jax.shard_map(
        functools.partial(on_device, n_gx, n_gy),
        mesh=mesh,
        in_specs=placed,
        out_specs=P(("groups", "gy"), "gx"),
        check_vma=False,
    )
```

```python
import functools

import jax
import jax.numpy as jnp
from jax import lax
from jax.experimental import pallas as pl
from jax.experimental.pallas import tpu as pltpu
from jax.sharding import PartitionSpec as P

EPS = 1e-05
LANES = 128
GU_TILE = 256
OUT_TILE = 512
COST = pl.CostEstimate(flops=1000, bytes_accessed=1000, transcendentals=0)
VMEM_LIMIT = 64 * 1024 * 1024 - 64 * 1024
ANY = pl.BlockSpec(memory_space=pl.ANY)
SMEM = pl.BlockSpec(memory_space=pltpu.SMEM)


def swap(value, axis, size, mask):
    return lax.ppermute(value, axis, [(i, i ^ mask) for i in range(size)])


def silu_product(gate, up, scale):
    gate = gate * scale
    return gate / (1.0 + jnp.exp(-gate)) * (up * scale)


class Group:
    def __init__(self, toks, block):
        self.toks, self.block, self.rows = toks, block, block * len(toks)

    def plain(self, table):
        return jnp.concatenate([lax.dynamic_slice_in_dim(t, table[i], self.block, 0) for t, i in self.toks], axis=0)


class GateUp:
    def __init__(self, group, place, low, width, recvs=(), carry=False, emit=False, squares=None, at=0, features=1):
        self.group, self.place, self.low, self.width, self.recvs = group, place, low, width, list(recvs)
        self.carry, self.emit, self.squares, self.at, self.features = carry, emit, squares, at, features
        rows, wide = group.rows, width + (LANES if carry else 0)
        self.outs = [jax.ShapeDtypeStruct((2, rows, wide) if squares is None else (rows, width), jnp.bfloat16)]
        if emit:
            self.outs.append(jax.ShapeDtypeStruct((rows, LANES), jnp.float32))

    def fits(self, depth, columns):
        return self.width % LANES == 0 and depth % LANES == 0 and self.group.block % 16 == 0

    def arrays(self):
        return [*self.recvs, *([self.squares[0], *self.squares[1]] if self.squares else [])]

    def plain(self, table, gate_matrix, up_matrix, down_matrix):
        tok, n = self.group.plain(table), self.width
        gate, up = (
            jnp.dot(
                tok, lax.dynamic_slice_in_dim(m, table[self.place] + self.low, n, 1), preferred_element_type=jnp.float32
            )
            for m in (gate_matrix, up_matrix)
        )
        for r in self.recvs:
            gate, up = gate + r[0, :, :n].astype(jnp.float32), up + r[1, :, :n].astype(jnp.float32)
        if self.squares:
            total = self.squares[0]
            for part in self.squares[1]:
                part = part[:, :, self.at : self.at + LANES].astype(jnp.float32)
                total = total + part[0] + part[1]
            return [silu_product(gate, up, lax.rsqrt(total[:, :1] / self.features + EPS)).astype(jnp.bfloat16)]
        if not self.carry:
            return [jnp.stack([gate, up]).astype(jnp.bfloat16)]
        values = tok.astype(jnp.float32)
        total = jnp.broadcast_to(jnp.sum(values * values, axis=1, keepdims=True), (tok.shape[0], LANES))
        for r in self.recvs:
            part = r[:, :, n : n + LANES].astype(jnp.float32)
            total = total + part[0] + part[1]
        high = total.astype(jnp.bfloat16).astype(jnp.float32)
        both = jnp.stack([jnp.concatenate([gate, high], axis=1), jnp.concatenate([up, total - high], axis=1)])
        return [both.astype(jnp.bfloat16)] + ([total] if self.emit else [])

    def scratch(self, depth):
        rows, n, tiles, n_recv = self.group.rows, self.width, pl.cdiv(self.width, GU_TILE), len(self.recvs)
        extra = len(self.squares[1]) if self.squares else n_recv if self.carry else 0
        return [
            pltpu.VMEM((tiles, depth, 2 * GU_TILE), jnp.bfloat16),
            pltpu.VMEM((n_recv, 2, rows, n) if n_recv else (1, 2, 16, LANES), jnp.bfloat16),
            pltpu.VMEM((extra, 2, rows, LANES) if extra else (1, 2, 16, LANES), jnp.bfloat16),
            pltpu.VMEM((rows, LANES) if self.squares or self.emit else (8, LANES), jnp.float32),
            pltpu.VMEM((tiles, 1 if self.squares else 2, rows, GU_TILE), jnp.bfloat16),
            pltpu.VMEM((2, rows, LANES) if self.carry else (2, 16, LANES), jnp.bfloat16),
            pltpu.SemaphoreType.DMA((2, tiles)),
            pltpu.SemaphoreType.DMA((n_recv + extra + 1,)),
            pltpu.SemaphoreType.DMA((tiles + 2,)),
        ]

    def bind(self, refs, table, arrays, outs, scratch):
        wbuf, rbuf, ebuf, qbuf, obuf, cbuf, wsem, rsem, osem = scratch
        n, rows, n_recv = self.width, self.group.rows, len(self.recvs)
        xbuf, hidden = refs["x"][id(self.group)], self.squares is not None
        full, rest = divmod(n, GU_TILE)
        tiles = full + (rest > 0)
        start = table[self.place] + self.low

        def weights(j, m):
            columns = pl.ds(pl.multiple_of(start + j * GU_TILE, LANES), m)
            return [
                pltpu.make_async_copy(refs[name].at[:, columns], wbuf.at[j, :, pl.ds(i * m, m)], wsem.at[i, j])
                for i, name in enumerate(("gate", "up"))
            ]

        def write(j, m):
            columns = pl.ds(pl.multiple_of(j * GU_TILE, LANES), m)
            if hidden:
                return pltpu.make_async_copy(obuf.at[j, 0, :, pl.ds(0, m)], outs[0].at[:, columns], osem.at[j])
            return pltpu.make_async_copy(obuf.at[j, :, :, pl.ds(0, m)], outs[0].at[:, :, columns], osem.at[j])

        def over_tiles(step):
            if full:
                @pl.loop(0, full)
                def _(j):
                    step(j, GU_TILE)
            if rest:
                step(full, rest)

        copies = [
            pltpu.make_async_copy(a.at[:, :, pl.ds(0, n)], rbuf.at[i], rsem.at[i]) for i, a in enumerate(arrays[:n_recv])
        ]
        extras = arrays[n_recv + 1 :] if hidden else arrays[:n_recv] if self.carry else []
        copies += [
            pltpu.make_async_copy(a.at[:, :, pl.ds(self.at if hidden else n, LANES)], ebuf.at[i], rsem.at[n_recv + i])
            for i, a in enumerate(extras)
        ]
        if hidden:
            copies.append(pltpu.make_async_copy(arrays[n_recv], qbuf, rsem.at[n_recv + len(extras)]))
        writes = []
        if self.carry:
            writes.append(pltpu.make_async_copy(cbuf, outs[0].at[:, :, pl.ds(n, LANES)], osem.at[tiles]))
        if self.emit:
            writes.append(pltpu.make_async_copy(qbuf, outs[1], osem.at[tiles + 1]))

        def begin():
            def step(j, m):
                for copy in weights(j, m):
                    copy.start()

            over_tiles(step)

        def compute():
            for copy in copies:
                copy.wait()
            extra = None
            for i in range(len(extras)):
                term = ebuf[i, 0].astype(jnp.float32) + ebuf[i, 1].astype(jnp.float32)
                extra = term if extra is None else extra + term
            if self.carry:
                values = xbuf[...].astype(jnp.float32)
                total = jnp.broadcast_to(jnp.sum(values * values, axis=1, keepdims=True), (rows, LANES))
                total = total if extra is None else total + extra
                high = total.astype(jnp.bfloat16)
                cbuf[0] = high
                cbuf[1] = (total - high.astype(jnp.float32)).astype(jnp.bfloat16)
                if self.emit:
                    qbuf[...] = total
                for copy in writes:
                    copy.start()
            if hidden:
                total = qbuf[...] if extra is None else qbuf[...] + extra
                qbuf[...] = lax.rsqrt(total / self.features + EPS)

            def step(j, m):
                for copy in weights(j, m):
                    copy.wait()
                both = jnp.dot(xbuf[...], wbuf[j, :, pl.ds(0, 2 * m)], preferred_element_type=jnp.float32)
                gate, up = both[:, :m], both[:, m:]
                columns = pl.ds(pl.multiple_of(j * GU_TILE, LANES), m)
                for r in range(n_recv):
                    gate = gate + rbuf[r, 0, :, columns].astype(jnp.float32)
                    up = up + rbuf[r, 1, :, columns].astype(jnp.float32)
                if hidden:
                    obuf[j, 0, :, pl.ds(0, m)] = silu_product(gate, up, qbuf[:, :1]).astype(jnp.bfloat16)
                else:
                    obuf[j, 0, :, pl.ds(0, m)] = gate.astype(jnp.bfloat16)
                    obuf[j, 1, :, pl.ds(0, m)] = up.astype(jnp.bfloat16)
                write(j, m).start()

            over_tiles(step)

        def drain():
            over_tiles(lambda j, m: write(j, m).wait())
            for copy in writes:
                copy.wait()

        return copies, begin, compute, drain


class Down:
    def __init__(self, parts, places, width, block, columns):
        self.parts, self.places, self.width, self.block, self.columns = parts, places, width, block, columns
        self.group, self.rows = None, sum(part[0][0].shape[0] for part in parts)
        self.outs = [jax.ShapeDtypeStruct((block, columns), jnp.bfloat16) for _ in range(self.rows // block)]

    def fits(self, depth, columns):
        sizes = [a.shape[1] for part in self.parts for a, _, _ in part]
        return all(n % LANES == 0 for n in sizes) and columns % OUT_TILE == 0 and self.block % 16 == 0

    def arrays(self):
        return [a for part in self.parts for a, _, _ in part]

    def plain(self, table, gate_matrix, up_matrix, down_matrix):
        result = jnp.concatenate(
            [
                sum(
                    jnp.dot(
                        a,
                        lax.dynamic_slice_in_dim(down_matrix, table[place] + low, a.shape[1], 0),
                        preferred_element_type=jnp.float32,
                    )
                    for a, place, low in part
                )
                for part in self.parts
            ],
            axis=0,
        )
        return jnp.split(result.astype(jnp.bfloat16), len(self.outs))

    def scratch(self, depth):
        tiles, whole = self.columns // OUT_TILE, len(self.places) * self.width
        return [
            pltpu.VMEM((self.rows, whole), jnp.bfloat16),
            pltpu.VMEM((tiles, whole, OUT_TILE), jnp.bfloat16),
            pltpu.VMEM((tiles, self.rows, OUT_TILE), jnp.bfloat16),
            pltpu.SemaphoreType.DMA((len(self.arrays()),)),
            pltpu.SemaphoreType.DMA((len(self.places), tiles)),
            pltpu.SemaphoreType.DMA((len(self.outs), tiles)),
        ]

    def bind(self, refs, table, arrays, outs, scratch):
        hbuf, dbuf, obuf, hsem, dsem, osem = scratch
        block, width, tiles = self.block, self.width, self.columns // OUT_TILE

        def columns(j):
            return pl.ds(pl.multiple_of(j * OUT_TILE, LANES), OUT_TILE)

        def weights(p, j):
            return pltpu.make_async_copy(
                refs["down"].at[pl.ds(pl.multiple_of(table[self.places[p]], LANES), width), columns(j)],
                dbuf.at[j, pl.ds(p * width, width)],
                dsem.at[p, j],
            )

        def write(i, j):
            return pltpu.make_async_copy(
                obuf.at[j, pl.ds(i * block, block)], outs[i].at[:, columns(j)], osem.at[i, j]
            )

        copies, row = [], 0
        for part in self.parts:
            rows = part[0][0].shape[0]
            for a, place, low in part:
                units = pl.ds(self.places.index(place) * width + low, a.shape[1])
                i = len(copies)
                copies.append(pltpu.make_async_copy(arrays[i], hbuf.at[pl.ds(row, rows), units], hsem.at[i]))
            row += rows

        def begin():
            @pl.loop(0, tiles)
            def _(j):
                for p in range(len(self.places)):
                    weights(p, j).start()

        def compute():
            for copy in copies:
                copy.wait()

            @pl.loop(0, tiles)
            def _(j):
                for p in range(len(self.places)):
                    weights(p, j).wait()
                result = jnp.dot(hbuf[...], dbuf[j], preferred_element_type=jnp.float32)
                obuf[j] = result.astype(jnp.bfloat16)
                for i in range(len(outs)):
                    write(i, j).start()

        def drain():
            @pl.loop(0, tiles)
            def _(j):
                for i in range(len(outs)):
                    write(i, j).wait()

        return copies, begin, compute, drain


def run(phases, table, gate_matrix, up_matrix, down_matrix, dep):
    depth, columns = gate_matrix.shape[0], down_matrix.shape[1]
    if not all(p.fits(depth, columns) for p in phases):
        return [p.plain(table, gate_matrix, up_matrix, down_matrix) for p in phases]
    operands = [gate_matrix, up_matrix, down_matrix]

    def index(array):
        for i, known in enumerate(operands):
            if known is array:
                return i
        operands.append(array)
        return len(operands) - 1

    groups = []
    for p in phases:
        if p.group is not None and all(p.group is not g for g in groups):
            groups.append(p.group)
    tok_places = [[index(t) for t, _ in g.toks] for g in groups]
    where = [[index(a) for a in p.arrays()] for p in phases]
    index(dep)
    outs = [o for p in phases for o in p.outs]
    scratch = [p.scratch(depth) for p in phases]

    def kernel(table_ref, *args):
        args = list(args)
        arrays = [args.pop(0) for _ in operands]
        out_refs = [args.pop(0) for _ in outs]
        refs = {"gate": arrays[0], "up": arrays[1], "down": arrays[2], "x": {}}
        ready = {}
        for g, places in zip(groups, tok_places):
            xbuf, xsem = args.pop(0), args.pop(0)
            refs["x"][id(g)] = xbuf
            ready[id(g)] = [
                pltpu.make_async_copy(
                    arrays[place].at[pl.ds(pl.multiple_of(table_ref[i], 16), g.block)],
                    xbuf.at[pl.ds(j * g.block, g.block)],
                    xsem.at[j],
                )
                for j, (place, (_, i)) in enumerate(zip(places, g.toks))
            ]
        bound = []
        for p, places, buffers in zip(phases, where, scratch):
            mine = [out_refs.pop(0) for _ in p.outs]
            held = [args.pop(0) for _ in buffers]
            bound.append(p.bind(refs, table_ref, [arrays[i] for i in places], mine, held))
        for copies in ready.values():
            for copy in copies:
                copy.start()
        for copies, begin, _, _ in bound:
            for copy in copies:
                copy.start()
            begin()
        for p, (_, _, compute, _) in zip(phases, bound):
            for copy in ready.pop(id(p.group), []):
                copy.wait()
            compute()
        for _, _, _, drain in bound:
            drain()

    results = list(
        pl.pallas_call(
            kernel,
            out_shape=outs,
            in_specs=[SMEM] + [ANY] * len(operands),
            out_specs=[ANY] * len(outs),
            scratch_shapes=[
                *[
                    buffer
                    for g in groups
                    for buffer in (pltpu.VMEM((g.rows, depth), jnp.bfloat16), pltpu.SemaphoreType.DMA((len(g.toks),)))
                ],
                *[buffer for buffers in scratch for buffer in buffers],
            ],
            compiler_params=pltpu.CompilerParams(vmem_limit_bytes=VMEM_LIMIT),
            cost_estimate=COST,
            name="step_" + "".join("g" if p.group is not None else "d" for p in phases),
        )(table, *operands)
    )
    return [[results.pop(0) for _ in p.outs] for p in phases]


STEPS = (
    ("s0",),
    ("s1",),
    ("x0",),
    ("x1",),
    ("h0",),
    ("h1",),
    ("r0", "r1", "s2", "s3"),
    ("x2",),
    ("x3",),
    ("s4",),
    ("h2",),
    ("h3",),
    ("x4",),
    ("r2", "r3", "d1"),
    ("h4",),
    ("z", "r4", "d02"),
)


def cut(width, part, parts):
    unit = LANES if width % LANES == 0 else 1
    return width // unit * part // parts * unit


def on_device(n_gx, n_gy, tokens, gate_matrix, up_matrix, down_matrix):
    features = tokens.shape[1] * n_gx
    width = gate_matrix.shape[1] // n_gx
    block, columns = tokens.shape[0], down_matrix.shape[1]
    far = [2 * k for k in range(1, n_gx // 2)]

    def core(value):
        return swap(value, "gx", n_gx, 1)

    gathered = lax.all_gather(tokens, "gy", axis=0, tiled=True)
    table = jnp.concatenate(
        [
            (lax.axis_index("gx") ^ jnp.arange(n_gx, dtype=jnp.int32)) * width,
            (lax.axis_index("gy") ^ jnp.arange(n_gy, dtype=jnp.int32)) * block,
            jnp.zeros((1,), jnp.int32),
        ]
    )
    sets = [[0], list(range(2, n_gy)), [1]]
    groups = [Group([(gathered, n_gx + j) if j else (tokens, n_gx + n_gy) for j in js], block) for js in sets]
    squares = {}
    half = cut(width, 7, 13)
    jobs = [(0, 0, half), (0, half, width - half), (1, 0, half), (1, half, width - half), (2, 0, width)]
    firsts = [min(i for i, job in enumerate(jobs) if job[0] == g) for g in range(len(groups))]
    state = [dict() for _ in jobs]
    totals = {}
    chain = tokens

    def phases_of(kind, job):
        g, low, n = jobs[job]
        group, st, first = groups[g], state[job], low == 0
        if kind == "s":
            return [GateUp(group, k ^ 1, low, n, carry=first and k > 0) for k in [*far, 0]]
        if kind == "x":
            return [
                GateUp(group, k, low, n, [st["lent"][i]], carry=first, emit=first and i == 0)
                for i, k in enumerate(far)
            ]
        if kind == "h":
            recvs = [st["lent"][-1], *st["far"]]
            return [GateUp(group, 0, low, n, recvs, squares=squares[g], at=jobs[firsts[g]][2], features=features)]

    def down(gs):
        parts = [
            [(h, q, jobs[i][1]) for i, st in enumerate(state) if jobs[i][0] == g for h, q in st["pieces"]] for g in gs
        ]
        return Down(parts, list(range(n_gx)), width, block, columns)

    def deliver(kind, job, outs):
        g, st = jobs[job][0], state[job]
        if kind == "s":
            st["lent"] = [core(o[0]) for o in outs]
        elif kind == "x":
            st["far"] = [swap(o[0], "gx", n_gx, k) for o, k in zip(outs, far)]
            if job == firsts[g]:
                squares[g] = (outs[0][1], st["far"])
        elif kind == "h":
            st["pieces"] = [(outs[0][0], 0), (core(outs[0][0]), 1)]
            st["crossed"] = [swap(outs[0][0], "gx", n_gx, k) for k in far]

    def tied(values):
        nonlocal chain
        values, chain = lax.optimization_barrier((values, chain))
        return values

    def forward(job):
        crossed = tied(state[job]["crossed"])
        state[job]["pieces"] += [(h, k) for h, k in zip(crossed, far)]
        state[job]["pieces"] += [(core(h), k ^ 1) for h, k in zip(crossed, far)]

    def reduce_over_gy():
        parts = dict(zip(sets[1], totals[1]))
        mask = 1
        while mask < n_gy:
            for j in [j for j in parts if j & mask]:
                arrived = swap(parts.pop(j), "gy", n_gy, mask)
                if j == mask:
                    landed.append(arrived)
                    continue
                arrived = tied(arrived).astype(jnp.float32)
                parts[j ^ mask] = (parts[j ^ mask].astype(jnp.float32) + arrived).astype(jnp.bfloat16)
            mask *= 2

    landed = []
    for names in STEPS:
        items = []
        for name in names:
            kind, job = name[0], int(name[1:] or 0)
            if kind == "r":
                forward(job)
                continue
            if kind == "z":
                reduce_over_gy()
                continue
            if kind == "d":
                items.append((kind, [int(g) for g in name[1:]], [down([int(g) for g in name[1:]])]))
            else:
                items.append((kind, job, phases_of(kind, job)))
        results = run([p for _, _, ps in items for p in ps], table, gate_matrix, up_matrix, down_matrix, chain)
        chain = results[0][0]
        for kind, job, ps in items:
            outs = [results.pop(0) for _ in ps]
            if kind != "d":
                deliver(kind, job, outs)
                continue
            for g in job:
                totals[g] = [outs[0].pop(0) for _ in sets[g]]

    landed.append(swap(totals[2][0], "gy", n_gy, 1))
    return sum(part.astype(jnp.float32) for part in [totals[0][0], *landed]).astype(jnp.bfloat16)


def solution(mesh):
    n_gx, n_gy = mesh.shape["gx"], mesh.shape["gy"]
    placed = (P(("groups", "gy"), "gx"), P("gx", "gy"), P("gx", "gy"), P("gy", "gx"))
    return jax.shard_map(
        functools.partial(on_device, n_gx, n_gy),
        mesh=mesh,
        in_specs=placed,
        out_specs=P(("groups", "gy"), "gx"),
        check_vma=False,
    )
```

```python
import functools

import jax
import jax.numpy as jnp
from jax import lax
from jax.experimental import pallas as pl
from jax.experimental.pallas import tpu as pltpu
from jax.sharding import PartitionSpec as P

EPS = 1e-05
LANES = 128
GU_TILE = 256
OUT_TILE = 512
COST = pl.CostEstimate(flops=1000, bytes_accessed=1000, transcendentals=0)
VMEM_LIMIT = 64 * 1024 * 1024 - 64 * 1024
ANY = pl.BlockSpec(memory_space=pl.ANY)
SMEM = pl.BlockSpec(memory_space=pltpu.SMEM)


def swap(value, axis, size, mask):
    return lax.ppermute(value, axis, [(i, i ^ mask) for i in range(size)])


def silu_product(gate, up, scale):
    gate = gate * scale
    return gate / (1.0 + jnp.exp(-gate)) * (up * scale)


class Group:
    def __init__(self, blocks, names, block):
        self.blocks, self.names, self.block, self.rows = blocks, names, block, block * len(names)

    def arrays(self):
        return [self.blocks[name] for name in self.names]


class GateUp:
    def __init__(self, group, place, low, width, recvs=(), carry=False, emit=False, squares=None, at=0, features=1):
        self.group, self.place, self.low, self.width, self.recvs = group, place, low, width, list(recvs)
        self.carry, self.emit, self.squares, self.at, self.features = carry, emit, squares, at, features
        rows, wide = group.rows, width + (LANES if carry else 0)
        self.outs = [jax.ShapeDtypeStruct((2, rows, wide) if squares is None else (rows, width), jnp.bfloat16)]
        if emit:
            self.outs.append(jax.ShapeDtypeStruct((rows, LANES), jnp.float32))

    def fits(self, depth, columns):
        return self.width % LANES == 0 and depth % LANES == 0 and self.group.block % 16 == 0

    def arrays(self):
        return [*self.recvs, *([self.squares[0], *self.squares[1]] if self.squares else [])]

    def plain(self, table, gate_matrix, up_matrix, down_matrix):
        tok, n = jnp.concatenate(self.group.arrays(), axis=0), self.width
        gate, up = (
            jnp.dot(
                tok, lax.dynamic_slice_in_dim(m, table[self.place] + self.low, n, 1), preferred_element_type=jnp.float32
            )
            for m in (gate_matrix, up_matrix)
        )
        for r in self.recvs:
            gate, up = gate + r[0, :, :n].astype(jnp.float32), up + r[1, :, :n].astype(jnp.float32)
        if self.squares:
            total = self.squares[0]
            for part in self.squares[1]:
                part = part[:, :, self.at : self.at + LANES].astype(jnp.float32)
                total = total + part[0] + part[1]
            return [silu_product(gate, up, lax.rsqrt(total[:, :1] / self.features + EPS)).astype(jnp.bfloat16)]
        if not self.carry:
            return [jnp.stack([gate, up]).astype(jnp.bfloat16)]
        values = tok.astype(jnp.float32)
        total = jnp.broadcast_to(jnp.sum(values * values, axis=1, keepdims=True), (tok.shape[0], LANES))
        for r in self.recvs:
            part = r[:, :, n : n + LANES].astype(jnp.float32)
            total = total + part[0] + part[1]
        high = total.astype(jnp.bfloat16).astype(jnp.float32)
        both = jnp.stack([jnp.concatenate([gate, high], axis=1), jnp.concatenate([up, total - high], axis=1)])
        return [both.astype(jnp.bfloat16)] + ([total] if self.emit else [])

    def scratch(self, depth):
        rows, n, tiles, n_recv = self.group.rows, self.width, pl.cdiv(self.width, GU_TILE), len(self.recvs)
        extra = len(self.squares[1]) if self.squares else n_recv if self.carry else 0
        return [
            pltpu.VMEM((tiles, depth, 2 * GU_TILE), jnp.bfloat16),
            pltpu.VMEM((n_recv, 2, rows, n) if n_recv else (1, 2, 16, LANES), jnp.bfloat16),
            pltpu.VMEM((extra, 2, rows, LANES) if extra else (1, 2, 16, LANES), jnp.bfloat16),
            pltpu.VMEM((rows, LANES) if self.squares or self.emit else (8, LANES), jnp.float32),
            pltpu.VMEM((tiles, 1 if self.squares else 2, rows, GU_TILE), jnp.bfloat16),
            pltpu.VMEM((2, rows, LANES) if self.carry else (2, 16, LANES), jnp.bfloat16),
            pltpu.SemaphoreType.DMA((2, tiles)),
            pltpu.SemaphoreType.DMA((n_recv + extra + 1,)),
            pltpu.SemaphoreType.DMA((tiles + 2,)),
        ]

    def bind(self, refs, table, arrays, outs, scratch):
        wbuf, rbuf, ebuf, qbuf, obuf, cbuf, wsem, rsem, osem = scratch
        n, rows, n_recv = self.width, self.group.rows, len(self.recvs)
        xbuf, hidden = refs["x"][id(self.group)], self.squares is not None
        full, rest = divmod(n, GU_TILE)
        tiles = full + (rest > 0)
        start = table[self.place] + self.low

        def weights(j, m):
            columns = pl.ds(pl.multiple_of(start + j * GU_TILE, LANES), m)
            return [
                pltpu.make_async_copy(refs[name].at[:, columns], wbuf.at[j, :, pl.ds(i * m, m)], wsem.at[i, j])
                for i, name in enumerate(("gate", "up"))
            ]

        def write(j, m):
            columns = pl.ds(pl.multiple_of(j * GU_TILE, LANES), m)
            if hidden:
                return pltpu.make_async_copy(obuf.at[j, 0, :, pl.ds(0, m)], outs[0].at[:, columns], osem.at[j])
            return pltpu.make_async_copy(obuf.at[j, :, :, pl.ds(0, m)], outs[0].at[:, :, columns], osem.at[j])

        def over_tiles(step):
            if full:
                @pl.loop(0, full)
                def _(j):
                    step(j, GU_TILE)
            if rest:
                step(full, rest)

        copies = [
            pltpu.make_async_copy(a.at[:, :, pl.ds(0, n)], rbuf.at[i], rsem.at[i]) for i, a in enumerate(arrays[:n_recv])
        ]
        extras = arrays[n_recv + 1 :] if hidden else arrays[:n_recv] if self.carry else []
        copies += [
            pltpu.make_async_copy(a.at[:, :, pl.ds(self.at if hidden else n, LANES)], ebuf.at[i], rsem.at[n_recv + i])
            for i, a in enumerate(extras)
        ]
        if hidden:
            copies.append(pltpu.make_async_copy(arrays[n_recv], qbuf, rsem.at[n_recv + len(extras)]))
        writes = []
        if self.carry:
            writes.append(pltpu.make_async_copy(cbuf, outs[0].at[:, :, pl.ds(n, LANES)], osem.at[tiles]))
        if self.emit:
            writes.append(pltpu.make_async_copy(qbuf, outs[1], osem.at[tiles + 1]))

        def begin():
            def step(j, m):
                for copy in weights(j, m):
                    copy.start()

            over_tiles(step)

        def compute():
            for copy in copies:
                copy.wait()
            extra = None
            for i in range(len(extras)):
                term = ebuf[i, 0].astype(jnp.float32) + ebuf[i, 1].astype(jnp.float32)
                extra = term if extra is None else extra + term
            if self.carry:
                values = xbuf[...].astype(jnp.float32)
                total = jnp.broadcast_to(jnp.sum(values * values, axis=1, keepdims=True), (rows, LANES))
                total = total if extra is None else total + extra
                high = total.astype(jnp.bfloat16)
                cbuf[0] = high
                cbuf[1] = (total - high.astype(jnp.float32)).astype(jnp.bfloat16)
                if self.emit:
                    qbuf[...] = total
                for copy in writes:
                    copy.start()
            if hidden:
                total = qbuf[...] if extra is None else qbuf[...] + extra
                qbuf[...] = lax.rsqrt(total / self.features + EPS)

            def step(j, m):
                for copy in weights(j, m):
                    copy.wait()
                both = jnp.dot(xbuf[...], wbuf[j, :, pl.ds(0, 2 * m)], preferred_element_type=jnp.float32)
                gate, up = both[:, :m], both[:, m:]
                columns = pl.ds(pl.multiple_of(j * GU_TILE, LANES), m)
                for r in range(n_recv):
                    gate = gate + rbuf[r, 0, :, columns].astype(jnp.float32)
                    up = up + rbuf[r, 1, :, columns].astype(jnp.float32)
                if hidden:
                    obuf[j, 0, :, pl.ds(0, m)] = silu_product(gate, up, qbuf[:, :1]).astype(jnp.bfloat16)
                else:
                    obuf[j, 0, :, pl.ds(0, m)] = gate.astype(jnp.bfloat16)
                    obuf[j, 1, :, pl.ds(0, m)] = up.astype(jnp.bfloat16)
                write(j, m).start()

            over_tiles(step)

        def drain():
            over_tiles(lambda j, m: write(j, m).wait())
            for copy in writes:
                copy.wait()

        return copies, begin, compute, drain


class Down:
    def __init__(self, parts, places, width, block, columns):
        self.parts, self.places, self.width, self.block, self.columns = parts, places, width, block, columns
        self.group, self.rows = None, sum(part[0][0].shape[0] for part in parts)
        self.outs = [jax.ShapeDtypeStruct((block, columns), jnp.bfloat16) for _ in range(self.rows // block)]

    def fits(self, depth, columns):
        sizes = [a.shape[1] for part in self.parts for a, _, _ in part]
        return all(n % LANES == 0 for n in sizes) and columns % OUT_TILE == 0 and self.block % 16 == 0

    def arrays(self):
        return [a for part in self.parts for a, _, _ in part]

    def plain(self, table, gate_matrix, up_matrix, down_matrix):
        result = jnp.concatenate(
            [
                sum(
                    jnp.dot(
                        a,
                        lax.dynamic_slice_in_dim(down_matrix, table[place] + low, a.shape[1], 0),
                        preferred_element_type=jnp.float32,
                    )
                    for a, place, low in part
                )
                for part in self.parts
            ],
            axis=0,
        )
        return jnp.split(result.astype(jnp.bfloat16), len(self.outs))

    def scratch(self, depth):
        tiles, whole = self.columns // OUT_TILE, len(self.places) * self.width
        return [
            pltpu.VMEM((self.rows, whole), jnp.bfloat16),
            pltpu.VMEM((tiles, whole, OUT_TILE), jnp.bfloat16),
            pltpu.VMEM((tiles, self.rows, OUT_TILE), jnp.bfloat16),
            pltpu.SemaphoreType.DMA((len(self.arrays()),)),
            pltpu.SemaphoreType.DMA((len(self.places), tiles)),
            pltpu.SemaphoreType.DMA((len(self.outs), tiles)),
        ]

    def bind(self, refs, table, arrays, outs, scratch):
        hbuf, dbuf, obuf, hsem, dsem, osem = scratch
        block, width, tiles = self.block, self.width, self.columns // OUT_TILE

        def columns(j):
            return pl.ds(pl.multiple_of(j * OUT_TILE, LANES), OUT_TILE)

        def weights(p, j):
            return pltpu.make_async_copy(
                refs["down"].at[pl.ds(pl.multiple_of(table[self.places[p]], LANES), width), columns(j)],
                dbuf.at[j, pl.ds(p * width, width)],
                dsem.at[p, j],
            )

        def write(i, j):
            return pltpu.make_async_copy(
                obuf.at[j, pl.ds(i * block, block)], outs[i].at[:, columns(j)], osem.at[i, j]
            )

        copies, row = [], 0
        for part in self.parts:
            rows = part[0][0].shape[0]
            for a, place, low in part:
                units = pl.ds(self.places.index(place) * width + low, a.shape[1])
                i = len(copies)
                copies.append(pltpu.make_async_copy(arrays[i], hbuf.at[pl.ds(row, rows), units], hsem.at[i]))
            row += rows

        def begin():
            @pl.loop(0, tiles)
            def _(j):
                for p in range(len(self.places)):
                    weights(p, j).start()

        def compute():
            for copy in copies:
                copy.wait()

            @pl.loop(0, tiles)
            def _(j):
                for p in range(len(self.places)):
                    weights(p, j).wait()
                result = jnp.dot(hbuf[...], dbuf[j], preferred_element_type=jnp.float32)
                obuf[j] = result.astype(jnp.bfloat16)
                for i in range(len(outs)):
                    write(i, j).start()

        def drain():
            @pl.loop(0, tiles)
            def _(j):
                for i in range(len(outs)):
                    write(i, j).wait()

        return copies, begin, compute, drain


def run(phases, table, gate_matrix, up_matrix, down_matrix, dep):
    depth, columns = gate_matrix.shape[0], down_matrix.shape[1]
    if not all(p.fits(depth, columns) for p in phases):
        return [p.plain(table, gate_matrix, up_matrix, down_matrix) for p in phases]
    operands = [gate_matrix, up_matrix, down_matrix]

    def index(array):
        for i, known in enumerate(operands):
            if known is array:
                return i
        operands.append(array)
        return len(operands) - 1

    groups = []
    for p in phases:
        if p.group is not None and all(p.group is not g for g in groups):
            groups.append(p.group)
    tok_places = [[index(t) for t in g.arrays()] for g in groups]
    where = [[index(a) for a in p.arrays()] for p in phases]
    index(dep)
    outs = [o for p in phases for o in p.outs]
    scratch = [p.scratch(depth) for p in phases]

    def kernel(table_ref, *args):
        args = list(args)
        arrays = [args.pop(0) for _ in operands]
        out_refs = [args.pop(0) for _ in outs]
        refs = {"gate": arrays[0], "up": arrays[1], "down": arrays[2], "x": {}}
        ready = {}
        for g, places in zip(groups, tok_places):
            xbuf, xsem = args.pop(0), args.pop(0)
            refs["x"][id(g)] = xbuf
            ready[id(g)] = [
                pltpu.make_async_copy(arrays[place], xbuf.at[pl.ds(j * g.block, g.block)], xsem.at[j])
                for j, place in enumerate(places)
            ]
        bound = []
        for p, places, buffers in zip(phases, where, scratch):
            mine = [out_refs.pop(0) for _ in p.outs]
            held = [args.pop(0) for _ in buffers]
            bound.append(p.bind(refs, table_ref, [arrays[i] for i in places], mine, held))
        for copies in ready.values():
            for copy in copies:
                copy.start()
        for copies, begin, _, _ in bound:
            for copy in copies:
                copy.start()
            begin()
        for p, (_, _, compute, _) in zip(phases, bound):
            for copy in ready.pop(id(p.group), []):
                copy.wait()
            compute()
        for _, _, _, drain in bound:
            drain()

    results = list(
        pl.pallas_call(
            kernel,
            out_shape=outs,
            in_specs=[SMEM] + [ANY] * len(operands),
            out_specs=[ANY] * len(outs),
            scratch_shapes=[
                *[
                    buffer
                    for g in groups
                    for buffer in (pltpu.VMEM((g.rows, depth), jnp.bfloat16), pltpu.SemaphoreType.DMA((len(g.names),)))
                ],
                *[buffer for buffers in scratch for buffer in buffers],
            ],
            compiler_params=pltpu.CompilerParams(vmem_limit_bytes=VMEM_LIMIT),
            cost_estimate=COST,
            name="step_" + "".join("g" if p.group is not None else "d" for p in phases),
        )(table, *operands)
    )
    return [[results.pop(0) for _ in p.outs] for p in phases]


STEPS = (
    ("s0",),
    ("s1",),
    ("x0",),
    ("x1",),
    ("h0",),
    ("t", "h1"),
    ("r0", "r1", "s2", "s3"),
    ("x2",),
    ("x3",),
    ("b", "s4"),
    ("h2",),
    ("h3",),
    ("x4",),
    ("r2", "r3", "d1"),
    ("h4",),
    ("z", "r4", "d02"),
)


def cut(width, part, parts):
    unit = LANES if width % LANES == 0 else 1
    return width // unit * part // parts * unit


def on_device(n_gx, n_gy, tokens, gate_matrix, up_matrix, down_matrix):
    features = tokens.shape[1] * n_gx
    width = gate_matrix.shape[1] // n_gx
    block, columns = tokens.shape[0], down_matrix.shape[1]
    far = [2 * k for k in range(1, n_gx // 2)]

    def core(value):
        return swap(value, "gx", n_gx, 1)

    table = jnp.concatenate(
        [(lax.axis_index("gx") ^ jnp.arange(n_gx, dtype=jnp.int32)) * width, jnp.zeros((1,), jnp.int32)]
    )
    blocks = {0: tokens}
    sets = [[0], list(range(2, n_gy)), [1]]
    groups = [Group(blocks, js, block) for js in sets]
    squares = {}
    half = cut(width, 7, 13)
    jobs = [(0, 0, half), (0, half, width - half), (1, 0, half), (1, half, width - half), (2, 0, width)]
    firsts = [min(i for i, job in enumerate(jobs) if job[0] == g) for g in range(len(groups))]
    state = [dict() for _ in jobs]
    totals = {}
    chain = tokens

    def phases_of(kind, job):
        g, low, n = jobs[job]
        group, st, first = groups[g], state[job], low == 0
        if kind == "s":
            return [GateUp(group, k ^ 1, low, n, carry=first and k > 0) for k in [*far, 0]]
        if kind == "x":
            return [
                GateUp(group, k, low, n, [st["lent"][i]], carry=first, emit=first and i == 0)
                for i, k in enumerate(far)
            ]
        if kind == "h":
            recvs = [st["lent"][-1], *st["far"]]
            return [GateUp(group, 0, low, n, recvs, squares=squares[g], at=jobs[firsts[g]][2], features=features)]

    def down(gs):
        parts = [
            [(h, q, jobs[i][1]) for i, st in enumerate(state) if jobs[i][0] == g for h, q in st["pieces"]] for g in gs
        ]
        return Down(parts, list(range(n_gx)), width, block, columns)

    def deliver(kind, job, outs):
        g, st = jobs[job][0], state[job]
        if kind == "s":
            st["lent"] = [core(o[0]) for o in outs]
        elif kind == "x":
            st["far"] = [swap(o[0], "gx", n_gx, k) for o, k in zip(outs, far)]
            if job == firsts[g]:
                squares[g] = (outs[0][1], st["far"])
        elif kind == "h":
            st["pieces"] = [(outs[0][0], 0), (core(outs[0][0]), 1)]
            st["crossed"] = [swap(outs[0][0], "gx", n_gx, k) for k in far]

    def tied(values):
        nonlocal chain
        values, chain = lax.optimization_barrier((values, chain))
        return values

    def forward(job):
        crossed = tied(state[job]["crossed"])
        state[job]["pieces"] += [(h, k) for h, k in zip(crossed, far)]
        state[job]["pieces"] += [(core(h), k ^ 1) for h, k in zip(crossed, far)]

    def reduce_over_gy():
        parts = dict(zip(sets[1], totals[1]))
        mask = 1
        while mask < n_gy:
            for j in [j for j in parts if j & mask]:
                arrived = swap(parts.pop(j), "gy", n_gy, mask)
                if j == mask:
                    landed.append(arrived)
                    continue
                arrived = tied(arrived).astype(jnp.float32)
                parts[j ^ mask] = (parts[j ^ mask].astype(jnp.float32) + arrived).astype(jnp.bfloat16)
            mask *= 2

    def gather_over_gy(mask):
        got = [j for j in blocks if j]
        blocks.update(zip(got, tied([blocks[j] for j in got])))
        for j in list(blocks) if mask > 1 else got:
            blocks[j ^ mask] = swap(blocks[j], "gy", n_gy, mask)

    landed = []
    mask = n_gy // 2
    gather_over_gy(mask)
    for names in STEPS:
        items = []
        for name in names:
            kind, job = name[0], int(name[1:] or 0)
            if kind == "r":
                forward(job)
                continue
            while kind == "t" and mask > 1:
                mask //= 2
                gather_over_gy(mask)
            if kind == "b":
                blocks[1] = tied(swap(tokens, "gy", n_gy, 1))
            if kind == "z":
                reduce_over_gy()
            if kind in "tbz":
                continue
            if kind == "d":
                items.append((kind, [int(g) for g in name[1:]], [down([int(g) for g in name[1:]])]))
            else:
                items.append((kind, job, phases_of(kind, job)))
        results = run([p for _, _, ps in items for p in ps], table, gate_matrix, up_matrix, down_matrix, chain)
        chain = results[0][0]
        for kind, job, ps in items:
            outs = [results.pop(0) for _ in ps]
            if kind != "d":
                deliver(kind, job, outs)
                continue
            for g in job:
                totals[g] = [outs[0].pop(0) for _ in sets[g]]

    landed, last = lax.optimization_barrier((landed, totals[2][0]))
    landed.append(swap(last, "gy", n_gy, 1))
    return sum(part.astype(jnp.float32) for part in [totals[0][0], *landed]).astype(jnp.bfloat16)


def solution(mesh):
    n_gx, n_gy = mesh.shape["gx"], mesh.shape["gy"]
    placed = (P(("groups", "gy"), "gx"), P("gx", "gy"), P("gx", "gy"), P("gy", "gx"))
    return jax.shard_map(
        functools.partial(on_device, n_gx, n_gy),
        mesh=mesh,
        in_specs=placed,
        out_specs=P(("groups", "gy"), "gx"),
        check_vma=False,
    )
```

```python
import functools

import jax
import jax.numpy as jnp
from jax import lax
from jax.experimental import pallas as pl
from jax.experimental.pallas import tpu as pltpu
from jax.sharding import PartitionSpec as P

EPS = 1e-05
LANES = 128
GU_TILE = 256
OUT_TILE = 512
SHORT, LONG = 1000, 10**11
VMEM_LIMIT = 64 * 1024 * 1024 - 64 * 1024
ANY = pl.BlockSpec(memory_space=pl.ANY)
SMEM = pl.BlockSpec(memory_space=pltpu.SMEM)


def swap(value, axis, size, mask):
    return lax.ppermute(value, axis, [(i, i ^ mask) for i in range(size)])


def silu_product(gate, up, scale):
    gate = gate * scale
    return gate / (1.0 + jnp.exp(-gate)) * (up * scale)


class Group:
    def __init__(self, blocks, names, block):
        self.blocks, self.names, self.block, self.rows = blocks, names, block, block * len(names)

    def arrays(self):
        return [self.blocks[name] for name in self.names]


class GateUp:
    def __init__(self, group, place, low, width, recvs=(), carry=False, emit=False, squares=None, at=0, features=1):
        self.group, self.place, self.low, self.width, self.recvs = group, place, low, width, list(recvs)
        self.carry, self.emit, self.squares, self.at, self.features = carry, emit, squares, at, features
        rows, wide = group.rows, width + (LANES if carry else 0)
        self.outs = [jax.ShapeDtypeStruct((2, rows, wide) if squares is None else (rows, width), jnp.bfloat16)]
        if emit:
            self.outs.append(jax.ShapeDtypeStruct((rows, LANES), jnp.float32))

    def fits(self, depth, columns):
        return self.width % LANES == 0 and depth % LANES == 0 and self.group.block % 16 == 0

    def arrays(self):
        return [*self.recvs, *([self.squares[0], *self.squares[1]] if self.squares else [])]

    def plain(self, table, gate_matrix, up_matrix, down_matrix):
        tok, n = jnp.concatenate(self.group.arrays(), axis=0), self.width
        gate, up = (
            jnp.dot(
                tok, lax.dynamic_slice_in_dim(m, table[self.place] + self.low, n, 1), preferred_element_type=jnp.float32
            )
            for m in (gate_matrix, up_matrix)
        )
        for r in self.recvs:
            gate, up = gate + r[0, :, :n].astype(jnp.float32), up + r[1, :, :n].astype(jnp.float32)
        if self.squares:
            total = self.squares[0]
            for part in self.squares[1]:
                part = part[:, :, self.at : self.at + LANES].astype(jnp.float32)
                total = total + part[0] + part[1]
            return [silu_product(gate, up, lax.rsqrt(total[:, :1] / self.features + EPS)).astype(jnp.bfloat16)]
        if not self.carry:
            return [jnp.stack([gate, up]).astype(jnp.bfloat16)]
        values = tok.astype(jnp.float32)
        total = jnp.broadcast_to(jnp.sum(values * values, axis=1, keepdims=True), (tok.shape[0], LANES))
        for r in self.recvs:
            part = r[:, :, n : n + LANES].astype(jnp.float32)
            total = total + part[0] + part[1]
        high = total.astype(jnp.bfloat16).astype(jnp.float32)
        both = jnp.stack([jnp.concatenate([gate, high], axis=1), jnp.concatenate([up, total - high], axis=1)])
        return [both.astype(jnp.bfloat16)] + ([total] if self.emit else [])

    def scratch(self, depth):
        rows, n, tiles, n_recv = self.group.rows, self.width, pl.cdiv(self.width, GU_TILE), len(self.recvs)
        extra = len(self.squares[1]) if self.squares else n_recv if self.carry else 0
        return [
            pltpu.VMEM((tiles, depth, 2 * GU_TILE), jnp.bfloat16),
            pltpu.VMEM((n_recv, 2, rows, n) if n_recv else (1, 2, 16, LANES), jnp.bfloat16),
            pltpu.VMEM((extra, 2, rows, LANES) if extra else (1, 2, 16, LANES), jnp.bfloat16),
            pltpu.VMEM((rows, LANES) if self.squares or self.emit else (8, LANES), jnp.float32),
            pltpu.VMEM((tiles, 1 if self.squares else 2, rows, GU_TILE), jnp.bfloat16),
            pltpu.VMEM((2, rows, LANES) if self.carry else (2, 16, LANES), jnp.bfloat16),
            pltpu.SemaphoreType.DMA((2, tiles)),
            pltpu.SemaphoreType.DMA((n_recv + extra + 1,)),
            pltpu.SemaphoreType.DMA((tiles + 2,)),
        ]

    def bind(self, refs, table, arrays, outs, scratch):
        wbuf, rbuf, ebuf, qbuf, obuf, cbuf, wsem, rsem, osem = scratch
        n, rows, n_recv = self.width, self.group.rows, len(self.recvs)
        xbuf, hidden = refs["x"][id(self.group)], self.squares is not None
        full, rest = divmod(n, GU_TILE)
        tiles = full + (rest > 0)
        start = table[self.place] + self.low

        def weights(j, m):
            columns = pl.ds(pl.multiple_of(start + j * GU_TILE, LANES), m)
            return [
                pltpu.make_async_copy(refs[name].at[:, columns], wbuf.at[j, :, pl.ds(i * m, m)], wsem.at[i, j])
                for i, name in enumerate(("gate", "up"))
            ]

        def write(j, m):
            columns = pl.ds(pl.multiple_of(j * GU_TILE, LANES), m)
            if hidden:
                return pltpu.make_async_copy(obuf.at[j, 0, :, pl.ds(0, m)], outs[0].at[:, columns], osem.at[j])
            return pltpu.make_async_copy(obuf.at[j, :, :, pl.ds(0, m)], outs[0].at[:, :, columns], osem.at[j])

        def over_tiles(step):
            if full:
                @pl.loop(0, full)
                def _(j):
                    step(j, GU_TILE)
            if rest:
                step(full, rest)

        copies = [
            pltpu.make_async_copy(a.at[:, :, pl.ds(0, n)], rbuf.at[i], rsem.at[i]) for i, a in enumerate(arrays[:n_recv])
        ]
        extras = arrays[n_recv + 1 :] if hidden else arrays[:n_recv] if self.carry else []
        copies += [
            pltpu.make_async_copy(a.at[:, :, pl.ds(self.at if hidden else n, LANES)], ebuf.at[i], rsem.at[n_recv + i])
            for i, a in enumerate(extras)
        ]
        if hidden:
            copies.append(pltpu.make_async_copy(arrays[n_recv], qbuf, rsem.at[n_recv + len(extras)]))
        writes = []
        if self.carry:
            writes.append(pltpu.make_async_copy(cbuf, outs[0].at[:, :, pl.ds(n, LANES)], osem.at[tiles]))
        if self.emit:
            writes.append(pltpu.make_async_copy(qbuf, outs[1], osem.at[tiles + 1]))

        def begin():
            def step(j, m):
                for copy in weights(j, m):
                    copy.start()

            over_tiles(step)

        def compute():
            for copy in copies:
                copy.wait()
            extra = None
            for i in range(len(extras)):
                term = ebuf[i, 0].astype(jnp.float32) + ebuf[i, 1].astype(jnp.float32)
                extra = term if extra is None else extra + term
            if self.carry:
                values = xbuf[...].astype(jnp.float32)
                total = jnp.broadcast_to(jnp.sum(values * values, axis=1, keepdims=True), (rows, LANES))
                total = total if extra is None else total + extra
                high = total.astype(jnp.bfloat16)
                cbuf[0] = high
                cbuf[1] = (total - high.astype(jnp.float32)).astype(jnp.bfloat16)
                if self.emit:
                    qbuf[...] = total
                for copy in writes:
                    copy.start()
            if hidden:
                total = qbuf[...] if extra is None else qbuf[...] + extra
                qbuf[...] = lax.rsqrt(total / self.features + EPS)

            def step(j, m):
                for copy in weights(j, m):
                    copy.wait()
                both = jnp.dot(xbuf[...], wbuf[j, :, pl.ds(0, 2 * m)], preferred_element_type=jnp.float32)
                gate, up = both[:, :m], both[:, m:]
                columns = pl.ds(pl.multiple_of(j * GU_TILE, LANES), m)
                for r in range(n_recv):
                    gate = gate + rbuf[r, 0, :, columns].astype(jnp.float32)
                    up = up + rbuf[r, 1, :, columns].astype(jnp.float32)
                if hidden:
                    obuf[j, 0, :, pl.ds(0, m)] = silu_product(gate, up, qbuf[:, :1]).astype(jnp.bfloat16)
                else:
                    obuf[j, 0, :, pl.ds(0, m)] = gate.astype(jnp.bfloat16)
                    obuf[j, 1, :, pl.ds(0, m)] = up.astype(jnp.bfloat16)
                write(j, m).start()

            over_tiles(step)

        def drain():
            over_tiles(lambda j, m: write(j, m).wait())
            for copy in writes:
                copy.wait()

        return copies, begin, compute, drain


class Down:
    def __init__(self, parts, places, width, block, columns):
        self.parts, self.places, self.width, self.block, self.columns = parts, places, width, block, columns
        self.group, self.rows = None, sum(part[0][0].shape[0] for part in parts)
        self.outs = [jax.ShapeDtypeStruct((block, columns), jnp.bfloat16) for _ in range(self.rows // block)]

    def fits(self, depth, columns):
        sizes = [a.shape[1] for part in self.parts for a, _, _ in part]
        return all(n % LANES == 0 for n in sizes) and columns % OUT_TILE == 0 and self.block % 16 == 0

    def arrays(self):
        return [a for part in self.parts for a, _, _ in part]

    def plain(self, table, gate_matrix, up_matrix, down_matrix):
        result = jnp.concatenate(
            [
                sum(
                    jnp.dot(
                        a,
                        lax.dynamic_slice_in_dim(down_matrix, table[place] + low, a.shape[1], 0),
                        preferred_element_type=jnp.float32,
                    )
                    for a, place, low in part
                )
                for part in self.parts
            ],
            axis=0,
        )
        return jnp.split(result.astype(jnp.bfloat16), len(self.outs))

    def scratch(self, depth):
        tiles, whole = self.columns // OUT_TILE, len(self.places) * self.width
        return [
            pltpu.VMEM((self.rows, whole), jnp.bfloat16),
            pltpu.VMEM((tiles, whole, OUT_TILE), jnp.bfloat16),
            pltpu.VMEM((tiles, self.rows, OUT_TILE), jnp.bfloat16),
            pltpu.SemaphoreType.DMA((len(self.arrays()),)),
            pltpu.SemaphoreType.DMA((len(self.places), tiles)),
            pltpu.SemaphoreType.DMA((len(self.outs), tiles)),
        ]

    def bind(self, refs, table, arrays, outs, scratch):
        hbuf, dbuf, obuf, hsem, dsem, osem = scratch
        block, width, tiles = self.block, self.width, self.columns // OUT_TILE

        def columns(j):
            return pl.ds(pl.multiple_of(j * OUT_TILE, LANES), OUT_TILE)

        def weights(p, j):
            return pltpu.make_async_copy(
                refs["down"].at[pl.ds(pl.multiple_of(table[self.places[p]], LANES), width), columns(j)],
                dbuf.at[j, pl.ds(p * width, width)],
                dsem.at[p, j],
            )

        def write(i, j):
            return pltpu.make_async_copy(
                obuf.at[j, pl.ds(i * block, block)], outs[i].at[:, columns(j)], osem.at[i, j]
            )

        copies, row = [], 0
        for part in self.parts:
            rows = part[0][0].shape[0]
            for a, place, low in part:
                units = pl.ds(self.places.index(place) * width + low, a.shape[1])
                i = len(copies)
                copies.append(pltpu.make_async_copy(arrays[i], hbuf.at[pl.ds(row, rows), units], hsem.at[i]))
            row += rows

        def begin():
            @pl.loop(0, tiles)
            def _(j):
                for p in range(len(self.places)):
                    weights(p, j).start()

        def compute():
            for copy in copies:
                copy.wait()

            @pl.loop(0, tiles)
            def _(j):
                for p in range(len(self.places)):
                    weights(p, j).wait()
                result = jnp.dot(hbuf[...], dbuf[j], preferred_element_type=jnp.float32)
                obuf[j] = result.astype(jnp.bfloat16)
                for i in range(len(outs)):
                    write(i, j).start()

        def drain():
            @pl.loop(0, tiles)
            def _(j):
                for i in range(len(outs)):
                    write(i, j).wait()

        return copies, begin, compute, drain


def run(phases, table, gate_matrix, up_matrix, down_matrix, dep, work):
    depth, columns = gate_matrix.shape[0], down_matrix.shape[1]
    if not all(p.fits(depth, columns) for p in phases):
        return [p.plain(table, gate_matrix, up_matrix, down_matrix) for p in phases]
    operands = [gate_matrix, up_matrix, down_matrix]

    def index(array):
        for i, known in enumerate(operands):
            if known is array:
                return i
        operands.append(array)
        return len(operands) - 1

    groups = []
    for p in phases:
        if p.group is not None and all(p.group is not g for g in groups):
            groups.append(p.group)
    tok_places = [[index(t) for t in g.arrays()] for g in groups]
    where = [[index(a) for a in p.arrays()] for p in phases]
    index(dep)
    outs = [o for p in phases for o in p.outs]
    scratch = [p.scratch(depth) for p in phases]

    def kernel(table_ref, *args):
        args = list(args)
        arrays = [args.pop(0) for _ in operands]
        out_refs = [args.pop(0) for _ in outs]
        refs = {"gate": arrays[0], "up": arrays[1], "down": arrays[2], "x": {}}
        ready = {}
        for g, places in zip(groups, tok_places):
            xbuf, xsem = args.pop(0), args.pop(0)
            refs["x"][id(g)] = xbuf
            ready[id(g)] = [
                pltpu.make_async_copy(arrays[place], xbuf.at[pl.ds(j * g.block, g.block)], xsem.at[j])
                for j, place in enumerate(places)
            ]
        bound = []
        for p, places, buffers in zip(phases, where, scratch):
            mine = [out_refs.pop(0) for _ in p.outs]
            held = [args.pop(0) for _ in buffers]
            bound.append(p.bind(refs, table_ref, [arrays[i] for i in places], mine, held))
        for copies in ready.values():
            for copy in copies:
                copy.start()
        for copies, begin, _, _ in bound:
            for copy in copies:
                copy.start()
            begin()
        for p, (_, _, compute, _) in zip(phases, bound):
            for copy in ready.pop(id(p.group), []):
                copy.wait()
            compute()
        for _, _, _, drain in bound:
            drain()

    results = list(
        pl.pallas_call(
            kernel,
            out_shape=outs,
            in_specs=[SMEM] + [ANY] * len(operands),
            out_specs=[ANY] * len(outs),
            scratch_shapes=[
                *[
                    buffer
                    for g in groups
                    for buffer in (pltpu.VMEM((g.rows, depth), jnp.bfloat16), pltpu.SemaphoreType.DMA((len(g.names),)))
                ],
                *[buffer for buffers in scratch for buffer in buffers],
            ],
            compiler_params=pltpu.CompilerParams(vmem_limit_bytes=VMEM_LIMIT),
            cost_estimate=pl.CostEstimate(flops=work, bytes_accessed=1000, transcendentals=0),
            name="step_" + "".join("g" if p.group is not None else "d" for p in phases),
        )(table, *operands)
    )
    return [[results.pop(0) for _ in p.outs] for p in phases]


STEPS = (
    ("s0",),
    ("s1",),
    ("x0",),
    ("x1",),
    ("t", "h0"),
    ("h1",),
    ("r0", "s2", "s3"),
    ("r1", "x2"),
    ("x3",),
    ("b", "s4"),
    ("h2",),
    ("f0", "f1", "h3"),
    ("x4",),
    ("r2", "r3", "d1"),
    ("h4",),
    ("z", "r4", "d02"),
)


def cut(width, part, parts):
    unit = LANES if width % LANES == 0 else 1
    return width // unit * part // parts * unit


def on_device(n_gx, n_gy, tokens, gate_matrix, up_matrix, down_matrix):
    features = tokens.shape[1] * n_gx
    width = gate_matrix.shape[1] // n_gx
    block, columns = tokens.shape[0], down_matrix.shape[1]
    far = [2 * k for k in range(1, n_gx // 2)]

    def core(value):
        return swap(value, "gx", n_gx, 1)

    table = jnp.concatenate(
        [(lax.axis_index("gx") ^ jnp.arange(n_gx, dtype=jnp.int32)) * width, jnp.zeros((1,), jnp.int32)]
    )
    blocks = {0: tokens}
    sets = [[0], list(range(2, n_gy)), [1]]
    groups = [Group(blocks, js, block) for js in sets]
    squares = {}
    half = cut(width, 7, 13)
    early = cut(width, 7, 13)
    jobs = [(0, 0, early), (0, early, width - early), (1, 0, half), (1, half, width - half), (2, 0, width)]
    firsts = [min(i for i, job in enumerate(jobs) if job[0] == g) for g in range(len(groups))]
    state = [dict() for _ in jobs]
    totals = {}
    chain = tokens

    def phases_of(kind, job):
        g, low, n = jobs[job]
        group, st, first = groups[g], state[job], low == 0
        if kind == "s":
            return [GateUp(group, k ^ 1, low, n, carry=first and k > 0) for k in [*far, 0]]
        if kind == "x":
            return [
                GateUp(group, k, low, n, [st["lent"][i]], carry=first, emit=first and i == 0)
                for i, k in enumerate(far)
            ]
        if kind == "h":
            recvs = [st["lent"][-1], *st["far"]]
            return [GateUp(group, 0, low, n, recvs, squares=squares[g], at=jobs[firsts[g]][2], features=features)]

    def down(gs):
        parts = [
            [(h, q, jobs[i][1]) for i, st in enumerate(state) if jobs[i][0] == g for h, q in st["pieces"]] for g in gs
        ]
        return Down(parts, list(range(n_gx)), width, block, columns)

    def deliver(kind, job, outs):
        g, st = jobs[job][0], state[job]
        if kind == "s":
            st["lent"] = [core(o[0]) for o in outs]
        elif kind == "x":
            st["far"] = [swap(o[0], "gx", n_gx, k) for o, k in zip(outs, far)]
            if job == firsts[g]:
                squares[g] = (outs[0][1], st["far"])
        elif kind == "h":
            st["pieces"] = [(outs[0][0], 0), (core(outs[0][0]), 1)]
            st["crossed"] = [swap(outs[0][0], "gx", n_gx, k) for k in far]

    def tied(values):
        nonlocal chain
        values, chain = lax.optimization_barrier((values, chain))
        return values

    def forward(job):
        crossed = tied(state[job]["crossed"])
        state[job]["pieces"] += [(h, k) for h, k in zip(crossed, far)]
        state[job]["pieces"] += [(core(h), k ^ 1) for h, k in zip(crossed, far)]

    def reduce_over_gy():
        parts = dict(zip(sets[1], totals[1]))
        mask = 1
        while mask < n_gy:
            for j in [j for j in parts if j & mask]:
                arrived = swap(parts.pop(j), "gy", n_gy, mask)
                if j == mask:
                    landed.append(arrived)
                    continue
                arrived = tied(arrived).astype(jnp.float32)
                parts[j ^ mask] = (parts[j ^ mask].astype(jnp.float32) + arrived).astype(jnp.bfloat16)
            mask *= 2

    def gather_over_gy(mask):
        got = [j for j in blocks if j]
        blocks.update(zip(got, tied([blocks[j] for j in got])))
        for j in list(blocks) if mask > 1 else got:
            blocks[j ^ mask] = swap(blocks[j], "gy", n_gy, mask)

    landed = []
    mask = n_gy // 2
    gather_over_gy(mask)
    for names in STEPS:
        items, work = [], LONG if "long" in names else SHORT
        for name in names:
            if name == "long":
                continue
            kind, job = name[0], int(name[1:] or 0)
            if kind == "r":
                forward(job)
                continue
            while kind == "t" and mask > 1:
                mask //= 2
                gather_over_gy(mask)
            if kind == "f":
                held, places = zip(*state[job]["pieces"])
                state[job]["pieces"] = list(zip(tied(list(held)), places))
            if kind == "b":
                blocks[1] = tied(swap(tokens, "gy", n_gy, 1))
            if kind == "z":
                reduce_over_gy()
            if kind in "tfbz":
                continue
            if kind == "d":
                items.append((kind, [int(g) for g in name[1:]], [down([int(g) for g in name[1:]])]))
            else:
                items.append((kind, job, phases_of(kind, job)))
        results = run([p for _, _, ps in items for p in ps], table, gate_matrix, up_matrix, down_matrix, chain, work)
        chain = results[0][0]
        for kind, job, ps in items:
            outs = [results.pop(0) for _ in ps]
            if kind != "d":
                deliver(kind, job, outs)
                continue
            for g in job:
                totals[g] = [outs[0].pop(0) for _ in sets[g]]

    landed, last = lax.optimization_barrier((landed, totals[2][0]))
    landed.append(swap(last, "gy", n_gy, 1))
    return sum(part.astype(jnp.float32) for part in [totals[0][0], *landed]).astype(jnp.bfloat16)


def solution(mesh):
    n_gx, n_gy = mesh.shape["gx"], mesh.shape["gy"]
    placed = (P(("groups", "gy"), "gx"), P("gx", "gy"), P("gx", "gy"), P("gy", "gx"))
    return jax.shard_map(
        functools.partial(on_device, n_gx, n_gy),
        mesh=mesh,
        in_specs=placed,
        out_specs=P(("groups", "gy"), "gx"),
        check_vma=False,
    )
```

```python
import functools

import jax
import jax.numpy as jnp
from jax import lax
from jax.experimental import pallas as pl
from jax.experimental.pallas import tpu as pltpu
from jax.sharding import PartitionSpec as P

EPS = 1e-05
LANES = 128
GU_TILE = 256
OUT_TILE = 512
SHORT, LONG = 1000, 10**11
VMEM_LIMIT = 64 * 1024 * 1024 - 64 * 1024
ANY = pl.BlockSpec(memory_space=pl.ANY)
SMEM = pl.BlockSpec(memory_space=pltpu.SMEM)


def swap(value, axis, size, mask):
    return lax.ppermute(value, axis, [(i, i ^ mask) for i in range(size)])


def silu_product(gate, up, scale):
    gate = gate * scale
    return gate / (1.0 + jnp.exp(-gate)) * (up * scale)


class Group:
    def __init__(self, blocks, names, block):
        self.blocks, self.names, self.block, self.rows = blocks, names, block, block * len(names)

    def arrays(self):
        return [self.blocks[name] for name in self.names]


class GateUp:
    def __init__(self, group, place, low, width, recvs=(), carry=False, emit=False, squares=None, at=0, features=1):
        self.group, self.place, self.low, self.width, self.recvs = group, place, low, width, list(recvs)
        self.carry, self.emit, self.squares, self.at, self.features = carry, emit, squares, at, features
        rows, wide = group.rows, width + (LANES if carry else 0)
        self.outs = [jax.ShapeDtypeStruct((2, rows, wide) if squares is None else (rows, width), jnp.bfloat16)]
        if emit:
            self.outs.append(jax.ShapeDtypeStruct((rows, LANES), jnp.float32))

    def fits(self, depth, columns):
        return self.width % LANES == 0 and depth % LANES == 0 and self.group.block % 16 == 0

    def arrays(self):
        return [*self.recvs, *([self.squares[0], *self.squares[1]] if self.squares else [])]

    def plain(self, table, gate_matrix, up_matrix, down_matrix):
        tok, n = jnp.concatenate(self.group.arrays(), axis=0), self.width
        gate, up = (
            jnp.dot(
                tok, lax.dynamic_slice_in_dim(m, table[self.place] + self.low, n, 1), preferred_element_type=jnp.float32
            )
            for m in (gate_matrix, up_matrix)
        )
        for r in self.recvs:
            gate, up = gate + r[0, :, :n].astype(jnp.float32), up + r[1, :, :n].astype(jnp.float32)
        if self.squares:
            total = self.squares[0]
            for part in self.squares[1]:
                part = part[:, :, self.at : self.at + LANES].astype(jnp.float32)
                total = total + part[0] + part[1]
            return [silu_product(gate, up, lax.rsqrt(total[:, :1] / self.features + EPS)).astype(jnp.bfloat16)]
        if not self.carry:
            return [jnp.stack([gate, up]).astype(jnp.bfloat16)]
        values = tok.astype(jnp.float32)
        total = jnp.broadcast_to(jnp.sum(values * values, axis=1, keepdims=True), (tok.shape[0], LANES))
        for r in self.recvs:
            part = r[:, :, n : n + LANES].astype(jnp.float32)
            total = total + part[0] + part[1]
        high = total.astype(jnp.bfloat16).astype(jnp.float32)
        both = jnp.stack([jnp.concatenate([gate, high], axis=1), jnp.concatenate([up, total - high], axis=1)])
        return [both.astype(jnp.bfloat16)] + ([total] if self.emit else [])

    def scratch(self, depth):
        rows, n, tiles, n_recv = self.group.rows, self.width, pl.cdiv(self.width, GU_TILE), len(self.recvs)
        extra = len(self.squares[1]) if self.squares else n_recv if self.carry else 0
        return [
            pltpu.VMEM((tiles, depth, 2 * GU_TILE), jnp.bfloat16),
            pltpu.VMEM((n_recv, 2, rows, n) if n_recv else (1, 2, 16, LANES), jnp.bfloat16),
            pltpu.VMEM((extra, 2, rows, LANES) if extra else (1, 2, 16, LANES), jnp.bfloat16),
            pltpu.VMEM((rows, LANES) if self.squares or self.emit else (8, LANES), jnp.float32),
            pltpu.VMEM((tiles, 1 if self.squares else 2, rows, GU_TILE), jnp.bfloat16),
            pltpu.VMEM((2, rows, LANES) if self.carry else (2, 16, LANES), jnp.bfloat16),
            pltpu.SemaphoreType.DMA((2, tiles)),
            pltpu.SemaphoreType.DMA((n_recv + extra + 1,)),
            pltpu.SemaphoreType.DMA((tiles + 2,)),
        ]

    def bind(self, refs, table, arrays, outs, scratch):
        wbuf, rbuf, ebuf, qbuf, obuf, cbuf, wsem, rsem, osem = scratch
        n, rows, n_recv = self.width, self.group.rows, len(self.recvs)
        xbuf, hidden = refs["x"][id(self.group)], self.squares is not None
        full, rest = divmod(n, GU_TILE)
        tiles = full + (rest > 0)
        start = table[self.place] + self.low

        def weights(j, m):
            columns = pl.ds(pl.multiple_of(start + j * GU_TILE, LANES), m)
            return [
                pltpu.make_async_copy(refs[name].at[:, columns], wbuf.at[j, :, pl.ds(i * m, m)], wsem.at[i, j])
                for i, name in enumerate(("gate", "up"))
            ]

        def write(j, m):
            columns = pl.ds(pl.multiple_of(j * GU_TILE, LANES), m)
            if hidden:
                return pltpu.make_async_copy(obuf.at[j, 0, :, pl.ds(0, m)], outs[0].at[:, columns], osem.at[j])
            return pltpu.make_async_copy(obuf.at[j, :, :, pl.ds(0, m)], outs[0].at[:, :, columns], osem.at[j])

        def over_tiles(step):
            if full:
                @pl.loop(0, full)
                def _(j):
                    step(j, GU_TILE)
            if rest:
                step(full, rest)

        copies = [
            pltpu.make_async_copy(a.at[:, :, pl.ds(0, n)], rbuf.at[i], rsem.at[i]) for i, a in enumerate(arrays[:n_recv])
        ]
        extras = arrays[n_recv + 1 :] if hidden else arrays[:n_recv] if self.carry else []
        copies += [
            pltpu.make_async_copy(a.at[:, :, pl.ds(self.at if hidden else n, LANES)], ebuf.at[i], rsem.at[n_recv + i])
            for i, a in enumerate(extras)
        ]
        if hidden:
            copies.append(pltpu.make_async_copy(arrays[n_recv], qbuf, rsem.at[n_recv + len(extras)]))
        writes = []
        if self.carry:
            writes.append(pltpu.make_async_copy(cbuf, outs[0].at[:, :, pl.ds(n, LANES)], osem.at[tiles]))
        if self.emit:
            writes.append(pltpu.make_async_copy(qbuf, outs[1], osem.at[tiles + 1]))

        def begin():
            def step(j, m):
                for copy in weights(j, m):
                    copy.start()

            over_tiles(step)

        def compute():
            for copy in copies:
                copy.wait()
            extra = None
            for i in range(len(extras)):
                term = ebuf[i, 0].astype(jnp.float32) + ebuf[i, 1].astype(jnp.float32)
                extra = term if extra is None else extra + term
            if self.carry:
                values = xbuf[...].astype(jnp.float32)
                total = jnp.broadcast_to(jnp.sum(values * values, axis=1, keepdims=True), (rows, LANES))
                total = total if extra is None else total + extra
                high = total.astype(jnp.bfloat16)
                cbuf[0] = high
                cbuf[1] = (total - high.astype(jnp.float32)).astype(jnp.bfloat16)
                if self.emit:
                    qbuf[...] = total
                for copy in writes:
                    copy.start()
            if hidden:
                total = qbuf[...] if extra is None else qbuf[...] + extra
                qbuf[...] = lax.rsqrt(total / self.features + EPS)

            def step(j, m):
                for copy in weights(j, m):
                    copy.wait()
                both = jnp.dot(xbuf[...], wbuf[j, :, pl.ds(0, 2 * m)], preferred_element_type=jnp.float32)
                gate, up = both[:, :m], both[:, m:]
                columns = pl.ds(pl.multiple_of(j * GU_TILE, LANES), m)
                for r in range(n_recv):
                    gate = gate + rbuf[r, 0, :, columns].astype(jnp.float32)
                    up = up + rbuf[r, 1, :, columns].astype(jnp.float32)
                if hidden:
                    obuf[j, 0, :, pl.ds(0, m)] = silu_product(gate, up, qbuf[:, :1]).astype(jnp.bfloat16)
                else:
                    obuf[j, 0, :, pl.ds(0, m)] = gate.astype(jnp.bfloat16)
                    obuf[j, 1, :, pl.ds(0, m)] = up.astype(jnp.bfloat16)
                write(j, m).start()

            over_tiles(step)

        def drain():
            over_tiles(lambda j, m: write(j, m).wait())
            for copy in writes:
                copy.wait()

        return copies, begin, compute, drain


class Down:
    def __init__(self, parts, places, width, block, first, columns):
        self.parts, self.places, self.width, self.block = parts, places, width, block
        self.first, self.columns = first, columns
        self.group, self.rows = None, sum(part[0][0].shape[0] for part in parts)
        self.outs = [jax.ShapeDtypeStruct((block, columns), jnp.bfloat16) for _ in range(self.rows // block)]

    def fits(self, depth, columns):
        sizes = [a.shape[1] for part in self.parts for a, _, _ in part]
        return all(n % LANES == 0 for n in sizes) and self.columns % OUT_TILE == 0 and self.block % 16 == 0

    def arrays(self):
        return [a for part in self.parts for a, _, _ in part]

    def plain(self, table, gate_matrix, up_matrix, down_matrix):
        result = jnp.concatenate(
            [
                sum(
                    jnp.dot(
                        a,
                        lax.dynamic_slice_in_dim(
                            down_matrix[:, self.first : self.first + self.columns], table[place] + low, a.shape[1], 0
                        ),
                        preferred_element_type=jnp.float32,
                    )
                    for a, place, low in part
                )
                for part in self.parts
            ],
            axis=0,
        )
        return jnp.split(result.astype(jnp.bfloat16), len(self.outs))

    def scratch(self, depth):
        tiles, whole = self.columns // OUT_TILE, len(self.places) * self.width
        return [
            pltpu.VMEM((self.rows, whole), jnp.bfloat16),
            pltpu.VMEM((tiles, whole, OUT_TILE), jnp.bfloat16),
            pltpu.VMEM((tiles, self.rows, OUT_TILE), jnp.bfloat16),
            pltpu.SemaphoreType.DMA((len(self.arrays()),)),
            pltpu.SemaphoreType.DMA((len(self.places), tiles)),
            pltpu.SemaphoreType.DMA((len(self.outs), tiles)),
        ]

    def bind(self, refs, table, arrays, outs, scratch):
        hbuf, dbuf, obuf, hsem, dsem, osem = scratch
        block, width, tiles = self.block, self.width, self.columns // OUT_TILE

        def columns(j):
            return pl.ds(pl.multiple_of(j * OUT_TILE, LANES), OUT_TILE)

        def weights(p, j):
            taken = pl.ds(pl.multiple_of(self.first + j * OUT_TILE, LANES), OUT_TILE)
            return pltpu.make_async_copy(
                refs["down"].at[pl.ds(pl.multiple_of(table[self.places[p]], LANES), width), taken],
                dbuf.at[j, pl.ds(p * width, width)],
                dsem.at[p, j],
            )

        def write(i, j):
            return pltpu.make_async_copy(
                obuf.at[j, pl.ds(i * block, block)], outs[i].at[:, columns(j)], osem.at[i, j]
            )

        copies, row = [], 0
        for part in self.parts:
            rows = part[0][0].shape[0]
            for a, place, low in part:
                units = pl.ds(self.places.index(place) * width + low, a.shape[1])
                i = len(copies)
                copies.append(pltpu.make_async_copy(arrays[i], hbuf.at[pl.ds(row, rows), units], hsem.at[i]))
            row += rows

        def begin():
            @pl.loop(0, tiles)
            def _(j):
                for p in range(len(self.places)):
                    weights(p, j).start()

        def compute():
            for copy in copies:
                copy.wait()

            @pl.loop(0, tiles)
            def _(j):
                for p in range(len(self.places)):
                    weights(p, j).wait()
                result = jnp.dot(hbuf[...], dbuf[j], preferred_element_type=jnp.float32)
                obuf[j] = result.astype(jnp.bfloat16)
                for i in range(len(outs)):
                    write(i, j).start()

        def drain():
            @pl.loop(0, tiles)
            def _(j):
                for i in range(len(outs)):
                    write(i, j).wait()

        return copies, begin, compute, drain


def run(phases, table, gate_matrix, up_matrix, down_matrix, dep, work):
    depth, columns = gate_matrix.shape[0], down_matrix.shape[1]
    if not all(p.fits(depth, columns) for p in phases):
        return [p.plain(table, gate_matrix, up_matrix, down_matrix) for p in phases]
    operands = [gate_matrix, up_matrix, down_matrix]

    def index(array):
        for i, known in enumerate(operands):
            if known is array:
                return i
        operands.append(array)
        return len(operands) - 1

    groups = []
    for p in phases:
        if p.group is not None and all(p.group is not g for g in groups):
            groups.append(p.group)
    tok_places = [[index(t) for t in g.arrays()] for g in groups]
    where = [[index(a) for a in p.arrays()] for p in phases]
    index(dep)
    outs = [o for p in phases for o in p.outs]
    scratch = [p.scratch(depth) for p in phases]

    def kernel(table_ref, *args):
        args = list(args)
        arrays = [args.pop(0) for _ in operands]
        out_refs = [args.pop(0) for _ in outs]
        refs = {"gate": arrays[0], "up": arrays[1], "down": arrays[2], "x": {}}
        ready = {}
        for g, places in zip(groups, tok_places):
            xbuf, xsem = args.pop(0), args.pop(0)
            refs["x"][id(g)] = xbuf
            ready[id(g)] = [
                pltpu.make_async_copy(arrays[place], xbuf.at[pl.ds(j * g.block, g.block)], xsem.at[j])
                for j, place in enumerate(places)
            ]
        bound = []
        for p, places, buffers in zip(phases, where, scratch):
            mine = [out_refs.pop(0) for _ in p.outs]
            held = [args.pop(0) for _ in buffers]
            bound.append(p.bind(refs, table_ref, [arrays[i] for i in places], mine, held))
        for copies in ready.values():
            for copy in copies:
                copy.start()
        for copies, begin, _, _ in bound:
            for copy in copies:
                copy.start()
            begin()
        for p, (_, _, compute, _) in zip(phases, bound):
            for copy in ready.pop(id(p.group), []):
                copy.wait()
            compute()
        for _, _, _, drain in bound:
            drain()

    results = list(
        pl.pallas_call(
            kernel,
            out_shape=outs,
            in_specs=[SMEM] + [ANY] * len(operands),
            out_specs=[ANY] * len(outs),
            scratch_shapes=[
                *[
                    buffer
                    for g in groups
                    for buffer in (pltpu.VMEM((g.rows, depth), jnp.bfloat16), pltpu.SemaphoreType.DMA((len(g.names),)))
                ],
                *[buffer for buffers in scratch for buffer in buffers],
            ],
            compiler_params=pltpu.CompilerParams(vmem_limit_bytes=VMEM_LIMIT),
            cost_estimate=pl.CostEstimate(flops=work, bytes_accessed=1000, transcendentals=0),
            name="step_" + "".join("g" if p.group is not None else "d" for p in phases),
        )(table, *operands)
    )
    return [[results.pop(0) for _ in p.outs] for p in phases]


STEPS = (
    ("s0",),
    ("s1",),
    ("x0",),
    ("x1",),
    ("t", "h0"),
    ("h1",),
    ("r0", "s2"),
    ("s3",),
    ("r1", "x2", "long"),
    ("x3",),
    ("b", "s4"),
    ("h2",),
    ("f0", "f1", "h3"),
    ("x4",),
    ("r2", "r3", "d1"),
    ("h4",),
    ("z", "r4", "d02l"),
    ("d02r",),
)


def cut(width, part, parts):
    unit = LANES if width % LANES == 0 else 1
    return width // unit * part // parts * unit


def on_device(n_gx, n_gy, tokens, gate_matrix, up_matrix, down_matrix):
    features = tokens.shape[1] * n_gx
    width = gate_matrix.shape[1] // n_gx
    block, columns = tokens.shape[0], down_matrix.shape[1]
    far = [2 * k for k in range(1, n_gx // 2)]

    def core(value):
        return swap(value, "gx", n_gx, 1)

    table = jnp.concatenate(
        [(lax.axis_index("gx") ^ jnp.arange(n_gx, dtype=jnp.int32)) * width, jnp.zeros((1,), jnp.int32)]
    )
    blocks = {0: tokens}
    sets = [[0], list(range(2, n_gy)), [1]]
    groups = [Group(blocks, js, block) for js in sets]
    squares = {}
    half = cut(width, 7, 13)
    early = cut(width, 7, 13)
    jobs = [(0, 0, early), (0, early, width - early), (1, 0, half), (1, half, width - half), (2, 0, width)]
    firsts = [min(i for i, job in enumerate(jobs) if job[0] == g) for g in range(len(groups))]
    state = [dict() for _ in jobs]
    totals = {}
    chain = tokens

    def phases_of(kind, job):
        g, low, n = jobs[job]
        group, st, first = groups[g], state[job], low == 0
        if kind == "s":
            return [GateUp(group, k ^ 1, low, n, carry=first and k > 0) for k in [*far, 0]]
        if kind == "x":
            return [
                GateUp(group, k, low, n, [st["lent"][i]], carry=first, emit=first and i == 0)
                for i, k in enumerate(far)
            ]
        if kind == "h":
            recvs = [st["lent"][-1], *st["far"]]
            return [GateUp(group, 0, low, n, recvs, squares=squares[g], at=jobs[firsts[g]][2], features=features)]

    def down(gs, half):
        parts = [
            [(h, q, jobs[i][1]) for i, st in enumerate(state) if jobs[i][0] == g for h, q in st["pieces"]] for g in gs
        ]
        low, high = {"l": (0, columns // 2), "r": (columns // 2, columns)}.get(half, (0, columns))
        return Down(parts, list(range(n_gx)), width, block, low, high - low)

    def deliver(kind, job, outs):
        g, st = jobs[job][0], state[job]
        if kind == "s":
            st["lent"] = [core(o[0]) for o in outs]
        elif kind == "x":
            st["far"] = [swap(o[0], "gx", n_gx, k) for o, k in zip(outs, far)]
            if job == firsts[g]:
                squares[g] = (outs[0][1], st["far"])
        elif kind == "h":
            st["pieces"] = [(outs[0][0], 0), (core(outs[0][0]), 1)]
            st["crossed"] = [swap(outs[0][0], "gx", n_gx, k) for k in far]

    def tied(values):
        nonlocal chain
        values, chain = lax.optimization_barrier((values, chain))
        return values

    def forward(job):
        crossed = tied(state[job]["crossed"])
        state[job]["pieces"] += [(h, k) for h, k in zip(crossed, far)]
        state[job]["pieces"] += [(core(h), k ^ 1) for h, k in zip(crossed, far)]

    def reduce_over_gy():
        parts = dict(zip(sets[1], totals[1][0]))
        mask = 1
        while mask < n_gy:
            for j in [j for j in parts if j & mask]:
                arrived = swap(parts.pop(j), "gy", n_gy, mask)
                if j == mask:
                    landed.append(arrived)
                    continue
                arrived = tied(arrived).astype(jnp.float32)
                parts[j ^ mask] = (parts[j ^ mask].astype(jnp.float32) + arrived).astype(jnp.bfloat16)
            mask *= 2

    def gather_over_gy(mask):
        got = [j for j in blocks if j]
        blocks.update(zip(got, tied([blocks[j] for j in got])))
        for j in list(blocks) if mask > 1 else got:
            blocks[j ^ mask] = swap(blocks[j], "gy", n_gy, mask)

    landed = []
    mask = n_gy // 2
    gather_over_gy(mask)
    for names in STEPS:
        items, work = [], LONG if "long" in names else SHORT
        for name in names:
            if name == "long":
                continue
            kind, job = name[0], int(name[1:].rstrip("lr") or 0)
            if kind == "r":
                forward(job)
                continue
            while kind == "t" and mask > 1:
                mask //= 2
                gather_over_gy(mask)
            if kind == "f":
                held, places = zip(*state[job]["pieces"])
                state[job]["pieces"] = list(zip(tied(list(held)), places))
            if kind == "b":
                blocks[1] = tied(swap(tokens, "gy", n_gy, 1))
            if kind == "z":
                reduce_over_gy()
            if kind in "tfbz":
                continue
            if kind == "d":
                gs = [int(g) for g in name[1:] if g.isdigit()]
                items.append((kind, gs, [down(gs, name[-1])]))
            else:
                items.append((kind, job, phases_of(kind, job)))
        results = run([p for _, _, ps in items for p in ps], table, gate_matrix, up_matrix, down_matrix, chain, work)
        chain = results[0][0]
        for kind, job, ps in items:
            outs = [results.pop(0) for _ in ps]
            if kind != "d":
                deliver(kind, job, outs)
                continue
            for g in job:
                totals.setdefault(g, []).append([outs[0].pop(0) for _ in sets[g]])

    lefts, rights = ([total[i][0] for total in (totals[0], totals[2])] for i in (0, 1))
    left = swap(lefts[1], "gy", n_gy, 1)
    landed, last = lax.optimization_barrier((landed, rights[1]))
    right = swap(last, "gy", n_gy, 1)
    middle = columns // 2
    halves = []
    for low, parts in ((0, [lefts[0], left]), (middle, [rights[0], right])):
        parts += [part[:, low : low + parts[0].shape[1]] for part in landed]
        halves.append(sum(part.astype(jnp.float32) for part in parts).astype(jnp.bfloat16))
    return jnp.concatenate(halves, axis=1)


def solution(mesh):
    n_gx, n_gy = mesh.shape["gx"], mesh.shape["gy"]
    placed = (P(("groups", "gy"), "gx"), P("gx", "gy"), P("gx", "gy"), P("gy", "gx"))
    return jax.shard_map(
        functools.partial(on_device, n_gx, n_gy),
        mesh=mesh,
        in_specs=placed,
        out_specs=P(("groups", "gy"), "gx"),
        check_vma=False,
    )
```

```python
import functools

import jax
import jax.numpy as jnp
from jax import lax
from jax.experimental import pallas as pl
from jax.experimental.pallas import tpu as pltpu
from jax.sharding import PartitionSpec as P

EPS = 1e-05
LANES = 128
GU_TILE = 256
OUT_TILE = 512
SHORT, LONG = 1000, 10**11
VMEM_LIMIT = 64 * 1024 * 1024 - 64 * 1024
ANY = pl.BlockSpec(memory_space=pl.ANY)
SMEM = pl.BlockSpec(memory_space=pltpu.SMEM)


def swap(value, axis, size, mask):
    return lax.ppermute(value, axis, [(i, i ^ mask) for i in range(size)])


def silu_product(gate, up, scale):
    gate = gate * scale
    return gate / (1.0 + jnp.exp(-gate)) * (up * scale)


class Group:
    def __init__(self, blocks, names, block):
        self.blocks, self.names, self.block, self.rows = blocks, names, block, block * len(names)

    def arrays(self):
        return [self.blocks[name] for name in self.names]


class GateUp:
    def __init__(self, group, place, low, width, recvs=(), carry=False, emit=False, squares=None, at=0, features=1):
        self.group, self.place, self.low, self.width, self.recvs = group, place, low, width, list(recvs)
        self.carry, self.emit, self.squares, self.at, self.features = carry, emit, squares, at, features
        rows, wide = group.rows, width + (LANES if carry else 0)
        self.outs = [jax.ShapeDtypeStruct((2, rows, wide) if squares is None else (rows, width), jnp.bfloat16)]
        if emit:
            self.outs.append(jax.ShapeDtypeStruct((rows, LANES), jnp.float32))

    def fits(self, depth, columns):
        return self.width % LANES == 0 and depth % LANES == 0 and self.group.block % 16 == 0

    def arrays(self):
        return [*self.recvs, *([self.squares[0], *self.squares[1]] if self.squares else [])]

    def plain(self, table, gate_matrix, up_matrix, down_matrix):
        tok, n = jnp.concatenate(self.group.arrays(), axis=0), self.width
        gate, up = (
            jnp.dot(
                tok, lax.dynamic_slice_in_dim(m, table[self.place] + self.low, n, 1), preferred_element_type=jnp.float32
            )
            for m in (gate_matrix, up_matrix)
        )
        for r in self.recvs:
            gate, up = gate + r[0, :, :n].astype(jnp.float32), up + r[1, :, :n].astype(jnp.float32)
        if self.squares:
            total = self.squares[0]
            for part in self.squares[1]:
                part = part[:, :, self.at : self.at + LANES].astype(jnp.float32)
                total = total + part[0] + part[1]
            return [silu_product(gate, up, lax.rsqrt(total[:, :1] / self.features + EPS)).astype(jnp.bfloat16)]
        if not self.carry:
            return [jnp.stack([gate, up]).astype(jnp.bfloat16)]
        values = tok.astype(jnp.float32)
        total = jnp.broadcast_to(jnp.sum(values * values, axis=1, keepdims=True), (tok.shape[0], LANES))
        for r in self.recvs:
            part = r[:, :, n : n + LANES].astype(jnp.float32)
            total = total + part[0] + part[1]
        high = total.astype(jnp.bfloat16).astype(jnp.float32)
        both = jnp.stack([jnp.concatenate([gate, high], axis=1), jnp.concatenate([up, total - high], axis=1)])
        return [both.astype(jnp.bfloat16)] + ([total] if self.emit else [])

    def scratch(self, depth):
        rows, n, tiles, n_recv = self.group.rows, self.width, pl.cdiv(self.width, GU_TILE), len(self.recvs)
        extra = len(self.squares[1]) if self.squares else n_recv if self.carry else 0
        return [
            pltpu.VMEM((tiles, depth, 2 * GU_TILE), jnp.bfloat16),
            pltpu.VMEM((n_recv, 2, rows, n) if n_recv else (1, 2, 16, LANES), jnp.bfloat16),
            pltpu.VMEM((extra, 2, rows, LANES) if extra else (1, 2, 16, LANES), jnp.bfloat16),
            pltpu.VMEM((rows, LANES) if self.squares or self.emit else (8, LANES), jnp.float32),
            pltpu.VMEM((tiles, 1 if self.squares else 2, rows, GU_TILE), jnp.bfloat16),
            pltpu.VMEM((2, rows, LANES) if self.carry else (2, 16, LANES), jnp.bfloat16),
            pltpu.SemaphoreType.DMA((2, tiles)),
            pltpu.SemaphoreType.DMA((n_recv + extra + 1,)),
            pltpu.SemaphoreType.DMA((tiles + 2,)),
        ]

    def bind(self, refs, table, arrays, outs, scratch):
        wbuf, rbuf, ebuf, qbuf, obuf, cbuf, wsem, rsem, osem = scratch
        n, rows, n_recv = self.width, self.group.rows, len(self.recvs)
        xbuf, hidden = refs["x"][id(self.group)], self.squares is not None
        full, rest = divmod(n, GU_TILE)
        tiles = full + (rest > 0)
        start = table[self.place] + self.low

        def weights(j, m):
            columns = pl.ds(pl.multiple_of(start + j * GU_TILE, LANES), m)
            return [
                pltpu.make_async_copy(refs[name].at[:, columns], wbuf.at[j, :, pl.ds(i * m, m)], wsem.at[i, j])
                for i, name in enumerate(("gate", "up"))
            ]

        def write(j, m):
            columns = pl.ds(pl.multiple_of(j * GU_TILE, LANES), m)
            if hidden:
                return pltpu.make_async_copy(obuf.at[j, 0, :, pl.ds(0, m)], outs[0].at[:, columns], osem.at[j])
            return pltpu.make_async_copy(obuf.at[j, :, :, pl.ds(0, m)], outs[0].at[:, :, columns], osem.at[j])

        def over_tiles(step):
            if full:
                @pl.loop(0, full)
                def _(j):
                    step(j, GU_TILE)
            if rest:
                step(full, rest)

        copies = [
            pltpu.make_async_copy(a.at[:, :, pl.ds(0, n)], rbuf.at[i], rsem.at[i]) for i, a in enumerate(arrays[:n_recv])
        ]
        extras = arrays[n_recv + 1 :] if hidden else arrays[:n_recv] if self.carry else []
        copies += [
            pltpu.make_async_copy(a.at[:, :, pl.ds(self.at if hidden else n, LANES)], ebuf.at[i], rsem.at[n_recv + i])
            for i, a in enumerate(extras)
        ]
        if hidden:
            copies.append(pltpu.make_async_copy(arrays[n_recv], qbuf, rsem.at[n_recv + len(extras)]))
        writes = []
        if self.carry:
            writes.append(pltpu.make_async_copy(cbuf, outs[0].at[:, :, pl.ds(n, LANES)], osem.at[tiles]))
        if self.emit:
            writes.append(pltpu.make_async_copy(qbuf, outs[1], osem.at[tiles + 1]))

        def begin():
            def step(j, m):
                for copy in weights(j, m):
                    copy.start()

            over_tiles(step)

        def compute():
            for copy in copies:
                copy.wait()
            extra = None
            for i in range(len(extras)):
                term = ebuf[i, 0].astype(jnp.float32) + ebuf[i, 1].astype(jnp.float32)
                extra = term if extra is None else extra + term
            if self.carry:
                values = xbuf[...].astype(jnp.float32)
                total = jnp.broadcast_to(jnp.sum(values * values, axis=1, keepdims=True), (rows, LANES))
                total = total if extra is None else total + extra
                high = total.astype(jnp.bfloat16)
                cbuf[0] = high
                cbuf[1] = (total - high.astype(jnp.float32)).astype(jnp.bfloat16)
                if self.emit:
                    qbuf[...] = total
                for copy in writes:
                    copy.start()
            if hidden:
                total = qbuf[...] if extra is None else qbuf[...] + extra
                qbuf[...] = lax.rsqrt(total / self.features + EPS)

            def step(j, m):
                for copy in weights(j, m):
                    copy.wait()
                both = jnp.dot(xbuf[...], wbuf[j, :, pl.ds(0, 2 * m)], preferred_element_type=jnp.float32)
                gate, up = both[:, :m], both[:, m:]
                columns = pl.ds(pl.multiple_of(j * GU_TILE, LANES), m)
                for r in range(n_recv):
                    gate = gate + rbuf[r, 0, :, columns].astype(jnp.float32)
                    up = up + rbuf[r, 1, :, columns].astype(jnp.float32)
                if hidden:
                    obuf[j, 0, :, pl.ds(0, m)] = silu_product(gate, up, qbuf[:, :1]).astype(jnp.bfloat16)
                else:
                    obuf[j, 0, :, pl.ds(0, m)] = gate.astype(jnp.bfloat16)
                    obuf[j, 1, :, pl.ds(0, m)] = up.astype(jnp.bfloat16)
                write(j, m).start()

            over_tiles(step)

        def drain():
            over_tiles(lambda j, m: write(j, m).wait())
            for copy in writes:
                copy.wait()

        return copies, begin, compute, drain


class Down:
    def __init__(self, parts, places, width, block, first, columns):
        self.parts, self.places, self.width, self.block = parts, places, width, block
        self.first, self.columns = first, columns
        self.group, self.rows = None, sum(part[0][0].shape[0] for part in parts)
        self.outs = [jax.ShapeDtypeStruct((block, columns), jnp.bfloat16) for _ in range(self.rows // block)]

    def fits(self, depth, columns):
        sizes = [a.shape[1] for part in self.parts for a, _, _ in part]
        return all(n % LANES == 0 for n in sizes) and self.columns % OUT_TILE == 0 and self.block % 16 == 0

    def arrays(self):
        return [a for part in self.parts for a, _, _ in part]

    def plain(self, table, gate_matrix, up_matrix, down_matrix):
        result = jnp.concatenate(
            [
                sum(
                    jnp.dot(
                        a,
                        lax.dynamic_slice_in_dim(
                            down_matrix[:, self.first : self.first + self.columns], table[place] + low, a.shape[1], 0
                        ),
                        preferred_element_type=jnp.float32,
                    )
                    for a, place, low in part
                )
                for part in self.parts
            ],
            axis=0,
        )
        return jnp.split(result.astype(jnp.bfloat16), len(self.outs))

    def scratch(self, depth):
        tiles, whole = self.columns // OUT_TILE, len(self.places) * self.width
        return [
            pltpu.VMEM((self.rows, whole), jnp.bfloat16),
            pltpu.VMEM((tiles, whole, OUT_TILE), jnp.bfloat16),
            pltpu.VMEM((tiles, self.rows, OUT_TILE), jnp.bfloat16),
            pltpu.SemaphoreType.DMA((len(self.arrays()),)),
            pltpu.SemaphoreType.DMA((len(self.places), tiles)),
            pltpu.SemaphoreType.DMA((len(self.outs), tiles)),
        ]

    def bind(self, refs, table, arrays, outs, scratch):
        hbuf, dbuf, obuf, hsem, dsem, osem = scratch
        block, width, tiles = self.block, self.width, self.columns // OUT_TILE

        def columns(j):
            return pl.ds(pl.multiple_of(j * OUT_TILE, LANES), OUT_TILE)

        def weights(p, j):
            taken = pl.ds(pl.multiple_of(self.first + j * OUT_TILE, LANES), OUT_TILE)
            return pltpu.make_async_copy(
                refs["down"].at[pl.ds(pl.multiple_of(table[self.places[p]], LANES), width), taken],
                dbuf.at[j, pl.ds(p * width, width)],
                dsem.at[p, j],
            )

        def write(i, j):
            return pltpu.make_async_copy(
                obuf.at[j, pl.ds(i * block, block)], outs[i].at[:, columns(j)], osem.at[i, j]
            )

        copies, row = [], 0
        for part in self.parts:
            rows = part[0][0].shape[0]
            for a, place, low in part:
                units = pl.ds(self.places.index(place) * width + low, a.shape[1])
                i = len(copies)
                copies.append(pltpu.make_async_copy(arrays[i], hbuf.at[pl.ds(row, rows), units], hsem.at[i]))
            row += rows

        def begin():
            @pl.loop(0, tiles)
            def _(j):
                for p in range(len(self.places)):
                    weights(p, j).start()

        def compute():
            for copy in copies:
                copy.wait()

            @pl.loop(0, tiles)
            def _(j):
                for p in range(len(self.places)):
                    weights(p, j).wait()
                result = jnp.dot(hbuf[...], dbuf[j], preferred_element_type=jnp.float32)
                obuf[j] = result.astype(jnp.bfloat16)
                for i in range(len(outs)):
                    write(i, j).start()

        def drain():
            @pl.loop(0, tiles)
            def _(j):
                for i in range(len(outs)):
                    write(i, j).wait()

        return copies, begin, compute, drain


def run(phases, table, gate_matrix, up_matrix, down_matrix, dep, work):
    depth, columns = gate_matrix.shape[0], down_matrix.shape[1]
    if not all(p.fits(depth, columns) for p in phases):
        return [p.plain(table, gate_matrix, up_matrix, down_matrix) for p in phases]
    operands = [gate_matrix, up_matrix, down_matrix]

    def index(array):
        for i, known in enumerate(operands):
            if known is array:
                return i
        operands.append(array)
        return len(operands) - 1

    groups = []
    for p in phases:
        if p.group is not None and all(p.group is not g for g in groups):
            groups.append(p.group)
    tok_places = [[index(t) for t in g.arrays()] for g in groups]
    where = [[index(a) for a in p.arrays()] for p in phases]
    index(dep)
    outs = [o for p in phases for o in p.outs]
    scratch = [p.scratch(depth) for p in phases]

    def kernel(table_ref, *args):
        args = list(args)
        arrays = [args.pop(0) for _ in operands]
        out_refs = [args.pop(0) for _ in outs]
        refs = {"gate": arrays[0], "up": arrays[1], "down": arrays[2], "x": {}}
        ready = {}
        for g, places in zip(groups, tok_places):
            xbuf, xsem = args.pop(0), args.pop(0)
            refs["x"][id(g)] = xbuf
            ready[id(g)] = [
                pltpu.make_async_copy(arrays[place], xbuf.at[pl.ds(j * g.block, g.block)], xsem.at[j])
                for j, place in enumerate(places)
            ]
        bound = []
        for p, places, buffers in zip(phases, where, scratch):
            mine = [out_refs.pop(0) for _ in p.outs]
            held = [args.pop(0) for _ in buffers]
            bound.append(p.bind(refs, table_ref, [arrays[i] for i in places], mine, held))
        for copies in ready.values():
            for copy in copies:
                copy.start()
        for copies, begin, _, _ in bound:
            for copy in copies:
                copy.start()
            begin()
        for p, (_, _, compute, _) in zip(phases, bound):
            for copy in ready.pop(id(p.group), []):
                copy.wait()
            compute()
        for _, _, _, drain in bound:
            drain()

    results = list(
        pl.pallas_call(
            kernel,
            out_shape=outs,
            in_specs=[SMEM] + [ANY] * len(operands),
            out_specs=[ANY] * len(outs),
            scratch_shapes=[
                *[
                    buffer
                    for g in groups
                    for buffer in (pltpu.VMEM((g.rows, depth), jnp.bfloat16), pltpu.SemaphoreType.DMA((len(g.names),)))
                ],
                *[buffer for buffers in scratch for buffer in buffers],
            ],
            compiler_params=pltpu.CompilerParams(vmem_limit_bytes=VMEM_LIMIT),
            cost_estimate=pl.CostEstimate(flops=work, bytes_accessed=1000, transcendentals=0),
            name="step_" + "".join("g" if p.group is not None else "d" for p in phases),
        )(table, *operands)
    )
    return [[results.pop(0) for _ in p.outs] for p in phases]


STEPS = (
    ("s0",),
    ("s1",),
    ("x0",),
    ("t", "x1"),
    ("p0", "s2"),
    ("p1", "s3", "long"),
    ("x2",),
    ("h0",),
    ("h1",),
    ("x3",),
    ("b", "s4"),
    ("h2",),
    ("h3",),
    ("r0", "r1", "x4"),
    ("f0", "f1", "r2", "r3", "d1"),
    ("h4",),
    ("z", "r4", "d02"),
)


def cut(width, part, parts):
    unit = LANES if width % LANES == 0 else 1
    return width // unit * part // parts * unit


def on_device(n_gx, n_gy, tokens, gate_matrix, up_matrix, down_matrix):
    features = tokens.shape[1] * n_gx
    width = gate_matrix.shape[1] // n_gx
    block, columns = tokens.shape[0], down_matrix.shape[1]
    far = [2 * k for k in range(1, n_gx // 2)]

    def core(value):
        return swap(value, "gx", n_gx, 1)

    table = jnp.concatenate(
        [(lax.axis_index("gx") ^ jnp.arange(n_gx, dtype=jnp.int32)) * width, jnp.zeros((1,), jnp.int32)]
    )
    blocks = {0: tokens}
    sets = [[0], list(range(2, n_gy)), [1]]
    groups = [Group(blocks, js, block) for js in sets]
    squares = {}
    half = cut(width, 7, 13)
    early = cut(width, 6, 13)
    jobs = [(0, 0, early), (0, early, width - early), (1, 0, half), (1, half, width - half), (2, 0, width)]
    firsts = [min(i for i, job in enumerate(jobs) if job[0] == g) for g in range(len(groups))]
    state = [dict() for _ in jobs]
    totals = {}
    chain = tokens

    def phases_of(kind, job):
        g, low, n = jobs[job]
        group, st, first = groups[g], state[job], low == 0
        if kind == "s":
            return [GateUp(group, k ^ 1, low, n, carry=first and k > 0) for k in [*far, 0]]
        if kind == "x":
            return [
                GateUp(group, k, low, n, [st["lent"][i]], carry=first, emit=first and i == 0)
                for i, k in enumerate(far)
            ]
        if kind == "h":
            recvs = [st["lent"][-1], *st["far"]]
            return [GateUp(group, 0, low, n, recvs, squares=squares[g], at=jobs[firsts[g]][2], features=features)]

    def down(gs, half):
        parts = [
            [(h, q, jobs[i][1]) for i, st in enumerate(state) if jobs[i][0] == g for h, q in st["pieces"]] for g in gs
        ]
        low, high = {"l": (0, columns // 2), "r": (columns // 2, columns)}.get(half, (0, columns))
        return Down(parts, list(range(n_gx)), width, block, low, high - low)

    def deliver(kind, job, outs):
        g, st = jobs[job][0], state[job]
        if kind == "s":
            st["lent"] = [core(o[0]) for o in outs]
        elif kind == "x":
            st["far"] = [swap(o[0], "gx", n_gx, k) for o, k in zip(outs, far)]
            if job == firsts[g]:
                squares[g] = (outs[0][1], st["far"])
        elif kind == "h":
            st["pieces"] = [(outs[0][0], 0), (core(outs[0][0]), 1)]
            st["crossed"] = [swap(outs[0][0], "gx", n_gx, k) for k in far]

    def tied(values):
        nonlocal chain
        values, chain = lax.optimization_barrier((values, chain))
        return values

    def forward(job):
        crossed = tied(state[job]["crossed"])
        state[job]["pieces"] += [(h, k) for h, k in zip(crossed, far)]
        state[job]["pieces"] += [(core(h), k ^ 1) for h, k in zip(crossed, far)]

    def reduce_over_gy():
        parts = dict(zip(sets[1], totals[1][0]))
        mask = 1
        while mask < n_gy:
            for j in [j for j in parts if j & mask]:
                arrived = swap(parts.pop(j), "gy", n_gy, mask)
                if j == mask:
                    landed.append(arrived)
                    continue
                arrived = tied(arrived).astype(jnp.float32)
                parts[j ^ mask] = (parts[j ^ mask].astype(jnp.float32) + arrived).astype(jnp.bfloat16)
            mask *= 2

    def gather_over_gy(mask):
        got = [j for j in blocks if j]
        blocks.update(zip(got, tied([blocks[j] for j in got])))
        for j in list(blocks) if mask > 1 else got:
            blocks[j ^ mask] = swap(blocks[j], "gy", n_gy, mask)

    landed = []
    mask = n_gy // 2
    gather_over_gy(mask)
    for names in STEPS:
        items, work = [], LONG if "long" in names else SHORT
        for name in names:
            if name == "long":
                continue
            kind, job = name[0], int(name[1:].rstrip("lr") or 0)
            if kind == "r":
                forward(job)
                continue
            while kind == "t" and mask > 1:
                mask //= 2
                gather_over_gy(mask)
            if kind == "p":
                state[job]["far"] = tied(state[job]["far"])
                if job == firsts[jobs[job][0]]:
                    squares[jobs[job][0]] = (squares[jobs[job][0]][0], state[job]["far"])
            if kind == "f":
                held, places = zip(*state[job]["pieces"])
                state[job]["pieces"] = list(zip(tied(list(held)), places))
            if kind == "b":
                blocks[1] = tied(swap(tokens, "gy", n_gy, 1))
            if kind == "z":
                reduce_over_gy()
            if kind in "tpfbz":
                continue
            if kind == "d":
                gs = [int(g) for g in name[1:] if g.isdigit()]
                items.append((kind, gs, [down(gs, name[-1])]))
            else:
                items.append((kind, job, phases_of(kind, job)))
        results = run([p for _, _, ps in items for p in ps], table, gate_matrix, up_matrix, down_matrix, chain, work)
        chain = results[0][0]
        for kind, job, ps in items:
            outs = [results.pop(0) for _ in ps]
            if kind != "d":
                deliver(kind, job, outs)
                continue
            for g in job:
                totals.setdefault(g, []).append([outs[0].pop(0) for _ in sets[g]])

    landed, last = lax.optimization_barrier((landed, totals[2][0][0]))
    landed.append(swap(last, "gy", n_gy, 1))
    return sum(part.astype(jnp.float32) for part in [totals[0][0][0], *landed]).astype(jnp.bfloat16)


def solution(mesh):
    n_gx, n_gy = mesh.shape["gx"], mesh.shape["gy"]
    placed = (P(("groups", "gy"), "gx"), P("gx", "gy"), P("gx", "gy"), P("gy", "gx"))
    return jax.shard_map(
        functools.partial(on_device, n_gx, n_gy),
        mesh=mesh,
        in_specs=placed,
        out_specs=P(("groups", "gy"), "gx"),
        check_vma=False,
    )
```

```python
import functools

import jax
import jax.numpy as jnp
from jax import lax
from jax.experimental import pallas as pl
from jax.experimental.pallas import tpu as pltpu
from jax.sharding import PartitionSpec as P

EPS = 1e-05
LANES = 128
GU_TILE = 256
OUT_TILE = 512
SHORT, LONG = 1000, 10**11
VMEM_LIMIT = 64 * 1024 * 1024 - 64 * 1024
ANY = pl.BlockSpec(memory_space=pl.ANY)
SMEM = pl.BlockSpec(memory_space=pltpu.SMEM)


def swap(value, axis, size, mask):
    return lax.ppermute(value, axis, [(i, i ^ mask) for i in range(size)])


def silu_product(gate, up, scale):
    gate = gate * scale
    return gate / (1.0 + jnp.exp(-gate)) * (up * scale)


def row_squares(tok):
    values = tok.astype(jnp.float32)
    return jnp.sum(values * values, axis=1, keepdims=True)


def to_carry(total):
    high = total.astype(jnp.bfloat16).astype(jnp.float32)
    shape = (total.shape[0], LANES)
    first = lax.broadcasted_iota(jnp.int32, shape, 1) < LANES // 2
    return jnp.where(first, jnp.broadcast_to(high, shape), jnp.broadcast_to(total - high, shape)).astype(jnp.bfloat16)


def carried(columns):
    values = columns.astype(jnp.float32)
    return values[:, :1] + values[:, LANES // 2 : LANES // 2 + 1]


class Group:
    def __init__(self, blocks, names, block):
        self.blocks, self.names, self.block, self.rows = blocks, names, block, block * len(names)

    def arrays(self):
        return [self.blocks[name] for name in self.names]


class GateUp:
    def __init__(self, group, place, low, width, recvs=(), carry=False, emit=False, squares=None, at=0, features=1):
        self.group, self.place, self.low, self.width, self.recvs = group, place, low, width, list(recvs)
        self.carry, self.emit, self.squares, self.at, self.features = carry, emit, squares, at, features
        rows, wide = group.rows, width if squares else 2 * width + (LANES if carry else 0)
        self.outs = [jax.ShapeDtypeStruct((rows, wide), jnp.bfloat16)]
        if emit:
            self.outs.append(jax.ShapeDtypeStruct((rows, LANES), jnp.float32))

    def fits(self, depth, columns):
        return self.width % LANES == 0 and depth % LANES == 0 and self.group.block % 16 == 0

    def arrays(self):
        return [*self.recvs, *([self.squares[0], *self.squares[1]] if self.squares else [])]

    def plain(self, table, gate_matrix, up_matrix, down_matrix):
        tok, n = jnp.concatenate(self.group.arrays(), axis=0), self.width
        both = [
            jnp.dot(
                tok, lax.dynamic_slice_in_dim(m, table[self.place] + self.low, n, 1), preferred_element_type=jnp.float32
            )
            for m in (gate_matrix, up_matrix)
        ]
        both = jnp.concatenate(both, axis=1) + sum(r[:, : 2 * n].astype(jnp.float32) for r in self.recvs)
        if self.squares:
            total = self.squares[0][:, :1] + sum(carried(r[:, self.at : self.at + LANES]) for r in self.squares[1])
            scale = lax.rsqrt(total / self.features + EPS)
            return [silu_product(both[:, :n], both[:, n:], scale).astype(jnp.bfloat16)]
        if not self.carry:
            return [both.astype(jnp.bfloat16)]
        total = row_squares(tok) + sum(carried(r[:, 2 * n : 2 * n + LANES]) for r in self.recvs)
        result = jnp.concatenate([both.astype(jnp.bfloat16), to_carry(total)], axis=1)
        return [result] + ([jnp.broadcast_to(total, (tok.shape[0], LANES))] if self.emit else [])

    def scratch(self, depth):
        rows, n, tiles, n_recv = self.group.rows, self.width, pl.cdiv(self.width, GU_TILE), len(self.recvs)
        extra = len(self.squares[1]) if self.squares else n_recv if self.carry else 0
        return [
            pltpu.VMEM((tiles, depth, 2 * GU_TILE), jnp.bfloat16),
            pltpu.VMEM((n_recv, 2, rows, n) if n_recv else (1, 2, 16, LANES), jnp.bfloat16),
            pltpu.VMEM((extra, rows, LANES) if extra else (1, 16, LANES), jnp.bfloat16),
            pltpu.VMEM((rows, LANES) if self.squares or self.emit else (8, LANES), jnp.float32),
            pltpu.VMEM((tiles, 1 if self.squares else 2, rows, GU_TILE), jnp.bfloat16),
            pltpu.VMEM((rows if self.carry else 16, LANES), jnp.bfloat16),
            pltpu.SemaphoreType.DMA((2, tiles)),
            pltpu.SemaphoreType.DMA((2 * n_recv + extra + 1,)),
            pltpu.SemaphoreType.DMA((2, tiles + 1)),
        ]

    def bind(self, refs, table, arrays, outs, scratch):
        wbuf, rbuf, ebuf, qbuf, obuf, cbuf, wsem, rsem, osem = scratch
        n, rows, n_recv = self.width, self.group.rows, len(self.recvs)
        xbuf, hidden = refs["x"][id(self.group)], self.squares is not None
        full, rest = divmod(n, GU_TILE)
        tiles = full + (rest > 0)
        start = table[self.place] + self.low

        def weights(j, m):
            columns = pl.ds(pl.multiple_of(start + j * GU_TILE, LANES), m)
            return [
                pltpu.make_async_copy(refs[name].at[:, columns], wbuf.at[j, :, pl.ds(i * m, m)], wsem.at[i, j])
                for i, name in enumerate(("gate", "up"))
            ]

        def write(j, m):
            return [
                pltpu.make_async_copy(
                    obuf.at[j, i, :, pl.ds(0, m)],
                    outs[0].at[:, pl.ds(pl.multiple_of(i * n + j * GU_TILE, LANES), m)],
                    osem.at[i, j],
                )
                for i in range(1 if hidden else 2)
            ]

        def over_tiles(step):
            if full:
                @pl.loop(0, full)
                def _(j):
                    step(j, GU_TILE)
            if rest:
                step(full, rest)

        copies = [
            pltpu.make_async_copy(a.at[:, pl.ds(h * n, n)], rbuf.at[i, h], rsem.at[2 * i + h])
            for i, a in enumerate(arrays[:n_recv])
            for h in range(2)
        ]
        extras = arrays[n_recv + 1 :] if hidden else arrays[:n_recv] if self.carry else []
        copies += [
            pltpu.make_async_copy(
                a.at[:, pl.ds(self.at if hidden else 2 * n, LANES)], ebuf.at[i], rsem.at[2 * n_recv + i]
            )
            for i, a in enumerate(extras)
        ]
        if hidden:
            copies.append(pltpu.make_async_copy(arrays[n_recv], qbuf, rsem.at[2 * n_recv + len(extras)]))
        writes = []
        if self.carry:
            writes.append(pltpu.make_async_copy(cbuf, outs[0].at[:, pl.ds(2 * n, LANES)], osem.at[0, tiles]))
        if self.emit:
            writes.append(pltpu.make_async_copy(qbuf, outs[1], osem.at[1, tiles]))

        def begin():
            def step(j, m):
                for copy in weights(j, m):
                    copy.start()

            over_tiles(step)

        def compute():
            for copy in copies:
                copy.wait()
            if hidden or self.carry:
                total = qbuf[:, :1] if hidden else row_squares(xbuf[...])
                for i in range(len(extras)):
                    total = total + carried(ebuf[i])
            if self.carry:
                cbuf[...] = to_carry(total)
                if self.emit:
                    qbuf[...] = jnp.broadcast_to(total, (rows, LANES))
                for copy in writes:
                    copy.start()
            if hidden:
                qbuf[...] = jnp.broadcast_to(lax.rsqrt(total / self.features + EPS), (rows, LANES))

            def step(j, m):
                for copy in weights(j, m):
                    copy.wait()
                both = jnp.dot(xbuf[...], wbuf[j, :, pl.ds(0, 2 * m)], preferred_element_type=jnp.float32)
                gate, up = both[:, :m], both[:, m:]
                columns = pl.ds(pl.multiple_of(j * GU_TILE, LANES), m)
                for r in range(n_recv):
                    gate = gate + rbuf[r, 0, :, columns].astype(jnp.float32)
                    up = up + rbuf[r, 1, :, columns].astype(jnp.float32)
                if hidden:
                    obuf[j, 0, :, pl.ds(0, m)] = silu_product(gate, up, qbuf[:, :1]).astype(jnp.bfloat16)
                else:
                    obuf[j, 0, :, pl.ds(0, m)] = gate.astype(jnp.bfloat16)
                    obuf[j, 1, :, pl.ds(0, m)] = up.astype(jnp.bfloat16)
                for copy in write(j, m):
                    copy.start()

            over_tiles(step)

        def drain():
            def step(j, m):
                for copy in write(j, m):
                    copy.wait()

            over_tiles(step)
            for copy in writes:
                copy.wait()

        return copies, begin, compute, drain


class Down:
    def __init__(self, parts, places, width, block, first, columns):
        self.parts, self.places, self.width, self.block = parts, places, width, block
        self.first, self.columns = first, columns
        self.group, self.rows = None, sum(part[0][0].shape[0] for part in parts)
        self.outs = [jax.ShapeDtypeStruct((block, columns), jnp.bfloat16) for _ in range(self.rows // block)]

    def fits(self, depth, columns):
        sizes = [a.shape[1] for part in self.parts for a, _, _ in part]
        return all(n % LANES == 0 for n in sizes) and self.columns % OUT_TILE == 0 and self.block % 16 == 0

    def arrays(self):
        return [a for part in self.parts for a, _, _ in part]

    def plain(self, table, gate_matrix, up_matrix, down_matrix):
        result = jnp.concatenate(
            [
                sum(
                    jnp.dot(
                        a,
                        lax.dynamic_slice_in_dim(
                            down_matrix[:, self.first : self.first + self.columns], table[place] + low, a.shape[1], 0
                        ),
                        preferred_element_type=jnp.float32,
                    )
                    for a, place, low in part
                )
                for part in self.parts
            ],
            axis=0,
        )
        return jnp.split(result.astype(jnp.bfloat16), len(self.outs))

    def scratch(self, depth):
        tiles, whole = self.columns // OUT_TILE, len(self.places) * self.width
        return [
            pltpu.VMEM((self.rows, whole), jnp.bfloat16),
            pltpu.VMEM((tiles, whole, OUT_TILE), jnp.bfloat16),
            pltpu.VMEM((tiles, self.rows, OUT_TILE), jnp.bfloat16),
            pltpu.SemaphoreType.DMA((len(self.arrays()),)),
            pltpu.SemaphoreType.DMA((len(self.places), tiles)),
            pltpu.SemaphoreType.DMA((len(self.outs), tiles)),
        ]

    def bind(self, refs, table, arrays, outs, scratch):
        hbuf, dbuf, obuf, hsem, dsem, osem = scratch
        block, width, tiles = self.block, self.width, self.columns // OUT_TILE

        def columns(j):
            return pl.ds(pl.multiple_of(j * OUT_TILE, LANES), OUT_TILE)

        def weights(p, j):
            taken = pl.ds(pl.multiple_of(self.first + j * OUT_TILE, LANES), OUT_TILE)
            return pltpu.make_async_copy(
                refs["down"].at[pl.ds(pl.multiple_of(table[self.places[p]], LANES), width), taken],
                dbuf.at[j, pl.ds(p * width, width)],
                dsem.at[p, j],
            )

        def write(i, j):
            return pltpu.make_async_copy(
                obuf.at[j, pl.ds(i * block, block)], outs[i].at[:, columns(j)], osem.at[i, j]
            )

        copies, row = [], 0
        for part in self.parts:
            rows = part[0][0].shape[0]
            for a, place, low in part:
                units = pl.ds(self.places.index(place) * width + low, a.shape[1])
                i = len(copies)
                copies.append(pltpu.make_async_copy(arrays[i], hbuf.at[pl.ds(row, rows), units], hsem.at[i]))
            row += rows

        def begin():
            @pl.loop(0, tiles)
            def _(j):
                for p in range(len(self.places)):
                    weights(p, j).start()

        def compute():
            for copy in copies:
                copy.wait()

            @pl.loop(0, tiles)
            def _(j):
                for p in range(len(self.places)):
                    weights(p, j).wait()
                result = jnp.dot(hbuf[...], dbuf[j], preferred_element_type=jnp.float32)
                obuf[j] = result.astype(jnp.bfloat16)
                for i in range(len(outs)):
                    write(i, j).start()

        def drain():
            @pl.loop(0, tiles)
            def _(j):
                for i in range(len(outs)):
                    write(i, j).wait()

        return copies, begin, compute, drain


def run(phases, table, gate_matrix, up_matrix, down_matrix, dep, work):
    depth, columns = gate_matrix.shape[0], down_matrix.shape[1]
    if not all(p.fits(depth, columns) for p in phases):
        return [p.plain(table, gate_matrix, up_matrix, down_matrix) for p in phases]
    operands = [gate_matrix, up_matrix, down_matrix]

    def index(array):
        for i, known in enumerate(operands):
            if known is array:
                return i
        operands.append(array)
        return len(operands) - 1

    groups = []
    for p in phases:
        if p.group is not None and all(p.group is not g for g in groups):
            groups.append(p.group)
    tok_places = [[index(t) for t in g.arrays()] for g in groups]
    where = [[index(a) for a in p.arrays()] for p in phases]
    index(dep)
    outs = [o for p in phases for o in p.outs]
    scratch = [p.scratch(depth) for p in phases]

    def kernel(table_ref, *args):
        args = list(args)
        arrays = [args.pop(0) for _ in operands]
        out_refs = [args.pop(0) for _ in outs]
        refs = {"gate": arrays[0], "up": arrays[1], "down": arrays[2], "x": {}}
        ready = {}
        for g, places in zip(groups, tok_places):
            xbuf, xsem = args.pop(0), args.pop(0)
            refs["x"][id(g)] = xbuf
            ready[id(g)] = [
                pltpu.make_async_copy(arrays[place], xbuf.at[pl.ds(j * g.block, g.block)], xsem.at[j])
                for j, place in enumerate(places)
            ]
        bound = []
        for p, places, buffers in zip(phases, where, scratch):
            mine = [out_refs.pop(0) for _ in p.outs]
            held = [args.pop(0) for _ in buffers]
            bound.append(p.bind(refs, table_ref, [arrays[i] for i in places], mine, held))
        for copies in ready.values():
            for copy in copies:
                copy.start()
        for copies, begin, _, _ in bound:
            for copy in copies:
                copy.start()
            begin()
        for p, (_, _, compute, _) in zip(phases, bound):
            for copy in ready.pop(id(p.group), []):
                copy.wait()
            compute()
        for _, _, _, drain in bound:
            drain()

    results = list(
        pl.pallas_call(
            kernel,
            out_shape=outs,
            in_specs=[SMEM] + [ANY] * len(operands),
            out_specs=[ANY] * len(outs),
            scratch_shapes=[
                *[
                    buffer
                    for g in groups
                    for buffer in (pltpu.VMEM((g.rows, depth), jnp.bfloat16), pltpu.SemaphoreType.DMA((len(g.names),)))
                ],
                *[buffer for buffers in scratch for buffer in buffers],
            ],
            compiler_params=pltpu.CompilerParams(vmem_limit_bytes=VMEM_LIMIT),
            cost_estimate=pl.CostEstimate(flops=work, bytes_accessed=1000, transcendentals=0),
            name="step_" + "".join("g" if p.group is not None else "d" for p in phases),
        )(table, *operands)
    )
    return [[results.pop(0) for _ in p.outs] for p in phases]


STEPS = (
    ("s0",),
    ("s1",),
    ("x0",),
    ("t", "x1"),
    ("p0", "s2"),
    ("p1", "s3", "long"),
    ("x2",),
    ("h0",),
    ("h1",),
    ("x3",),
    ("b", "s4"),
    ("h2",),
    ("h3",),
    ("r0", "r1", "x4"),
    ("f0", "f1", "r2", "r3", "d1"),
    ("h4",),
    ("z", "r4", "d02"),
)


def cut(width, part, parts):
    unit = LANES if width % LANES == 0 else 1
    return width // unit * part // parts * unit


def on_device(n_gx, n_gy, tokens, gate_matrix, up_matrix, down_matrix):
    features = tokens.shape[1] * n_gx
    width = gate_matrix.shape[1] // n_gx
    block, columns = tokens.shape[0], down_matrix.shape[1]
    far = [2 * k for k in range(1, n_gx // 2)]

    def core(value):
        return swap(value, "gx", n_gx, 1)

    table = jnp.concatenate(
        [(lax.axis_index("gx") ^ jnp.arange(n_gx, dtype=jnp.int32)) * width, jnp.zeros((1,), jnp.int32)]
    )
    blocks = {0: tokens}
    sets = [[0], list(range(2, n_gy)), [1]]
    groups = [Group(blocks, js, block) for js in sets]
    squares = {}
    half = cut(width, 8, 13)
    early = cut(width, 7, 13)
    jobs = [(0, 0, early), (0, early, width - early), (1, 0, half), (1, half, width - half), (2, 0, width)]
    firsts = [min(i for i, job in enumerate(jobs) if job[0] == g) for g in range(len(groups))]
    state = [dict() for _ in jobs]
    totals = {}
    chain = tokens

    def phases_of(kind, job):
        g, low, n = jobs[job]
        group, st, first = groups[g], state[job], low == 0
        if kind == "s":
            return [GateUp(group, k ^ 1, low, n, carry=first and k > 0) for k in [*far, 0]]
        if kind == "x":
            return [
                GateUp(group, k, low, n, [st["lent"][i]], carry=first, emit=first and i == 0)
                for i, k in enumerate(far)
            ]
        if kind == "h":
            recvs = [st["lent"][-1], *st["far"]]
            return [GateUp(group, 0, low, n, recvs, squares=squares[g], at=2 * jobs[firsts[g]][2], features=features)]

    def down(gs, half):
        parts = [
            [(h, q, jobs[i][1]) for i, st in enumerate(state) if jobs[i][0] == g for h, q in st["pieces"]] for g in gs
        ]
        low, high = {"l": (0, columns // 2), "r": (columns // 2, columns)}.get(half, (0, columns))
        return Down(parts, list(range(n_gx)), width, block, low, high - low)

    def deliver(kind, job, outs):
        g, st = jobs[job][0], state[job]
        if kind == "s":
            st["lent"] = [core(o[0]) for o in outs]
        elif kind == "x":
            st["far"] = [swap(o[0], "gx", n_gx, k) for o, k in zip(outs, far)]
            if job == firsts[g]:
                squares[g] = (outs[0][1], st["far"])
        elif kind == "h":
            st["pieces"] = [(outs[0][0], 0), (core(outs[0][0]), 1)]
            st["crossed"] = [swap(outs[0][0], "gx", n_gx, k) for k in far]

    def tied(values):
        nonlocal chain
        values, chain = lax.optimization_barrier((values, chain))
        return values

    def forward(job):
        crossed = tied(state[job]["crossed"])
        state[job]["pieces"] += [(h, k) for h, k in zip(crossed, far)]
        state[job]["pieces"] += [(core(h), k ^ 1) for h, k in zip(crossed, far)]

    def reduce_over_gy():
        parts = dict(zip(sets[1], totals[1][0]))
        mask = 1
        while mask < n_gy:
            for j in [j for j in parts if j & mask]:
                arrived = swap(parts.pop(j), "gy", n_gy, mask)
                if j == mask:
                    landed.append(arrived)
                    continue
                arrived = tied(arrived).astype(jnp.float32)
                parts[j ^ mask] = (parts[j ^ mask].astype(jnp.float32) + arrived).astype(jnp.bfloat16)
            mask *= 2

    def gather_over_gy(mask):
        got = [j for j in blocks if j]
        blocks.update(zip(got, tied([blocks[j] for j in got])))
        for j in list(blocks) if mask > 1 else got:
            blocks[j ^ mask] = swap(blocks[j], "gy", n_gy, mask)

    landed = []
    mask = n_gy // 2
    gather_over_gy(mask)
    for names in STEPS:
        items, work = [], LONG if "long" in names else SHORT
        for name in names:
            if name == "long":
                continue
            kind, job = name[0], int(name[1:].rstrip("lr") or 0)
            if kind == "r":
                forward(job)
                continue
            while kind == "t" and mask > 1:
                mask //= 2
                gather_over_gy(mask)
            if kind == "p":
                state[job]["far"] = tied(state[job]["far"])
                if job == firsts[jobs[job][0]]:
                    squares[jobs[job][0]] = (squares[jobs[job][0]][0], state[job]["far"])
            if kind == "f":
                held, places = zip(*state[job]["pieces"])
                state[job]["pieces"] = list(zip(tied(list(held)), places))
            if kind == "b":
                blocks[1] = tied(swap(tokens, "gy", n_gy, 1))
            if kind == "z":
                reduce_over_gy()
            if kind in "tpfbz":
                continue
            if kind == "d":
                gs = [int(g) for g in name[1:] if g.isdigit()]
                items.append((kind, gs, [down(gs, name[-1])]))
            else:
                items.append((kind, job, phases_of(kind, job)))
        results = run([p for _, _, ps in items for p in ps], table, gate_matrix, up_matrix, down_matrix, chain, work)
        chain = results[0][0]
        for kind, job, ps in items:
            outs = [results.pop(0) for _ in ps]
            if kind != "d":
                deliver(kind, job, outs)
                continue
            for g in job:
                totals.setdefault(g, []).append([outs[0].pop(0) for _ in sets[g]])

    landed, last = lax.optimization_barrier((landed, totals[2][0][0]))
    landed.append(swap(last, "gy", n_gy, 1))
    return sum(part.astype(jnp.float32) for part in [totals[0][0][0], *landed]).astype(jnp.bfloat16)


def solution(mesh):
    n_gx, n_gy = mesh.shape["gx"], mesh.shape["gy"]
    placed = (P(("groups", "gy"), "gx"), P("gx", "gy"), P("gx", "gy"), P("gy", "gx"))
    return jax.shard_map(
        functools.partial(on_device, n_gx, n_gy),
        mesh=mesh,
        in_specs=placed,
        out_specs=P(("groups", "gy"), "gx"),
        check_vma=False,
    )
```

```python
import functools

import jax
import jax.numpy as jnp
from jax import lax
from jax.experimental import pallas as pl
from jax.experimental.pallas import tpu as pltpu
from jax.sharding import PartitionSpec as P

EPS = 1e-05
LANES = 128
GU_TILE = 256
OUT_TILE = 512
SHORT, LONG = 1000, 10**11
VMEM_LIMIT = 64 * 1024 * 1024 - 64 * 1024
ANY = pl.BlockSpec(memory_space=pl.ANY)
SMEM = pl.BlockSpec(memory_space=pltpu.SMEM)


def swap(value, axis, size, mask):
    return lax.ppermute(value, axis, [(i, i ^ mask) for i in range(size)])


def silu_product(gate, up, scale):
    gate = gate * scale
    return gate / (1.0 + jnp.exp(-gate)) * (up * scale)


def row_squares(tok):
    values = tok.astype(jnp.float32)
    return jnp.sum(values * values, axis=1, keepdims=True)


def to_carry(total):
    high = total.astype(jnp.bfloat16).astype(jnp.float32)
    shape = (total.shape[0], LANES)
    first = lax.broadcasted_iota(jnp.int32, shape, 1) < LANES // 2
    return jnp.where(first, jnp.broadcast_to(high, shape), jnp.broadcast_to(total - high, shape)).astype(jnp.bfloat16)


def carried(columns):
    values = columns.astype(jnp.float32)
    return values[:, :1] + values[:, LANES // 2 : LANES // 2 + 1]


class Group:
    def __init__(self, blocks, names, block):
        self.blocks, self.names, self.block, self.rows = blocks, names, block, block * len(names)

    def arrays(self):
        return [self.blocks[name] for name in self.names]


class GateUp:
    def __init__(self, group, place, low, width, recvs=(), carry=False, emit=False, squares=None, at=0, features=1):
        self.group, self.place, self.low, self.width, self.recvs = group, place, low, width, list(recvs)
        self.carry, self.emit, self.squares, self.at, self.features = carry, emit, squares, at, features
        rows, wide = group.rows, width if squares else 2 * width + (LANES if carry else 0)
        self.outs = [jax.ShapeDtypeStruct((rows, wide), jnp.bfloat16)]
        if emit:
            self.outs.append(jax.ShapeDtypeStruct((rows, LANES), jnp.float32))

    def fits(self, depth, columns):
        return self.width % LANES == 0 and depth % LANES == 0 and self.group.block % 16 == 0

    def arrays(self):
        return [*self.recvs, *([self.squares[0], *self.squares[1]] if self.squares else [])]

    def plain(self, table, gate_matrix, up_matrix, down_matrix):
        tok, n = jnp.concatenate(self.group.arrays(), axis=0), self.width
        both = [
            jnp.dot(
                tok, lax.dynamic_slice_in_dim(m, table[self.place] + self.low, n, 1), preferred_element_type=jnp.float32
            )
            for m in (gate_matrix, up_matrix)
        ]
        both = jnp.concatenate(both, axis=1) + sum(r[:, : 2 * n].astype(jnp.float32) for r in self.recvs)
        if self.squares:
            total = self.squares[0][:, :1] + sum(carried(r[:, self.at : self.at + LANES]) for r in self.squares[1])
            scale = lax.rsqrt(total / self.features + EPS)
            return [silu_product(both[:, :n], both[:, n:], scale).astype(jnp.bfloat16)]
        if not self.carry:
            return [both.astype(jnp.bfloat16)]
        total = row_squares(tok) + sum(carried(r[:, 2 * n : 2 * n + LANES]) for r in self.recvs)
        result = jnp.concatenate([both.astype(jnp.bfloat16), to_carry(total)], axis=1)
        return [result] + ([jnp.broadcast_to(total, (tok.shape[0], LANES))] if self.emit else [])

    def scratch(self, depth):
        rows, n, tiles, n_recv = self.group.rows, self.width, pl.cdiv(self.width, GU_TILE), len(self.recvs)
        extra = len(self.squares[1]) if self.squares else n_recv if self.carry else 0
        return [
            pltpu.VMEM((tiles, depth, 2 * GU_TILE), jnp.bfloat16),
            pltpu.VMEM((n_recv, 2, rows, n) if n_recv else (1, 2, 16, LANES), jnp.bfloat16),
            pltpu.VMEM((extra, rows, LANES) if extra else (1, 16, LANES), jnp.bfloat16),
            pltpu.VMEM((rows, LANES) if self.squares or self.emit else (8, LANES), jnp.float32),
            pltpu.VMEM((tiles, 1 if self.squares else 2, rows, GU_TILE), jnp.bfloat16),
            pltpu.VMEM((rows if self.carry else 16, LANES), jnp.bfloat16),
            pltpu.SemaphoreType.DMA((2, tiles)),
            pltpu.SemaphoreType.DMA((2 * n_recv + extra + 1,)),
            pltpu.SemaphoreType.DMA((2, tiles + 1)),
        ]

    def bind(self, refs, table, arrays, outs, scratch):
        wbuf, rbuf, ebuf, qbuf, obuf, cbuf, wsem, rsem, osem = scratch
        n, rows, n_recv = self.width, self.group.rows, len(self.recvs)
        xbuf, hidden = refs["x"][id(self.group)], self.squares is not None
        full, rest = divmod(n, GU_TILE)
        tiles = full + (rest > 0)
        start = table[self.place] + self.low

        def weights(j, m):
            columns = pl.ds(pl.multiple_of(start + j * GU_TILE, LANES), m)
            return [
                pltpu.make_async_copy(refs[name].at[:, columns], wbuf.at[j, :, pl.ds(i * m, m)], wsem.at[i, j])
                for i, name in enumerate(("gate", "up"))
            ]

        def write(j, m):
            return [
                pltpu.make_async_copy(
                    obuf.at[j, i, :, pl.ds(0, m)],
                    outs[0].at[:, pl.ds(pl.multiple_of(i * n + j * GU_TILE, LANES), m)],
                    osem.at[i, j],
                )
                for i in range(1 if hidden else 2)
            ]

        def over_tiles(step):
            if full:
                @pl.loop(0, full)
                def _(j):
                    step(j, GU_TILE)
            if rest:
                step(full, rest)

        copies = [
            pltpu.make_async_copy(a.at[:, pl.ds(h * n, n)], rbuf.at[i, h], rsem.at[2 * i + h])
            for i, a in enumerate(arrays[:n_recv])
            for h in range(2)
        ]
        extras = arrays[n_recv + 1 :] if hidden else arrays[:n_recv] if self.carry else []
        copies += [
            pltpu.make_async_copy(
                a.at[:, pl.ds(self.at if hidden else 2 * n, LANES)], ebuf.at[i], rsem.at[2 * n_recv + i]
            )
            for i, a in enumerate(extras)
        ]
        if hidden:
            copies.append(pltpu.make_async_copy(arrays[n_recv], qbuf, rsem.at[2 * n_recv + len(extras)]))
        writes = []
        if self.carry:
            writes.append(pltpu.make_async_copy(cbuf, outs[0].at[:, pl.ds(2 * n, LANES)], osem.at[0, tiles]))
        if self.emit:
            writes.append(pltpu.make_async_copy(qbuf, outs[1], osem.at[1, tiles]))

        def begin():
            def step(j, m):
                for copy in weights(j, m):
                    copy.start()

            over_tiles(step)

        def compute():
            for copy in copies:
                copy.wait()
            if hidden or self.carry:
                total = qbuf[:, :1] if hidden else row_squares(xbuf[...])
                for i in range(len(extras)):
                    total = total + carried(ebuf[i])
            if self.carry:
                cbuf[...] = to_carry(total)
                if self.emit:
                    qbuf[...] = jnp.broadcast_to(total, (rows, LANES))
                for copy in writes:
                    copy.start()
            if hidden:
                qbuf[...] = jnp.broadcast_to(lax.rsqrt(total / self.features + EPS), (rows, LANES))

            def step(j, m):
                for copy in weights(j, m):
                    copy.wait()
                both = jnp.dot(xbuf[...], wbuf[j, :, pl.ds(0, 2 * m)], preferred_element_type=jnp.float32)
                gate, up = both[:, :m], both[:, m:]
                columns = pl.ds(pl.multiple_of(j * GU_TILE, LANES), m)
                for r in range(n_recv):
                    gate = gate + rbuf[r, 0, :, columns].astype(jnp.float32)
                    up = up + rbuf[r, 1, :, columns].astype(jnp.float32)
                if hidden:
                    obuf[j, 0, :, pl.ds(0, m)] = silu_product(gate, up, qbuf[:, :1]).astype(jnp.bfloat16)
                else:
                    obuf[j, 0, :, pl.ds(0, m)] = gate.astype(jnp.bfloat16)
                    obuf[j, 1, :, pl.ds(0, m)] = up.astype(jnp.bfloat16)
                for copy in write(j, m):
                    copy.start()

            over_tiles(step)

        def drain():
            def step(j, m):
                for copy in write(j, m):
                    copy.wait()

            over_tiles(step)
            for copy in writes:
                copy.wait()

        return copies, begin, compute, drain


class Down:
    def __init__(self, parts, places, width, block, first, columns):
        self.parts, self.places, self.width, self.block = parts, places, width, block
        self.first, self.columns = first, columns
        self.group, self.rows = None, sum(part[0][0].shape[0] for part in parts)
        self.outs = [jax.ShapeDtypeStruct((block, columns), jnp.bfloat16) for _ in range(self.rows // block)]

    def fits(self, depth, columns):
        sizes = [a.shape[1] for part in self.parts for a, _, _ in part]
        return all(n % LANES == 0 for n in sizes) and self.columns % OUT_TILE == 0 and self.block % 16 == 0

    def arrays(self):
        return [a for part in self.parts for a, _, _ in part]

    def plain(self, table, gate_matrix, up_matrix, down_matrix):
        result = jnp.concatenate(
            [
                sum(
                    jnp.dot(
                        a,
                        lax.dynamic_slice_in_dim(
                            down_matrix[:, self.first : self.first + self.columns], table[place] + low, a.shape[1], 0
                        ),
                        preferred_element_type=jnp.float32,
                    )
                    for a, place, low in part
                )
                for part in self.parts
            ],
            axis=0,
        )
        return jnp.split(result.astype(jnp.bfloat16), len(self.outs))

    def scratch(self, depth):
        tiles, whole = self.columns // OUT_TILE, len(self.places) * self.width
        return [
            pltpu.VMEM((self.rows, whole), jnp.bfloat16),
            pltpu.VMEM((tiles, whole, OUT_TILE), jnp.bfloat16),
            pltpu.VMEM((tiles, self.rows, OUT_TILE), jnp.bfloat16),
            pltpu.SemaphoreType.DMA((len(self.arrays()),)),
            pltpu.SemaphoreType.DMA((len(self.places), tiles)),
            pltpu.SemaphoreType.DMA((len(self.outs), tiles)),
        ]

    def bind(self, refs, table, arrays, outs, scratch):
        hbuf, dbuf, obuf, hsem, dsem, osem = scratch
        block, width, tiles = self.block, self.width, self.columns // OUT_TILE

        def columns(j):
            return pl.ds(pl.multiple_of(j * OUT_TILE, LANES), OUT_TILE)

        def weights(p, j):
            taken = pl.ds(pl.multiple_of(self.first + j * OUT_TILE, LANES), OUT_TILE)
            return pltpu.make_async_copy(
                refs["down"].at[pl.ds(pl.multiple_of(table[self.places[p]], LANES), width), taken],
                dbuf.at[j, pl.ds(p * width, width)],
                dsem.at[p, j],
            )

        def write(i, j):
            return pltpu.make_async_copy(
                obuf.at[j, pl.ds(i * block, block)], outs[i].at[:, columns(j)], osem.at[i, j]
            )

        copies, row = [], 0
        for part in self.parts:
            rows = part[0][0].shape[0]
            for a, place, low in part:
                units = pl.ds(self.places.index(place) * width + low, a.shape[1])
                i = len(copies)
                copies.append(pltpu.make_async_copy(arrays[i], hbuf.at[pl.ds(row, rows), units], hsem.at[i]))
            row += rows

        def begin():
            @pl.loop(0, tiles)
            def _(j):
                for p in range(len(self.places)):
                    weights(p, j).start()

        def compute():
            for copy in copies:
                copy.wait()

            @pl.loop(0, tiles)
            def _(j):
                for p in range(len(self.places)):
                    weights(p, j).wait()
                result = jnp.dot(hbuf[...], dbuf[j], preferred_element_type=jnp.float32)
                obuf[j] = result.astype(jnp.bfloat16)
                for i in range(len(outs)):
                    write(i, j).start()

        def drain():
            @pl.loop(0, tiles)
            def _(j):
                for i in range(len(outs)):
                    write(i, j).wait()

        return copies, begin, compute, drain


def run(phases, table, gate_matrix, up_matrix, down_matrix, dep, work):
    depth, columns = gate_matrix.shape[0], down_matrix.shape[1]
    if not all(p.fits(depth, columns) for p in phases):
        return [p.plain(table, gate_matrix, up_matrix, down_matrix) for p in phases]
    operands = [gate_matrix, up_matrix, down_matrix]

    def index(array):
        for i, known in enumerate(operands):
            if known is array:
                return i
        operands.append(array)
        return len(operands) - 1

    groups = []
    for p in phases:
        if p.group is not None and all(p.group is not g for g in groups):
            groups.append(p.group)
    tok_places = [[index(t) for t in g.arrays()] for g in groups]
    where = [[index(a) for a in p.arrays()] for p in phases]
    index(dep)
    outs = [o for p in phases for o in p.outs]
    scratch = [p.scratch(depth) for p in phases]

    def kernel(table_ref, *args):
        args = list(args)
        arrays = [args.pop(0) for _ in operands]
        out_refs = [args.pop(0) for _ in outs]
        refs = {"gate": arrays[0], "up": arrays[1], "down": arrays[2], "x": {}}
        ready = {}
        for g, places in zip(groups, tok_places):
            xbuf, xsem = args.pop(0), args.pop(0)
            refs["x"][id(g)] = xbuf
            ready[id(g)] = [
                pltpu.make_async_copy(arrays[place], xbuf.at[pl.ds(j * g.block, g.block)], xsem.at[j])
                for j, place in enumerate(places)
            ]
        bound = []
        for p, places, buffers in zip(phases, where, scratch):
            mine = [out_refs.pop(0) for _ in p.outs]
            held = [args.pop(0) for _ in buffers]
            bound.append(p.bind(refs, table_ref, [arrays[i] for i in places], mine, held))
        for copies in ready.values():
            for copy in copies:
                copy.start()
        for copies, begin, _, _ in bound:
            for copy in copies:
                copy.start()
            begin()
        for p, (_, _, compute, _) in zip(phases, bound):
            for copy in ready.pop(id(p.group), []):
                copy.wait()
            compute()
        for _, _, _, drain in bound:
            drain()

    results = list(
        pl.pallas_call(
            kernel,
            out_shape=outs,
            in_specs=[SMEM] + [ANY] * len(operands),
            out_specs=[ANY] * len(outs),
            scratch_shapes=[
                *[
                    buffer
                    for g in groups
                    for buffer in (pltpu.VMEM((g.rows, depth), jnp.bfloat16), pltpu.SemaphoreType.DMA((len(g.names),)))
                ],
                *[buffer for buffers in scratch for buffer in buffers],
            ],
            compiler_params=pltpu.CompilerParams(vmem_limit_bytes=VMEM_LIMIT),
            cost_estimate=pl.CostEstimate(flops=work, bytes_accessed=1000, transcendentals=0),
            name="step_" + "".join("g" if p.group is not None else "d" for p in phases),
        )(table, *operands)
    )
    return [[results.pop(0) for _ in p.outs] for p in phases]


STEPS = (
    ("s0",),
    ("s1",),
    ("x0",),
    ("t", "x1"),
    ("p0", "s2"),
    ("p1", "s3", "long"),
    ("x2",),
    ("h0",),
    ("h1",),
    ("x3",),
    ("b", "s4"),
    ("h2", "long"),
    ("h3",),
    ("r0", "r1", "x4"),
    ("f0", "f1", "r2", "r3", "d1"),
    ("h4",),
    ("z", "r4", "d02"),
)


def cut(width, part, parts):
    unit = LANES if width % LANES == 0 else 1
    return width // unit * part // parts * unit


def on_device(n_gx, n_gy, tokens, gate_matrix, up_matrix, down_matrix):
    features = tokens.shape[1] * n_gx
    width = gate_matrix.shape[1] // n_gx
    block, columns = tokens.shape[0], down_matrix.shape[1]
    far = [2 * k for k in range(1, n_gx // 2)]

    def core(value):
        return swap(value, "gx", n_gx, 1)

    table = jnp.concatenate(
        [(lax.axis_index("gx") ^ jnp.arange(n_gx, dtype=jnp.int32)) * width, jnp.zeros((1,), jnp.int32)]
    )
    blocks = {0: tokens}
    sets = [[0], list(range(2, n_gy)), [1]]
    groups = [Group(blocks, js, block) for js in sets]
    squares = {}
    half = cut(width, 7, 13)
    early = cut(width, 7, 13)
    jobs = [(0, 0, early), (0, early, width - early), (1, 0, half), (1, half, width - half), (2, 0, width)]
    firsts = [min(i for i, job in enumerate(jobs) if job[0] == g) for g in range(len(groups))]
    state = [dict() for _ in jobs]
    totals = {}
    chain = tokens

    def phases_of(kind, job):
        g, low, n = jobs[job]
        group, st, first = groups[g], state[job], low == 0
        if kind == "s":
            return [GateUp(group, k ^ 1, low, n, carry=first and k > 0) for k in [*far, 0]]
        if kind == "x":
            return [
                GateUp(group, k, low, n, [st["lent"][i]], carry=first, emit=first and i == 0)
                for i, k in enumerate(far)
            ]
        if kind == "h":
            recvs = [st["lent"][-1], *st["far"]]
            return [GateUp(group, 0, low, n, recvs, squares=squares[g], at=2 * jobs[firsts[g]][2], features=features)]

    def down(gs, half):
        parts = [
            [(h, q, jobs[i][1]) for i, st in enumerate(state) if jobs[i][0] == g for h, q in st["pieces"]] for g in gs
        ]
        low, high = {"l": (0, columns // 2), "r": (columns // 2, columns)}.get(half, (0, columns))
        return Down(parts, list(range(n_gx)), width, block, low, high - low)

    def deliver(kind, job, outs):
        g, st = jobs[job][0], state[job]
        if kind == "s":
            st["lent"] = [core(o[0]) for o in outs]
        elif kind == "x":
            st["far"] = [swap(o[0], "gx", n_gx, k) for o, k in zip(outs, far)]
            if job == firsts[g]:
                squares[g] = (outs[0][1], st["far"])
        elif kind == "h":
            st["pieces"] = [(outs[0][0], 0), (core(outs[0][0]), 1)]
            st["crossed"] = [swap(outs[0][0], "gx", n_gx, k) for k in far]

    def tied(values):
        nonlocal chain
        values, chain = lax.optimization_barrier((values, chain))
        return values

    def forward(job):
        crossed = tied(state[job]["crossed"])
        state[job]["pieces"] += [(h, k) for h, k in zip(crossed, far)]
        state[job]["pieces"] += [(core(h), k ^ 1) for h, k in zip(crossed, far)]

    def reduce_over_gy():
        parts = dict(zip(sets[1], totals[1][0]))
        mask = 1
        while mask < n_gy:
            for j in [j for j in parts if j & mask]:
                arrived = swap(parts.pop(j), "gy", n_gy, mask)
                if j == mask:
                    landed.append(arrived)
                    continue
                arrived = tied(arrived).astype(jnp.float32)
                parts[j ^ mask] = (parts[j ^ mask].astype(jnp.float32) + arrived).astype(jnp.bfloat16)
            mask *= 2

    def gather_over_gy(mask):
        got = [j for j in blocks if j]
        blocks.update(zip(got, tied([blocks[j] for j in got])))
        for j in list(blocks) if mask > 1 else got:
            blocks[j ^ mask] = swap(blocks[j], "gy", n_gy, mask)

    landed = []
    mask = n_gy // 2
    gather_over_gy(mask)
    for names in STEPS:
        items, work = [], LONG if "long" in names else SHORT
        for name in names:
            if name == "long":
                continue
            kind, job = name[0], int(name[1:].rstrip("lr") or 0)
            if kind == "r":
                forward(job)
                continue
            while kind == "t" and mask > 1:
                mask //= 2
                gather_over_gy(mask)
            if kind == "p":
                state[job]["far"] = tied(state[job]["far"])
                if job == firsts[jobs[job][0]]:
                    squares[jobs[job][0]] = (squares[jobs[job][0]][0], state[job]["far"])
            if kind == "f":
                held, places = zip(*state[job]["pieces"])
                state[job]["pieces"] = list(zip(tied(list(held)), places))
            if kind == "b":
                blocks[1] = tied(swap(tokens, "gy", n_gy, 1))
            if kind == "z":
                reduce_over_gy()
            if kind in "tpfbz":
                continue
            if kind == "d":
                gs = [int(g) for g in name[1:] if g.isdigit()]
                items.append((kind, gs, [down(gs, name[-1])]))
            else:
                items.append((kind, job, phases_of(kind, job)))
        results = run([p for _, _, ps in items for p in ps], table, gate_matrix, up_matrix, down_matrix, chain, work)
        chain = results[0][0]
        for kind, job, ps in items:
            outs = [results.pop(0) for _ in ps]
            if kind != "d":
                deliver(kind, job, outs)
                continue
            for g in job:
                totals.setdefault(g, []).append([outs[0].pop(0) for _ in sets[g]])

    landed, last = lax.optimization_barrier((landed, totals[2][0][0]))
    landed.append(swap(last, "gy", n_gy, 1))
    return sum(part.astype(jnp.float32) for part in [totals[0][0][0], *landed]).astype(jnp.bfloat16)


def solution(mesh):
    n_gx, n_gy = mesh.shape["gx"], mesh.shape["gy"]
    placed = (P(("groups", "gy"), "gx"), P("gx", "gy"), P("gx", "gy"), P("gy", "gx"))
    return jax.shard_map(
        functools.partial(on_device, n_gx, n_gy),
        mesh=mesh,
        in_specs=placed,
        out_specs=P(("groups", "gy"), "gx"),
        check_vma=False,
    )
```

```python
import functools

import jax
import jax.numpy as jnp
from jax import lax
from jax.experimental import pallas as pl
from jax.experimental.pallas import tpu as pltpu
from jax.sharding import PartitionSpec as P

EPS = 1e-05
LANES = 128
GU_TILE = 256
OUT_TILE = 512
CUTS = 4
SHORT, LONG = 1000, 10**11
VMEM_LIMIT = 64 * 1024 * 1024 - 64 * 1024
ANY = pl.BlockSpec(memory_space=pl.ANY)
SMEM = pl.BlockSpec(memory_space=pltpu.SMEM)


def swap(value, axis, size, mask):
    return lax.ppermute(value, axis, [(i, i ^ mask) for i in range(size)])


def silu_product(gate, up, scale):
    gate = gate * scale
    return gate / (1.0 + jnp.exp(-gate)) * (up * scale)


def row_squares(tok):
    values = tok.astype(jnp.float32)
    return jnp.sum(values * values, axis=1, keepdims=True)


def to_carry(total):
    high = total.astype(jnp.bfloat16).astype(jnp.float32)
    shape = (total.shape[0], LANES)
    first = lax.broadcasted_iota(jnp.int32, shape, 1) < LANES // 2
    return jnp.where(first, jnp.broadcast_to(high, shape), jnp.broadcast_to(total - high, shape)).astype(jnp.bfloat16)


def carried(columns):
    values = columns.astype(jnp.float32)
    return values[:, :1] + values[:, LANES // 2 : LANES // 2 + 1]


class Group:
    def __init__(self, blocks, names, block):
        self.blocks, self.names, self.block, self.rows = blocks, names, block, block * len(names)

    def arrays(self):
        return [self.blocks[name] for name in self.names]


class GateUp:
    def __init__(self, group, place, low, width, recvs=(), carry=False, emit=False, squares=None, at=0, features=1):
        self.group, self.place, self.low, self.width, self.recvs = group, place, low, width, list(recvs)
        self.carry, self.emit, self.squares, self.at, self.features = carry, emit, squares, at, features
        rows, wide = group.rows, width if squares else 2 * width + (LANES if carry else 0)
        self.outs = [jax.ShapeDtypeStruct((rows, wide), jnp.bfloat16)]
        if emit:
            self.outs.append(jax.ShapeDtypeStruct((rows, LANES), jnp.float32))

    def fits(self, depth, columns):
        return self.width % LANES == 0 and depth % (16 * CUTS) == 0 and self.group.block % 16 == 0

    def arrays(self):
        return [*self.recvs, *([self.squares[0], *self.squares[1]] if self.squares else [])]

    def plain(self, table, gate_matrix, up_matrix, down_matrix):
        tok, n = jnp.concatenate(self.group.arrays(), axis=0), self.width
        both = [
            jnp.dot(
                tok, lax.dynamic_slice_in_dim(m, table[self.place] + self.low, n, 1), preferred_element_type=jnp.float32
            )
            for m in (gate_matrix, up_matrix)
        ]
        both = jnp.concatenate(both, axis=1) + sum(r[:, : 2 * n].astype(jnp.float32) for r in self.recvs)
        if self.squares:
            total = self.squares[0][:, :1] + sum(carried(r[:, self.at : self.at + LANES]) for r in self.squares[1])
            scale = lax.rsqrt(total / self.features + EPS)
            return [silu_product(both[:, :n], both[:, n:], scale).astype(jnp.bfloat16)]
        if not self.carry:
            return [both.astype(jnp.bfloat16)]
        total = row_squares(tok) + sum(carried(r[:, 2 * n : 2 * n + LANES]) for r in self.recvs)
        result = jnp.concatenate([both.astype(jnp.bfloat16), to_carry(total)], axis=1)
        return [result] + ([jnp.broadcast_to(total, (tok.shape[0], LANES))] if self.emit else [])

    def scratch(self, depth):
        rows, n, tiles, n_recv = self.group.rows, self.width, pl.cdiv(self.width, GU_TILE), len(self.recvs)
        extra = len(self.squares[1]) if self.squares else n_recv if self.carry else 0
        return [
            pltpu.VMEM((tiles, depth, 2 * GU_TILE), jnp.bfloat16),
            pltpu.VMEM((n_recv, 2, rows, n) if n_recv else (1, 2, 16, LANES), jnp.bfloat16),
            pltpu.VMEM((extra, rows, LANES) if extra else (1, 16, LANES), jnp.bfloat16),
            pltpu.VMEM((rows, LANES) if self.squares or self.emit else (8, LANES), jnp.float32),
            pltpu.VMEM((tiles, 1 if self.squares else 2, rows, GU_TILE), jnp.bfloat16),
            pltpu.VMEM((rows if self.carry else 16, LANES), jnp.bfloat16),
            pltpu.SemaphoreType.DMA((2, tiles)),
            pltpu.SemaphoreType.DMA((2 * n_recv + extra + 1,)),
            pltpu.SemaphoreType.DMA((2, tiles + 1)),
        ]

    def bind(self, refs, table, arrays, outs, scratch):
        wbuf, rbuf, ebuf, qbuf, obuf, cbuf, wsem, rsem, osem = scratch
        n, rows, n_recv = self.width, self.group.rows, len(self.recvs)
        xbuf, hidden = refs["x"][id(self.group)], self.squares is not None
        full, rest = divmod(n, GU_TILE)
        tiles = full + (rest > 0)
        start = table[self.place] + self.low

        def weights(j, m, cuts=1):
            columns = pl.ds(pl.multiple_of(start + j * GU_TILE, LANES), m)
            rows_each = wbuf.shape[1] // cuts
            return [
                pltpu.make_async_copy(
                    refs[name].at[pl.ds(k * rows_each, rows_each), columns],
                    wbuf.at[j, pl.ds(k * rows_each, rows_each), pl.ds(i * m, m)],
                    wsem.at[i, j],
                )
                for k in range(cuts)
                for i, name in enumerate(("gate", "up"))
            ]

        def write(j, m):
            return [
                pltpu.make_async_copy(
                    obuf.at[j, i, :, pl.ds(0, m)],
                    outs[0].at[:, pl.ds(pl.multiple_of(i * n + j * GU_TILE, LANES), m)],
                    osem.at[i, j],
                )
                for i in range(1 if hidden else 2)
            ]

        def over_tiles(step):
            if full:
                @pl.loop(0, full)
                def _(j):
                    step(j, GU_TILE)
            if rest:
                step(full, rest)

        copies = [
            pltpu.make_async_copy(a.at[:, pl.ds(h * n, n)], rbuf.at[i, h], rsem.at[2 * i + h])
            for i, a in enumerate(arrays[:n_recv])
            for h in range(2)
        ]
        extras = arrays[n_recv + 1 :] if hidden else arrays[:n_recv] if self.carry else []
        copies += [
            pltpu.make_async_copy(
                a.at[:, pl.ds(self.at if hidden else 2 * n, LANES)], ebuf.at[i], rsem.at[2 * n_recv + i]
            )
            for i, a in enumerate(extras)
        ]
        if hidden:
            copies.append(pltpu.make_async_copy(arrays[n_recv], qbuf, rsem.at[2 * n_recv + len(extras)]))
        writes = []
        if self.carry:
            writes.append(pltpu.make_async_copy(cbuf, outs[0].at[:, pl.ds(2 * n, LANES)], osem.at[0, tiles]))
        if self.emit:
            writes.append(pltpu.make_async_copy(qbuf, outs[1], osem.at[1, tiles]))

        def begin():
            def step(j, m):
                for copy in weights(j, m, CUTS):
                    copy.start()

            over_tiles(step)

        def compute():
            for copy in copies:
                copy.wait()
            if hidden or self.carry:
                total = qbuf[:, :1] if hidden else row_squares(xbuf[...])
                for i in range(len(extras)):
                    total = total + carried(ebuf[i])
            if self.carry:
                cbuf[...] = to_carry(total)
                if self.emit:
                    qbuf[...] = jnp.broadcast_to(total, (rows, LANES))
                for copy in writes:
                    copy.start()
            if hidden:
                qbuf[...] = jnp.broadcast_to(lax.rsqrt(total / self.features + EPS), (rows, LANES))

            def step(j, m):
                for copy in weights(j, m):
                    copy.wait()
                both = jnp.dot(xbuf[...], wbuf[j, :, pl.ds(0, 2 * m)], preferred_element_type=jnp.float32)
                gate, up = both[:, :m], both[:, m:]
                columns = pl.ds(pl.multiple_of(j * GU_TILE, LANES), m)
                for r in range(n_recv):
                    gate = gate + rbuf[r, 0, :, columns].astype(jnp.float32)
                    up = up + rbuf[r, 1, :, columns].astype(jnp.float32)
                if hidden:
                    obuf[j, 0, :, pl.ds(0, m)] = silu_product(gate, up, qbuf[:, :1]).astype(jnp.bfloat16)
                else:
                    obuf[j, 0, :, pl.ds(0, m)] = gate.astype(jnp.bfloat16)
                    obuf[j, 1, :, pl.ds(0, m)] = up.astype(jnp.bfloat16)
                for copy in write(j, m):
                    copy.start()

            over_tiles(step)

        def drain():
            def step(j, m):
                for copy in write(j, m):
                    copy.wait()

            over_tiles(step)
            for copy in writes:
                copy.wait()

        return copies, begin, compute, drain


class Down:
    def __init__(self, parts, places, width, block, first, columns):
        self.parts, self.places, self.width, self.block = parts, places, width, block
        self.first, self.columns = first, columns
        self.group, self.rows = None, sum(part[0][0].shape[0] for part in parts)
        self.outs = [jax.ShapeDtypeStruct((block, columns), jnp.bfloat16) for _ in range(self.rows // block)]

    def fits(self, depth, columns):
        sizes = [a.shape[1] for part in self.parts for a, _, _ in part]
        whole = all(n % LANES == 0 for n in sizes) and self.width % (16 * CUTS) == 0
        return whole and self.columns % OUT_TILE == 0 and self.block % 16 == 0

    def arrays(self):
        return [a for part in self.parts for a, _, _ in part]

    def plain(self, table, gate_matrix, up_matrix, down_matrix):
        result = jnp.concatenate(
            [
                sum(
                    jnp.dot(
                        a,
                        lax.dynamic_slice_in_dim(
                            down_matrix[:, self.first : self.first + self.columns], table[place] + low, a.shape[1], 0
                        ),
                        preferred_element_type=jnp.float32,
                    )
                    for a, place, low in part
                )
                for part in self.parts
            ],
            axis=0,
        )
        return jnp.split(result.astype(jnp.bfloat16), len(self.outs))

    def scratch(self, depth):
        tiles, whole = self.columns // OUT_TILE, len(self.places) * self.width
        return [
            pltpu.VMEM((self.rows, whole), jnp.bfloat16),
            pltpu.VMEM((tiles, whole, OUT_TILE), jnp.bfloat16),
            pltpu.VMEM((tiles, self.rows, OUT_TILE), jnp.bfloat16),
            pltpu.SemaphoreType.DMA((len(self.arrays()),)),
            pltpu.SemaphoreType.DMA((len(self.places), tiles)),
            pltpu.SemaphoreType.DMA((len(self.outs), tiles)),
        ]

    def bind(self, refs, table, arrays, outs, scratch):
        hbuf, dbuf, obuf, hsem, dsem, osem = scratch
        block, width, tiles = self.block, self.width, self.columns // OUT_TILE

        def columns(j):
            return pl.ds(pl.multiple_of(j * OUT_TILE, LANES), OUT_TILE)

        def weights(p, j, cuts=1):
            taken = pl.ds(pl.multiple_of(self.first + j * OUT_TILE, LANES), OUT_TILE)
            each = width // cuts
            return [
                pltpu.make_async_copy(
                    refs["down"].at[pl.ds(pl.multiple_of(table[self.places[p]] + k * each, 16), each), taken],
                    dbuf.at[j, pl.ds(p * width + k * each, each)],
                    dsem.at[p, j],
                )
                for k in range(cuts)
            ]

        def write(i, j):
            return pltpu.make_async_copy(
                obuf.at[j, pl.ds(i * block, block)], outs[i].at[:, columns(j)], osem.at[i, j]
            )

        copies, row = [], 0
        for part in self.parts:
            rows = part[0][0].shape[0]
            for a, place, low in part:
                units = pl.ds(self.places.index(place) * width + low, a.shape[1])
                i = len(copies)
                copies.append(pltpu.make_async_copy(arrays[i], hbuf.at[pl.ds(row, rows), units], hsem.at[i]))
            row += rows

        def begin():
            @pl.loop(0, tiles)
            def _(j):
                for p in range(len(self.places)):
                    for copy in weights(p, j, CUTS):
                        copy.start()

        def compute():
            for copy in copies:
                copy.wait()

            @pl.loop(0, tiles)
            def _(j):
                for p in range(len(self.places)):
                    weights(p, j)[0].wait()
                result = jnp.dot(hbuf[...], dbuf[j], preferred_element_type=jnp.float32)
                obuf[j] = result.astype(jnp.bfloat16)
                for i in range(len(outs)):
                    write(i, j).start()

        def drain():
            @pl.loop(0, tiles)
            def _(j):
                for i in range(len(outs)):
                    write(i, j).wait()

        return copies, begin, compute, drain


def run(phases, table, gate_matrix, up_matrix, down_matrix, dep, work):
    depth, columns = gate_matrix.shape[0], down_matrix.shape[1]
    if not all(p.fits(depth, columns) for p in phases):
        return [p.plain(table, gate_matrix, up_matrix, down_matrix) for p in phases]
    operands = [gate_matrix, up_matrix, down_matrix]

    def index(array):
        for i, known in enumerate(operands):
            if known is array:
                return i
        operands.append(array)
        return len(operands) - 1

    groups = []
    for p in phases:
        if p.group is not None and all(p.group is not g for g in groups):
            groups.append(p.group)
    tok_places = [[index(t) for t in g.arrays()] for g in groups]
    where = [[index(a) for a in p.arrays()] for p in phases]
    index(dep)
    outs = [o for p in phases for o in p.outs]
    scratch = [p.scratch(depth) for p in phases]

    def kernel(table_ref, *args):
        args = list(args)
        arrays = [args.pop(0) for _ in operands]
        out_refs = [args.pop(0) for _ in outs]
        refs = {"gate": arrays[0], "up": arrays[1], "down": arrays[2], "x": {}}
        ready = {}
        for g, places in zip(groups, tok_places):
            xbuf, xsem = args.pop(0), args.pop(0)
            refs["x"][id(g)] = xbuf
            ready[id(g)] = [
                pltpu.make_async_copy(arrays[place], xbuf.at[pl.ds(j * g.block, g.block)], xsem.at[j])
                for j, place in enumerate(places)
            ]
        bound = []
        for p, places, buffers in zip(phases, where, scratch):
            mine = [out_refs.pop(0) for _ in p.outs]
            held = [args.pop(0) for _ in buffers]
            bound.append(p.bind(refs, table_ref, [arrays[i] for i in places], mine, held))
        for copies in ready.values():
            for copy in copies:
                copy.start()
        for copies, begin, _, _ in bound:
            for copy in copies:
                copy.start()
            begin()
        for p, (_, _, compute, _) in zip(phases, bound):
            for copy in ready.pop(id(p.group), []):
                copy.wait()
            compute()
        for _, _, _, drain in bound:
            drain()

    results = list(
        pl.pallas_call(
            kernel,
            out_shape=outs,
            in_specs=[SMEM] + [ANY] * len(operands),
            out_specs=[ANY] * len(outs),
            scratch_shapes=[
                *[
                    buffer
                    for g in groups
                    for buffer in (pltpu.VMEM((g.rows, depth), jnp.bfloat16), pltpu.SemaphoreType.DMA((len(g.names),)))
                ],
                *[buffer for buffers in scratch for buffer in buffers],
            ],
            compiler_params=pltpu.CompilerParams(vmem_limit_bytes=VMEM_LIMIT),
            cost_estimate=pl.CostEstimate(flops=work, bytes_accessed=1000, transcendentals=0),
            name="step_" + "".join("g" if p.group is not None else "d" for p in phases),
        )(table, *operands)
    )
    return [[results.pop(0) for _ in p.outs] for p in phases]


STEPS = (
    ("s0",),
    ("s1",),
    ("x0",),
    ("t", "x1"),
    ("p0", "s2"),
    ("p1", "s3", "long"),
    ("x2",),
    ("h0",),
    ("h1",),
    ("x3",),
    ("b", "s4"),
    ("h2", "long"),
    ("h3",),
    ("r0", "r1", "x4"),
    ("f0", "f1", "r2", "r3", "d1"),
    ("h4",),
    ("z", "r4", "d02"),
)


def cut(width, part, parts):
    unit = LANES if width % LANES == 0 else 1
    return width // unit * part // parts * unit


def on_device(n_gx, n_gy, tokens, gate_matrix, up_matrix, down_matrix):
    features = tokens.shape[1] * n_gx
    width = gate_matrix.shape[1] // n_gx
    block, columns = tokens.shape[0], down_matrix.shape[1]
    far = [2 * k for k in range(1, n_gx // 2)]

    def core(value):
        return swap(value, "gx", n_gx, 1)

    table = jnp.concatenate(
        [(lax.axis_index("gx") ^ jnp.arange(n_gx, dtype=jnp.int32)) * width, jnp.zeros((1,), jnp.int32)]
    )
    blocks = {0: tokens}
    sets = [[0], list(range(2, n_gy)), [1]]
    groups = [Group(blocks, js, block) for js in sets]
    squares = {}
    half = cut(width, 7, 13)
    early = cut(width, 7, 13)
    jobs = [(0, 0, early), (0, early, width - early), (1, 0, half), (1, half, width - half), (2, 0, width)]
    firsts = [min(i for i, job in enumerate(jobs) if job[0] == g) for g in range(len(groups))]
    state = [dict() for _ in jobs]
    totals = {}
    chain = tokens

    def phases_of(kind, job):
        g, low, n = jobs[job]
        group, st, first = groups[g], state[job], low == 0
        if kind == "s":
            return [GateUp(group, k ^ 1, low, n, carry=first and k > 0) for k in [*far, 0]]
        if kind == "x":
            return [
                GateUp(group, k, low, n, [st["lent"][i]], carry=first, emit=first and i == 0)
                for i, k in enumerate(far)
            ]
        if kind == "h":
            recvs = [st["lent"][-1], *st["far"]]
            return [GateUp(group, 0, low, n, recvs, squares=squares[g], at=2 * jobs[firsts[g]][2], features=features)]

    def down(gs, half):
        parts = [
            [(h, q, jobs[i][1]) for i, st in enumerate(state) if jobs[i][0] == g for h, q in st["pieces"]] for g in gs
        ]
        low, high = {"l": (0, columns // 2), "r": (columns // 2, columns)}.get(half, (0, columns))
        return Down(parts, list(range(n_gx)), width, block, low, high - low)

    def deliver(kind, job, outs):
        g, st = jobs[job][0], state[job]
        if kind == "s":
            st["lent"] = [core(o[0]) for o in outs]
        elif kind == "x":
            st["far"] = [swap(o[0], "gx", n_gx, k) for o, k in zip(outs, far)]
            if job == firsts[g]:
                squares[g] = (outs[0][1], st["far"])
        elif kind == "h":
            st["pieces"] = [(outs[0][0], 0), (core(outs[0][0]), 1)]
            st["crossed"] = [swap(outs[0][0], "gx", n_gx, k) for k in far]

    def tied(values):
        nonlocal chain
        values, chain = lax.optimization_barrier((values, chain))
        return values

    def forward(job):
        crossed = tied(state[job]["crossed"])
        state[job]["pieces"] += [(h, k) for h, k in zip(crossed, far)]
        state[job]["pieces"] += [(core(h), k ^ 1) for h, k in zip(crossed, far)]

    def reduce_over_gy():
        parts = dict(zip(sets[1], totals[1][0]))
        mask = 1
        while mask < n_gy:
            for j in [j for j in parts if j & mask]:
                arrived = swap(parts.pop(j), "gy", n_gy, mask)
                if j == mask:
                    landed.append(arrived)
                    continue
                arrived = tied(arrived).astype(jnp.float32)
                parts[j ^ mask] = (parts[j ^ mask].astype(jnp.float32) + arrived).astype(jnp.bfloat16)
            mask *= 2

    def gather_over_gy(mask):
        got = [j for j in blocks if j]
        blocks.update(zip(got, tied([blocks[j] for j in got])))
        for j in list(blocks) if mask > 1 else got:
            blocks[j ^ mask] = swap(blocks[j], "gy", n_gy, mask)

    landed = []
    mask = n_gy // 2
    gather_over_gy(mask)
    for names in STEPS:
        items, work = [], LONG if "long" in names else SHORT
        for name in names:
            if name == "long":
                continue
            kind, job = name[0], int(name[1:].rstrip("lr") or 0)
            if kind == "r":
                forward(job)
                continue
            while kind == "t" and mask > 1:
                mask //= 2
                gather_over_gy(mask)
            if kind == "p":
                state[job]["far"] = tied(state[job]["far"])
                if job == firsts[jobs[job][0]]:
                    squares[jobs[job][0]] = (squares[jobs[job][0]][0], state[job]["far"])
            if kind == "f":
                held, places = zip(*state[job]["pieces"])
                state[job]["pieces"] = list(zip(tied(list(held)), places))
            if kind == "b":
                blocks[1] = tied(swap(tokens, "gy", n_gy, 1))
            if kind == "z":
                reduce_over_gy()
            if kind in "tpfbz":
                continue
            if kind == "d":
                gs = [int(g) for g in name[1:] if g.isdigit()]
                items.append((kind, gs, [down(gs, name[-1])]))
            else:
                items.append((kind, job, phases_of(kind, job)))
        results = run([p for _, _, ps in items for p in ps], table, gate_matrix, up_matrix, down_matrix, chain, work)
        chain = results[0][0]
        for kind, job, ps in items:
            outs = [results.pop(0) for _ in ps]
            if kind != "d":
                deliver(kind, job, outs)
                continue
            for g in job:
                totals.setdefault(g, []).append([outs[0].pop(0) for _ in sets[g]])

    landed, last = lax.optimization_barrier((landed, totals[2][0][0]))
    landed.append(swap(last, "gy", n_gy, 1))
    return sum(part.astype(jnp.float32) for part in [totals[0][0][0], *landed]).astype(jnp.bfloat16)


def solution(mesh):
    n_gx, n_gy = mesh.shape["gx"], mesh.shape["gy"]
    placed = (P(("groups", "gy"), "gx"), P("gx", "gy"), P("gx", "gy"), P("gy", "gx"))
    return jax.shard_map(
        functools.partial(on_device, n_gx, n_gy),
        mesh=mesh,
        in_specs=placed,
        out_specs=P(("groups", "gy"), "gx"),
        check_vma=False,
    )
```

```python
import functools

import jax
import jax.numpy as jnp
from jax import lax
from jax.experimental import pallas as pl
from jax.experimental.pallas import tpu as pltpu
from jax.sharding import PartitionSpec as P

EPS = 1e-05
LANES = 128
GU_TILE = 512
OUT_TILE = 1024
CUTS = 4
SHORT, LONG = 1000, 10**11
VMEM_LIMIT = 64 * 1024 * 1024 - 64 * 1024
ANY = pl.BlockSpec(memory_space=pl.ANY)
SMEM = pl.BlockSpec(memory_space=pltpu.SMEM)


def swap(value, axis, size, mask):
    return lax.ppermute(value, axis, [(i, i ^ mask) for i in range(size)])


def silu_product(gate, up, scale):
    gate = gate * scale
    return gate / (1.0 + jnp.exp(-gate)) * (up * scale)


def row_squares(tok):
    values = tok.astype(jnp.float32)
    return jnp.sum(values * values, axis=1, keepdims=True)


def to_carry(total):
    high = total.astype(jnp.bfloat16).astype(jnp.float32)
    shape = (total.shape[0], LANES)
    first = lax.broadcasted_iota(jnp.int32, shape, 1) < LANES // 2
    return jnp.where(first, jnp.broadcast_to(high, shape), jnp.broadcast_to(total - high, shape)).astype(jnp.bfloat16)


def carried(columns):
    values = columns.astype(jnp.float32)
    return values[:, :1] + values[:, LANES // 2 : LANES // 2 + 1]


class Group:
    def __init__(self, blocks, names, block):
        self.blocks, self.names, self.block, self.rows = blocks, names, block, block * len(names)

    def arrays(self):
        return [self.blocks[name] for name in self.names]


class GateUp:
    def __init__(self, group, place, low, width, recvs=(), carry=False, emit=False, squares=None, at=0, features=1):
        self.group, self.place, self.low, self.width, self.recvs = group, place, low, width, list(recvs)
        self.carry, self.emit, self.squares, self.at, self.features = carry, emit, squares, at, features
        rows, wide = group.rows, width if squares else 2 * width + (LANES if carry else 0)
        self.outs = [jax.ShapeDtypeStruct((rows, wide), jnp.bfloat16)]
        if emit:
            self.outs.append(jax.ShapeDtypeStruct((rows, LANES), jnp.float32))

    def fits(self, depth, columns):
        return self.width % LANES == 0 and depth % (16 * CUTS) == 0 and self.group.block % 16 == 0

    def arrays(self):
        return [*self.recvs, *([self.squares[0], *self.squares[1]] if self.squares else [])]

    def plain(self, table, gate_matrix, up_matrix, down_matrix):
        tok, n = jnp.concatenate(self.group.arrays(), axis=0), self.width
        both = [
            jnp.dot(
                tok, lax.dynamic_slice_in_dim(m, table[self.place] + self.low, n, 1), preferred_element_type=jnp.float32
            )
            for m in (gate_matrix, up_matrix)
        ]
        both = jnp.concatenate(both, axis=1) + sum(r[:, : 2 * n].astype(jnp.float32) for r in self.recvs)
        if self.squares:
            total = self.squares[0][:, :1] + sum(carried(r[:, self.at : self.at + LANES]) for r in self.squares[1])
            scale = lax.rsqrt(total / self.features + EPS)
            return [silu_product(both[:, :n], both[:, n:], scale).astype(jnp.bfloat16)]
        if not self.carry:
            return [both.astype(jnp.bfloat16)]
        total = row_squares(tok) + sum(carried(r[:, 2 * n : 2 * n + LANES]) for r in self.recvs)
        result = jnp.concatenate([both.astype(jnp.bfloat16), to_carry(total)], axis=1)
        return [result] + ([jnp.broadcast_to(total, (tok.shape[0], LANES))] if self.emit else [])

    def scratch(self, depth):
        rows, n, tiles, n_recv = self.group.rows, self.width, pl.cdiv(self.width, GU_TILE), len(self.recvs)
        extra = len(self.squares[1]) if self.squares else n_recv if self.carry else 0
        return [
            pltpu.VMEM((tiles, depth, 2 * GU_TILE), jnp.bfloat16),
            pltpu.VMEM((n_recv, 2, rows, n) if n_recv else (1, 2, 16, LANES), jnp.bfloat16),
            pltpu.VMEM((extra, rows, LANES) if extra else (1, 16, LANES), jnp.bfloat16),
            pltpu.VMEM((rows, LANES) if self.squares or self.emit else (8, LANES), jnp.float32),
            pltpu.VMEM((tiles, 1 if self.squares else 2, rows, GU_TILE), jnp.bfloat16),
            pltpu.VMEM((rows if self.carry else 16, LANES), jnp.bfloat16),
            pltpu.SemaphoreType.DMA((2, tiles)),
            pltpu.SemaphoreType.DMA((2 * n_recv + extra + 1,)),
            pltpu.SemaphoreType.DMA((2, tiles + 1)),
        ]

    def bind(self, refs, table, arrays, outs, scratch):
        wbuf, rbuf, ebuf, qbuf, obuf, cbuf, wsem, rsem, osem = scratch
        n, rows, n_recv = self.width, self.group.rows, len(self.recvs)
        xbuf, hidden = refs["x"][id(self.group)], self.squares is not None
        full, rest = divmod(n, GU_TILE)
        tiles = full + (rest > 0)
        start = table[self.place] + self.low

        def weights(j, m, cuts=1):
            columns = pl.ds(pl.multiple_of(start + j * GU_TILE, LANES), m)
            rows_each = wbuf.shape[1] // cuts
            return [
                pltpu.make_async_copy(
                    refs[name].at[pl.ds(k * rows_each, rows_each), columns],
                    wbuf.at[j, pl.ds(k * rows_each, rows_each), pl.ds(i * m, m)],
                    wsem.at[i, j],
                )
                for k in range(cuts)
                for i, name in enumerate(("gate", "up"))
            ]

        def write(j, m):
            return [
                pltpu.make_async_copy(
                    obuf.at[j, i, :, pl.ds(0, m)],
                    outs[0].at[:, pl.ds(pl.multiple_of(i * n + j * GU_TILE, LANES), m)],
                    osem.at[i, j],
                )
                for i in range(1 if hidden else 2)
            ]

        def over_tiles(step):
            if full:
                @pl.loop(0, full)
                def _(j):
                    step(j, GU_TILE)
            if rest:
                step(full, rest)

        copies = [
            pltpu.make_async_copy(a.at[:, pl.ds(h * n, n)], rbuf.at[i, h], rsem.at[2 * i + h])
            for i, a in enumerate(arrays[:n_recv])
            for h in range(2)
        ]
        extras = arrays[n_recv + 1 :] if hidden else arrays[:n_recv] if self.carry else []
        copies += [
            pltpu.make_async_copy(
                a.at[:, pl.ds(self.at if hidden else 2 * n, LANES)], ebuf.at[i], rsem.at[2 * n_recv + i]
            )
            for i, a in enumerate(extras)
        ]
        if hidden:
            copies.append(pltpu.make_async_copy(arrays[n_recv], qbuf, rsem.at[2 * n_recv + len(extras)]))
        writes = []
        if self.carry:
            writes.append(pltpu.make_async_copy(cbuf, outs[0].at[:, pl.ds(2 * n, LANES)], osem.at[0, tiles]))
        if self.emit:
            writes.append(pltpu.make_async_copy(qbuf, outs[1], osem.at[1, tiles]))

        def begin():
            def step(j, m):
                for copy in weights(j, m, CUTS):
                    copy.start()

            over_tiles(step)

        def compute():
            for copy in copies:
                copy.wait()
            if hidden or self.carry:
                total = qbuf[:, :1] if hidden else row_squares(xbuf[...])
                for i in range(len(extras)):
                    total = total + carried(ebuf[i])
            if self.carry:
                cbuf[...] = to_carry(total)
                if self.emit:
                    qbuf[...] = jnp.broadcast_to(total, (rows, LANES))
                for copy in writes:
                    copy.start()
            if hidden:
                qbuf[...] = jnp.broadcast_to(lax.rsqrt(total / self.features + EPS), (rows, LANES))

            def step(j, m):
                for copy in weights(j, m):
                    copy.wait()
                both = jnp.dot(xbuf[...], wbuf[j, :, pl.ds(0, 2 * m)], preferred_element_type=jnp.float32)
                gate, up = both[:, :m], both[:, m:]
                columns = pl.ds(pl.multiple_of(j * GU_TILE, LANES), m)
                for r in range(n_recv):
                    gate = gate + rbuf[r, 0, :, columns].astype(jnp.float32)
                    up = up + rbuf[r, 1, :, columns].astype(jnp.float32)
                if hidden:
                    obuf[j, 0, :, pl.ds(0, m)] = silu_product(gate, up, qbuf[:, :1]).astype(jnp.bfloat16)
                else:
                    obuf[j, 0, :, pl.ds(0, m)] = gate.astype(jnp.bfloat16)
                    obuf[j, 1, :, pl.ds(0, m)] = up.astype(jnp.bfloat16)
                for copy in write(j, m):
                    copy.start()

            over_tiles(step)

        def drain():
            def step(j, m):
                for copy in write(j, m):
                    copy.wait()

            over_tiles(step)
            for copy in writes:
                copy.wait()

        return copies, begin, compute, drain


class Down:
    def __init__(self, parts, places, width, block, first, columns):
        self.parts, self.places, self.width, self.block = parts, places, width, block
        self.first, self.columns = first, columns
        self.group, self.rows = None, sum(part[0][0].shape[0] for part in parts)
        self.outs = [jax.ShapeDtypeStruct((block, columns), jnp.bfloat16) for _ in range(self.rows // block)]

    def fits(self, depth, columns):
        sizes = [a.shape[1] for part in self.parts for a, _, _ in part]
        whole = all(n % LANES == 0 for n in sizes) and self.width % (16 * CUTS) == 0
        return whole and self.columns % OUT_TILE == 0 and self.block % 16 == 0

    def arrays(self):
        return [a for part in self.parts for a, _, _ in part]

    def plain(self, table, gate_matrix, up_matrix, down_matrix):
        result = jnp.concatenate(
            [
                sum(
                    jnp.dot(
                        a,
                        lax.dynamic_slice_in_dim(
                            down_matrix[:, self.first : self.first + self.columns], table[place] + low, a.shape[1], 0
                        ),
                        preferred_element_type=jnp.float32,
                    )
                    for a, place, low in part
                )
                for part in self.parts
            ],
            axis=0,
        )
        return jnp.split(result.astype(jnp.bfloat16), len(self.outs))

    def scratch(self, depth):
        tiles, whole = self.columns // OUT_TILE, len(self.places) * self.width
        return [
            pltpu.VMEM((self.rows, whole), jnp.bfloat16),
            pltpu.VMEM((tiles, whole, OUT_TILE), jnp.bfloat16),
            pltpu.VMEM((tiles, self.rows, OUT_TILE), jnp.bfloat16),
            pltpu.SemaphoreType.DMA((len(self.arrays()),)),
            pltpu.SemaphoreType.DMA((len(self.places), tiles)),
            pltpu.SemaphoreType.DMA((len(self.outs), tiles)),
        ]

    def bind(self, refs, table, arrays, outs, scratch):
        hbuf, dbuf, obuf, hsem, dsem, osem = scratch
        block, width, tiles = self.block, self.width, self.columns // OUT_TILE

        def columns(j):
            return pl.ds(pl.multiple_of(j * OUT_TILE, LANES), OUT_TILE)

        def weights(p, j, cuts=1):
            taken = pl.ds(pl.multiple_of(self.first + j * OUT_TILE, LANES), OUT_TILE)
            each = width // cuts
            return [
                pltpu.make_async_copy(
                    refs["down"].at[pl.ds(pl.multiple_of(table[self.places[p]] + k * each, 16), each), taken],
                    dbuf.at[j, pl.ds(p * width + k * each, each)],
                    dsem.at[p, j],
                )
                for k in range(cuts)
            ]

        def write(i, j):
            return pltpu.make_async_copy(
                obuf.at[j, pl.ds(i * block, block)], outs[i].at[:, columns(j)], osem.at[i, j]
            )

        copies, row = [], 0
        for part in self.parts:
            rows = part[0][0].shape[0]
            for a, place, low in part:
                units = pl.ds(self.places.index(place) * width + low, a.shape[1])
                i = len(copies)
                copies.append(pltpu.make_async_copy(arrays[i], hbuf.at[pl.ds(row, rows), units], hsem.at[i]))
            row += rows

        def begin():
            @pl.loop(0, tiles)
            def _(j):
                for p in range(len(self.places)):
                    for copy in weights(p, j, CUTS):
                        copy.start()

        def compute():
            for copy in copies:
                copy.wait()

            @pl.loop(0, tiles)
            def _(j):
                for p in range(len(self.places)):
                    weights(p, j)[0].wait()
                result = jnp.dot(hbuf[...], dbuf[j], preferred_element_type=jnp.float32)
                obuf[j] = result.astype(jnp.bfloat16)
                for i in range(len(outs)):
                    write(i, j).start()

        def drain():
            @pl.loop(0, tiles)
            def _(j):
                for i in range(len(outs)):
                    write(i, j).wait()

        return copies, begin, compute, drain


def run(phases, table, gate_matrix, up_matrix, down_matrix, dep, work):
    depth, columns = gate_matrix.shape[0], down_matrix.shape[1]
    if not all(p.fits(depth, columns) for p in phases):
        return [p.plain(table, gate_matrix, up_matrix, down_matrix) for p in phases]
    operands = [gate_matrix, up_matrix, down_matrix]

    def index(array):
        for i, known in enumerate(operands):
            if known is array:
                return i
        operands.append(array)
        return len(operands) - 1

    groups = []
    for p in phases:
        if p.group is not None and all(p.group is not g for g in groups):
            groups.append(p.group)
    tok_places = [[index(t) for t in g.arrays()] for g in groups]
    where = [[index(a) for a in p.arrays()] for p in phases]
    index(dep)
    outs = [o for p in phases for o in p.outs]
    scratch = [p.scratch(depth) for p in phases]

    def kernel(table_ref, *args):
        args = list(args)
        arrays = [args.pop(0) for _ in operands]
        out_refs = [args.pop(0) for _ in outs]
        refs = {"gate": arrays[0], "up": arrays[1], "down": arrays[2], "x": {}}
        ready = {}
        for g, places in zip(groups, tok_places):
            xbuf, xsem = args.pop(0), args.pop(0)
            refs["x"][id(g)] = xbuf
            ready[id(g)] = [
                pltpu.make_async_copy(arrays[place], xbuf.at[pl.ds(j * g.block, g.block)], xsem.at[j])
                for j, place in enumerate(places)
            ]
        bound = []
        for p, places, buffers in zip(phases, where, scratch):
            mine = [out_refs.pop(0) for _ in p.outs]
            held = [args.pop(0) for _ in buffers]
            bound.append(p.bind(refs, table_ref, [arrays[i] for i in places], mine, held))
        for copies in ready.values():
            for copy in copies:
                copy.start()
        for copies, begin, _, _ in bound:
            for copy in copies:
                copy.start()
            begin()
        for p, (_, _, compute, _) in zip(phases, bound):
            for copy in ready.pop(id(p.group), []):
                copy.wait()
            compute()
        for _, _, _, drain in bound:
            drain()

    results = list(
        pl.pallas_call(
            kernel,
            out_shape=outs,
            in_specs=[SMEM] + [ANY] * len(operands),
            out_specs=[ANY] * len(outs),
            scratch_shapes=[
                *[
                    buffer
                    for g in groups
                    for buffer in (pltpu.VMEM((g.rows, depth), jnp.bfloat16), pltpu.SemaphoreType.DMA((len(g.names),)))
                ],
                *[buffer for buffers in scratch for buffer in buffers],
            ],
            compiler_params=pltpu.CompilerParams(vmem_limit_bytes=VMEM_LIMIT),
            cost_estimate=pl.CostEstimate(flops=work, bytes_accessed=1000, transcendentals=0),
            name="step_" + "".join("g" if p.group is not None else "d" for p in phases),
        )(table, *operands)
    )
    return [[results.pop(0) for _ in p.outs] for p in phases]


STEPS = (
    ("s0",),
    ("s1",),
    ("x0",),
    ("t", "x1"),
    ("p0", "s2"),
    ("p1", "s3", "long"),
    ("x2",),
    ("h0",),
    ("h1",),
    ("x3",),
    ("b", "s4"),
    ("h2", "long"),
    ("h3",),
    ("r0", "r1", "x4"),
    ("f0", "f1", "r2", "r3", "d1"),
    ("h4",),
    ("z", "r4", "d02"),
)


def cut(width, part, parts):
    unit = LANES if width % LANES == 0 else 1
    return width // unit * part // parts * unit


def on_device(n_gx, n_gy, tokens, gate_matrix, up_matrix, down_matrix):
    features = tokens.shape[1] * n_gx
    width = gate_matrix.shape[1] // n_gx
    block, columns = tokens.shape[0], down_matrix.shape[1]
    far = [2 * k for k in range(1, n_gx // 2)]

    def core(value):
        return swap(value, "gx", n_gx, 1)

    table = jnp.concatenate(
        [(lax.axis_index("gx") ^ jnp.arange(n_gx, dtype=jnp.int32)) * width, jnp.zeros((1,), jnp.int32)]
    )
    blocks = {0: tokens}
    sets = [[0], list(range(2, n_gy)), [1]]
    groups = [Group(blocks, js, block) for js in sets]
    squares = {}
    half = cut(width, 7, 13)
    early = cut(width, 7, 13)
    jobs = [(0, 0, early), (0, early, width - early), (1, 0, half), (1, half, width - half), (2, 0, width)]
    firsts = [min(i for i, job in enumerate(jobs) if job[0] == g) for g in range(len(groups))]
    state = [dict() for _ in jobs]
    totals = {}
    chain = tokens

    def phases_of(kind, job):
        g, low, n = jobs[job]
        group, st, first = groups[g], state[job], low == 0
        if kind == "s":
            return [GateUp(group, k ^ 1, low, n, carry=first and k > 0) for k in [*far, 0]]
        if kind == "x":
            return [
                GateUp(group, k, low, n, [st["lent"][i]], carry=first, emit=first and i == 0)
                for i, k in enumerate(far)
            ]
        if kind == "h":
            recvs = [st["lent"][-1], *st["far"]]
            return [GateUp(group, 0, low, n, recvs, squares=squares[g], at=2 * jobs[firsts[g]][2], features=features)]

    def down(gs, half):
        parts = [
            [(h, q, jobs[i][1]) for i, st in enumerate(state) if jobs[i][0] == g for h, q in st["pieces"]] for g in gs
        ]
        low, high = {"l": (0, columns // 2), "r": (columns // 2, columns)}.get(half, (0, columns))
        return Down(parts, list(range(n_gx)), width, block, low, high - low)

    def deliver(kind, job, outs):
        g, st = jobs[job][0], state[job]
        if kind == "s":
            st["lent"] = [core(o[0]) for o in outs]
        elif kind == "x":
            st["far"] = [swap(o[0], "gx", n_gx, k) for o, k in zip(outs, far)]
            if job == firsts[g]:
                squares[g] = (outs[0][1], st["far"])
        elif kind == "h":
            st["pieces"] = [(outs[0][0], 0), (core(outs[0][0]), 1)]
            st["crossed"] = [swap(outs[0][0], "gx", n_gx, k) for k in far]

    def tied(values):
        nonlocal chain
        values, chain = lax.optimization_barrier((values, chain))
        return values

    def forward(job):
        crossed = tied(state[job]["crossed"])
        state[job]["pieces"] += [(h, k) for h, k in zip(crossed, far)]
        state[job]["pieces"] += [(core(h), k ^ 1) for h, k in zip(crossed, far)]

    def reduce_over_gy():
        parts = dict(zip(sets[1], totals[1][0]))
        mask = 1
        while mask < n_gy:
            for j in [j for j in parts if j & mask]:
                arrived = swap(parts.pop(j), "gy", n_gy, mask)
                if j == mask:
                    landed.append(arrived)
                    continue
                arrived = tied(arrived).astype(jnp.float32)
                parts[j ^ mask] = (parts[j ^ mask].astype(jnp.float32) + arrived).astype(jnp.bfloat16)
            mask *= 2

    def gather_over_gy(mask):
        got = [j for j in blocks if j]
        blocks.update(zip(got, tied([blocks[j] for j in got])))
        for j in list(blocks) if mask > 1 else got:
            blocks[j ^ mask] = swap(blocks[j], "gy", n_gy, mask)

    landed = []
    mask = n_gy // 2
    gather_over_gy(mask)
    for names in STEPS:
        items, work = [], LONG if "long" in names else SHORT
        for name in names:
            if name == "long":
                continue
            kind, job = name[0], int(name[1:].rstrip("lr") or 0)
            if kind == "r":
                forward(job)
                continue
            while kind == "t" and mask > 1:
                mask //= 2
                gather_over_gy(mask)
            if kind == "p":
                state[job]["far"] = tied(state[job]["far"])
                if job == firsts[jobs[job][0]]:
                    squares[jobs[job][0]] = (squares[jobs[job][0]][0], state[job]["far"])
            if kind == "f":
                held, places = zip(*state[job]["pieces"])
                state[job]["pieces"] = list(zip(tied(list(held)), places))
            if kind == "b":
                blocks[1] = tied(swap(tokens, "gy", n_gy, 1))
            if kind == "z":
                reduce_over_gy()
            if kind in "tpfbz":
                continue
            if kind == "d":
                gs = [int(g) for g in name[1:] if g.isdigit()]
                items.append((kind, gs, [down(gs, name[-1])]))
            else:
                items.append((kind, job, phases_of(kind, job)))
        results = run([p for _, _, ps in items for p in ps], table, gate_matrix, up_matrix, down_matrix, chain, work)
        chain = results[0][0]
        for kind, job, ps in items:
            outs = [results.pop(0) for _ in ps]
            if kind != "d":
                deliver(kind, job, outs)
                continue
            for g in job:
                totals.setdefault(g, []).append([outs[0].pop(0) for _ in sets[g]])

    landed, last = lax.optimization_barrier((landed, totals[2][0][0]))
    landed.append(swap(last, "gy", n_gy, 1))
    return sum(part.astype(jnp.float32) for part in [totals[0][0][0], *landed]).astype(jnp.bfloat16)


def solution(mesh):
    n_gx, n_gy = mesh.shape["gx"], mesh.shape["gy"]
    placed = (P(("groups", "gy"), "gx"), P("gx", "gy"), P("gx", "gy"), P("gy", "gx"))
    return jax.shard_map(
        functools.partial(on_device, n_gx, n_gy),
        mesh=mesh,
        in_specs=placed,
        out_specs=P(("groups", "gy"), "gx"),
        check_vma=False,
    )
```

```python
import functools

import jax
import jax.numpy as jnp
from jax import lax
from jax.experimental import pallas as pl
from jax.experimental.pallas import tpu as pltpu
from jax.sharding import PartitionSpec as P

EPS = 1e-05
LANES = 128
GU_TILE = 256
OUT_TILE = 512
CUTS = 4
SHORT, LONG = 1000, 10**11
VMEM_LIMIT = 64 * 1024 * 1024 - 64 * 1024
ANY = pl.BlockSpec(memory_space=pl.ANY)
SMEM = pl.BlockSpec(memory_space=pltpu.SMEM)


def swap(value, axis, size, mask):
    return lax.ppermute(value, axis, [(i, i ^ mask) for i in range(size)])


def silu_product(gate, up, scale):
    gate = gate * scale
    return gate / (1.0 + jnp.exp(-gate)) * (up * scale)


def row_squares(tok):
    values = tok.astype(jnp.float32)
    return jnp.sum(values * values, axis=1, keepdims=True)


def to_carry(total):
    high = total.astype(jnp.bfloat16).astype(jnp.float32)
    shape = (total.shape[0], LANES)
    first = lax.broadcasted_iota(jnp.int32, shape, 1) < LANES // 2
    return jnp.where(first, jnp.broadcast_to(high, shape), jnp.broadcast_to(total - high, shape)).astype(jnp.bfloat16)


def carried(columns):
    values = columns.astype(jnp.float32)
    return values[:, :1] + values[:, LANES // 2 : LANES // 2 + 1]


class Group:
    def __init__(self, blocks, names, block):
        self.blocks, self.names, self.block, self.rows = blocks, names, block, block * len(names)

    def arrays(self):
        return [self.blocks[name] for name in self.names]


class GateUp:
    def __init__(self, group, place, low, width, recvs=(), carry=False, emit=False, squares=None, at=0, features=1):
        self.group, self.place, self.low, self.width, self.recvs = group, place, low, width, list(recvs)
        self.carry, self.emit, self.squares, self.at, self.features = carry, emit, squares, at, features
        rows, wide = group.rows, width if squares else 2 * width + (LANES if carry else 0)
        self.outs = [jax.ShapeDtypeStruct((rows, wide), jnp.bfloat16)]
        if emit:
            self.outs.append(jax.ShapeDtypeStruct((rows, LANES), jnp.float32))

    def fits(self, depth, columns):
        return self.width % LANES == 0 and depth % (16 * CUTS) == 0 and self.group.block % 16 == 0

    def arrays(self):
        return [*self.recvs, *([self.squares[0], *self.squares[1]] if self.squares else [])]

    def plain(self, table, gate_matrix, up_matrix, down_matrix):
        tok, n = jnp.concatenate(self.group.arrays(), axis=0), self.width
        both = [
            jnp.dot(
                tok, lax.dynamic_slice_in_dim(m, table[self.place] + self.low, n, 1), preferred_element_type=jnp.float32
            )
            for m in (gate_matrix, up_matrix)
        ]
        both = jnp.concatenate(both, axis=1) + sum(r[:, : 2 * n].astype(jnp.float32) for r in self.recvs)
        if self.squares:
            total = self.squares[0][:, :1] + sum(carried(r[:, self.at : self.at + LANES]) for r in self.squares[1])
            scale = lax.rsqrt(total / self.features + EPS)
            return [silu_product(both[:, :n], both[:, n:], scale).astype(jnp.bfloat16)]
        if not self.carry:
            return [both.astype(jnp.bfloat16)]
        total = row_squares(tok) + sum(carried(r[:, 2 * n : 2 * n + LANES]) for r in self.recvs)
        result = jnp.concatenate([both.astype(jnp.bfloat16), to_carry(total)], axis=1)
        return [result] + ([jnp.broadcast_to(total, (tok.shape[0], LANES))] if self.emit else [])

    def scratch(self, depth):
        rows, n, tiles, n_recv = self.group.rows, self.width, pl.cdiv(self.width, GU_TILE), len(self.recvs)
        extra = len(self.squares[1]) if self.squares else n_recv if self.carry else 0
        return [
            pltpu.VMEM((tiles, depth, 2 * GU_TILE), jnp.bfloat16),
            pltpu.VMEM((n_recv, 2, rows, tiles * GU_TILE) if n_recv else (1, 2, 16, LANES), jnp.bfloat16),
            pltpu.VMEM((extra, rows, LANES) if extra else (1, 16, LANES), jnp.bfloat16),
            pltpu.VMEM((rows, LANES) if self.squares or self.emit else (8, LANES), jnp.float32),
            pltpu.VMEM((tiles, 1 if self.squares else 2, rows, GU_TILE), jnp.bfloat16),
            pltpu.VMEM((rows if self.carry else 16, LANES), jnp.bfloat16),
            pltpu.SemaphoreType.DMA((2, tiles)),
            pltpu.SemaphoreType.DMA((2 * n_recv + extra + 1,)),
            pltpu.SemaphoreType.DMA((2, tiles + 1)),
        ]

    def bind(self, refs, table, arrays, outs, scratch):
        wbuf, rbuf, ebuf, qbuf, obuf, cbuf, wsem, rsem, osem = scratch
        n, rows, n_recv = self.width, self.group.rows, len(self.recvs)
        xbuf, hidden = refs["x"][id(self.group)], self.squares is not None
        full, rest = divmod(n, GU_TILE)
        tiles = full + (rest > 0)
        start = table[self.place] + self.low

        def weights(j, m, cuts=1):
            columns = pl.ds(pl.multiple_of(start + j * GU_TILE, LANES), m)
            rows_each = wbuf.shape[1] // cuts
            return [
                pltpu.make_async_copy(
                    refs[name].at[pl.ds(k * rows_each, rows_each), columns],
                    wbuf.at[j, pl.ds(k * rows_each, rows_each), pl.ds(i * GU_TILE, m)],
                    wsem.at[i, j],
                )
                for k in range(cuts)
                for i, name in enumerate(("gate", "up"))
            ]

        def write(j, m):
            return [
                pltpu.make_async_copy(
                    obuf.at[j, i, :, pl.ds(0, m)],
                    outs[0].at[:, pl.ds(pl.multiple_of(i * n + j * GU_TILE, LANES), m)],
                    osem.at[i, j],
                )
                for i in range(1 if hidden else 2)
            ]

        def over_tiles(step):
            if full:
                @pl.loop(0, full)
                def _(j):
                    step(j, GU_TILE)
            if rest:
                step(full, rest)

        copies = [
            pltpu.make_async_copy(a.at[:, pl.ds(h * n, n)], rbuf.at[i, h, :, pl.ds(0, n)], rsem.at[2 * i + h])
            for i, a in enumerate(arrays[:n_recv])
            for h in range(2)
        ]
        extras = arrays[n_recv + 1 :] if hidden else arrays[:n_recv] if self.carry else []
        copies += [
            pltpu.make_async_copy(
                a.at[:, pl.ds(self.at if hidden else 2 * n, LANES)], ebuf.at[i], rsem.at[2 * n_recv + i]
            )
            for i, a in enumerate(extras)
        ]
        if hidden:
            copies.append(pltpu.make_async_copy(arrays[n_recv], qbuf, rsem.at[2 * n_recv + len(extras)]))
        writes = []
        if self.carry:
            writes.append(pltpu.make_async_copy(cbuf, outs[0].at[:, pl.ds(2 * n, LANES)], osem.at[0, tiles]))
        if self.emit:
            writes.append(pltpu.make_async_copy(qbuf, outs[1], osem.at[1, tiles]))

        def begin():
            def step(j, m):
                for copy in weights(j, m, CUTS):
                    copy.start()

            over_tiles(step)

        def compute():
            for copy in copies:
                copy.wait()
            if hidden or self.carry:
                total = qbuf[:, :1] if hidden else row_squares(xbuf[...])
                for i in range(len(extras)):
                    total = total + carried(ebuf[i])
            if self.carry:
                cbuf[...] = to_carry(total)
                if self.emit:
                    qbuf[...] = jnp.broadcast_to(total, (rows, LANES))
                for copy in writes:
                    copy.start()
            if hidden:
                qbuf[...] = jnp.broadcast_to(lax.rsqrt(total / self.features + EPS), (rows, LANES))

            def with_width(j, step):
                if not rest:
                    return step(j, GU_TILE)
                if full:
                    pl.when(j < full)(lambda: step(j, GU_TILE))
                pl.when(j == full)(lambda: step(full, rest))

            def wait(j, m):
                for copy in weights(j, m):
                    copy.wait()

            def send(j, m):
                for copy in write(j, m):
                    copy.start()

            @pl.loop(0, tiles)
            def _(j):
                with_width(j, wait)
                both = jnp.dot(xbuf[...], wbuf[j], preferred_element_type=jnp.float32)
                gate, up = both[:, :GU_TILE], both[:, GU_TILE:]
                columns = pl.ds(pl.multiple_of(j * GU_TILE, LANES), GU_TILE)
                for r in range(n_recv):
                    gate = gate + rbuf[r, 0, :, columns].astype(jnp.float32)
                    up = up + rbuf[r, 1, :, columns].astype(jnp.float32)
                if hidden:
                    obuf[j, 0] = silu_product(gate, up, qbuf[:, :1]).astype(jnp.bfloat16)
                else:
                    obuf[j, 0] = gate.astype(jnp.bfloat16)
                    obuf[j, 1] = up.astype(jnp.bfloat16)
                with_width(j, send)

        def drain():
            def step(j, m):
                for copy in write(j, m):
                    copy.wait()

            over_tiles(step)
            for copy in writes:
                copy.wait()

        return copies, begin, compute, drain


class Down:
    def __init__(self, parts, places, width, block, first, columns):
        self.parts, self.places, self.width, self.block = parts, places, width, block
        self.first, self.columns = first, columns
        self.group, self.rows = None, sum(part[0][0].shape[0] for part in parts)
        self.outs = [jax.ShapeDtypeStruct((block, columns), jnp.bfloat16) for _ in range(self.rows // block)]

    def fits(self, depth, columns):
        sizes = [a.shape[1] for part in self.parts for a, _, _ in part]
        whole = all(n % LANES == 0 for n in sizes) and self.width % (16 * CUTS) == 0
        return whole and self.columns % OUT_TILE == 0 and self.block % 16 == 0

    def arrays(self):
        return [a for part in self.parts for a, _, _ in part]

    def plain(self, table, gate_matrix, up_matrix, down_matrix):
        result = jnp.concatenate(
            [
                sum(
                    jnp.dot(
                        a,
                        lax.dynamic_slice_in_dim(
                            down_matrix[:, self.first : self.first + self.columns], table[place] + low, a.shape[1], 0
                        ),
                        preferred_element_type=jnp.float32,
                    )
                    for a, place, low in part
                )
                for part in self.parts
            ],
            axis=0,
        )
        return jnp.split(result.astype(jnp.bfloat16), len(self.outs))

    def scratch(self, depth):
        tiles, whole = self.columns // OUT_TILE, len(self.places) * self.width
        return [
            pltpu.VMEM((self.rows, whole), jnp.bfloat16),
            pltpu.VMEM((tiles, whole, OUT_TILE), jnp.bfloat16),
            pltpu.VMEM((tiles, self.rows, OUT_TILE), jnp.bfloat16),
            pltpu.SemaphoreType.DMA((len(self.arrays()),)),
            pltpu.SemaphoreType.DMA((len(self.places), tiles)),
            pltpu.SemaphoreType.DMA((len(self.outs), tiles)),
        ]

    def bind(self, refs, table, arrays, outs, scratch):
        hbuf, dbuf, obuf, hsem, dsem, osem = scratch
        block, width, tiles = self.block, self.width, self.columns // OUT_TILE

        def columns(j):
            return pl.ds(pl.multiple_of(j * OUT_TILE, LANES), OUT_TILE)

        def weights(p, j, cuts=1):
            taken = pl.ds(pl.multiple_of(self.first + j * OUT_TILE, LANES), OUT_TILE)
            each = width // cuts
            return [
                pltpu.make_async_copy(
                    refs["down"].at[pl.ds(pl.multiple_of(table[self.places[p]] + k * each, 16), each), taken],
                    dbuf.at[j, pl.ds(p * width + k * each, each)],
                    dsem.at[p, j],
                )
                for k in range(cuts)
            ]

        def write(i, j):
            return pltpu.make_async_copy(
                obuf.at[j, pl.ds(i * block, block)], outs[i].at[:, columns(j)], osem.at[i, j]
            )

        copies, row = [], 0
        for part in self.parts:
            rows = part[0][0].shape[0]
            for a, place, low in part:
                units = pl.ds(self.places.index(place) * width + low, a.shape[1])
                i = len(copies)
                copies.append(pltpu.make_async_copy(arrays[i], hbuf.at[pl.ds(row, rows), units], hsem.at[i]))
            row += rows

        def begin():
            @pl.loop(0, tiles)
            def _(j):
                for p in range(len(self.places)):
                    for copy in weights(p, j, CUTS):
                        copy.start()

        def compute():
            for copy in copies:
                copy.wait()

            @pl.loop(0, tiles)
            def _(j):
                for p in range(len(self.places)):
                    weights(p, j)[0].wait()
                result = jnp.dot(hbuf[...], dbuf[j], preferred_element_type=jnp.float32)
                obuf[j] = result.astype(jnp.bfloat16)
                for i in range(len(outs)):
                    write(i, j).start()

        def drain():
            @pl.loop(0, tiles)
            def _(j):
                for i in range(len(outs)):
                    write(i, j).wait()

        return copies, begin, compute, drain


def run(phases, table, gate_matrix, up_matrix, down_matrix, dep, work):
    depth, columns = gate_matrix.shape[0], down_matrix.shape[1]
    if not all(p.fits(depth, columns) for p in phases):
        return [p.plain(table, gate_matrix, up_matrix, down_matrix) for p in phases]
    operands = [gate_matrix, up_matrix, down_matrix]

    def index(array):
        for i, known in enumerate(operands):
            if known is array:
                return i
        operands.append(array)
        return len(operands) - 1

    groups = []
    for p in phases:
        if p.group is not None and all(p.group is not g for g in groups):
            groups.append(p.group)
    tok_places = [[index(t) for t in g.arrays()] for g in groups]
    where = [[index(a) for a in p.arrays()] for p in phases]
    index(dep)
    outs = [o for p in phases for o in p.outs]
    scratch = [p.scratch(depth) for p in phases]

    def kernel(table_ref, *args):
        args = list(args)
        arrays = [args.pop(0) for _ in operands]
        out_refs = [args.pop(0) for _ in outs]
        refs = {"gate": arrays[0], "up": arrays[1], "down": arrays[2], "x": {}}
        ready = {}
        for g, places in zip(groups, tok_places):
            xbuf, xsem = args.pop(0), args.pop(0)
            refs["x"][id(g)] = xbuf
            ready[id(g)] = [
                pltpu.make_async_copy(arrays[place], xbuf.at[pl.ds(j * g.block, g.block)], xsem.at[j])
                for j, place in enumerate(places)
            ]
        bound = []
        for p, places, buffers in zip(phases, where, scratch):
            mine = [out_refs.pop(0) for _ in p.outs]
            held = [args.pop(0) for _ in buffers]
            bound.append(p.bind(refs, table_ref, [arrays[i] for i in places], mine, held))
        for copies in ready.values():
            for copy in copies:
                copy.start()
        for copies, begin, _, _ in bound:
            for copy in copies:
                copy.start()
            begin()
        for p, (_, _, compute, _) in zip(phases, bound):
            for copy in ready.pop(id(p.group), []):
                copy.wait()
            compute()
        for _, _, _, drain in bound:
            drain()

    results = list(
        pl.pallas_call(
            kernel,
            out_shape=outs,
            in_specs=[SMEM] + [ANY] * len(operands),
            out_specs=[ANY] * len(outs),
            scratch_shapes=[
                *[
                    buffer
                    for g in groups
                    for buffer in (pltpu.VMEM((g.rows, depth), jnp.bfloat16), pltpu.SemaphoreType.DMA((len(g.names),)))
                ],
                *[buffer for buffers in scratch for buffer in buffers],
            ],
            compiler_params=pltpu.CompilerParams(vmem_limit_bytes=VMEM_LIMIT),
            cost_estimate=pl.CostEstimate(flops=work, bytes_accessed=1000, transcendentals=0),
            name="step_" + "".join("g" if p.group is not None else "d" for p in phases),
        )(table, *operands)
    )
    return [[results.pop(0) for _ in p.outs] for p in phases]


STEPS = (
    ("s0",),
    ("s1",),
    ("x0",),
    ("t", "x1"),
    ("p0", "s2"),
    ("p1", "s3", "long"),
    ("x2",),
    ("h0",),
    ("h1",),
    ("x3",),
    ("b", "s4"),
    ("h2", "long"),
    ("h3",),
    ("r0", "r1", "x4"),
    ("f0", "f1", "r2", "r3", "d1"),
    ("h4",),
    ("z", "r4", "d02"),
)


def cut(width, part, parts):
    unit = LANES if width % LANES == 0 else 1
    return width // unit * part // parts * unit


def on_device(n_gx, n_gy, tokens, gate_matrix, up_matrix, down_matrix):
    features = tokens.shape[1] * n_gx
    width = gate_matrix.shape[1] // n_gx
    block, columns = tokens.shape[0], down_matrix.shape[1]
    far = [2 * k for k in range(1, n_gx // 2)]

    def core(value):
        return swap(value, "gx", n_gx, 1)

    table = jnp.concatenate(
        [(lax.axis_index("gx") ^ jnp.arange(n_gx, dtype=jnp.int32)) * width, jnp.zeros((1,), jnp.int32)]
    )
    blocks = {0: tokens}
    sets = [[0], list(range(2, n_gy)), [1]]
    groups = [Group(blocks, js, block) for js in sets]
    squares = {}
    half = cut(width, 7, 13)
    early = cut(width, 7, 13)
    jobs = [(0, 0, early), (0, early, width - early), (1, 0, half), (1, half, width - half), (2, 0, width)]
    firsts = [min(i for i, job in enumerate(jobs) if job[0] == g) for g in range(len(groups))]
    state = [dict() for _ in jobs]
    totals = {}
    chain = tokens

    def phases_of(kind, job):
        g, low, n = jobs[job]
        group, st, first = groups[g], state[job], low == 0
        if kind == "s":
            return [GateUp(group, k ^ 1, low, n, carry=first and k > 0) for k in [*far, 0]]
        if kind == "x":
            return [
                GateUp(group, k, low, n, [st["lent"][i]], carry=first, emit=first and i == 0)
                for i, k in enumerate(far)
            ]
        if kind == "h":
            recvs = [st["lent"][-1], *st["far"]]
            return [GateUp(group, 0, low, n, recvs, squares=squares[g], at=2 * jobs[firsts[g]][2], features=features)]

    def down(gs, half):
        parts = [
            [(h, q, jobs[i][1]) for i, st in enumerate(state) if jobs[i][0] == g for h, q in st["pieces"]] for g in gs
        ]
        low, high = {"l": (0, columns // 2), "r": (columns // 2, columns)}.get(half, (0, columns))
        return Down(parts, list(range(n_gx)), width, block, low, high - low)

    def deliver(kind, job, outs):
        g, st = jobs[job][0], state[job]
        if kind == "s":
            st["lent"] = [core(o[0]) for o in outs]
        elif kind == "x":
            st["far"] = [swap(o[0], "gx", n_gx, k) for o, k in zip(outs, far)]
            if job == firsts[g]:
                squares[g] = (outs[0][1], st["far"])
        elif kind == "h":
            st["pieces"] = [(outs[0][0], 0), (core(outs[0][0]), 1)]
            st["crossed"] = [swap(outs[0][0], "gx", n_gx, k) for k in far]

    def tied(values):
        nonlocal chain
        values, chain = lax.optimization_barrier((values, chain))
        return values

    def forward(job):
        crossed = tied(state[job]["crossed"])
        state[job]["pieces"] += [(h, k) for h, k in zip(crossed, far)]
        state[job]["pieces"] += [(core(h), k ^ 1) for h, k in zip(crossed, far)]

    def reduce_over_gy():
        parts = dict(zip(sets[1], totals[1][0]))
        mask = 1
        while mask < n_gy:
            for j in [j for j in parts if j & mask]:
                arrived = swap(parts.pop(j), "gy", n_gy, mask)
                if j == mask:
                    landed.append(arrived)
                    continue
                arrived = tied(arrived).astype(jnp.float32)
                parts[j ^ mask] = (parts[j ^ mask].astype(jnp.float32) + arrived).astype(jnp.bfloat16)
            mask *= 2

    def gather_over_gy(mask):
        got = [j for j in blocks if j]
        blocks.update(zip(got, tied([blocks[j] for j in got])))
        for j in list(blocks) if mask > 1 else got:
            blocks[j ^ mask] = swap(blocks[j], "gy", n_gy, mask)

    landed = []
    mask = n_gy // 2
    gather_over_gy(mask)
    for names in STEPS:
        items, work = [], LONG if "long" in names else SHORT
        for name in names:
            if name == "long":
                continue
            kind, job = name[0], int(name[1:].rstrip("lr") or 0)
            if kind == "r":
                forward(job)
                continue
            while kind == "t" and mask > 1:
                mask //= 2
                gather_over_gy(mask)
            if kind == "p":
                state[job]["far"] = tied(state[job]["far"])
                if job == firsts[jobs[job][0]]:
                    squares[jobs[job][0]] = (squares[jobs[job][0]][0], state[job]["far"])
            if kind == "f":
                held, places = zip(*state[job]["pieces"])
                state[job]["pieces"] = list(zip(tied(list(held)), places))
            if kind == "b":
                blocks[1] = tied(swap(tokens, "gy", n_gy, 1))
            if kind == "z":
                reduce_over_gy()
            if kind in "tpfbz":
                continue
            if kind == "d":
                gs = [int(g) for g in name[1:] if g.isdigit()]
                items.append((kind, gs, [down(gs, name[-1])]))
            else:
                items.append((kind, job, phases_of(kind, job)))
        results = run([p for _, _, ps in items for p in ps], table, gate_matrix, up_matrix, down_matrix, chain, work)
        chain = results[0][0]
        for kind, job, ps in items:
            outs = [results.pop(0) for _ in ps]
            if kind != "d":
                deliver(kind, job, outs)
                continue
            for g in job:
                totals.setdefault(g, []).append([outs[0].pop(0) for _ in sets[g]])

    landed, last = lax.optimization_barrier((landed, totals[2][0][0]))
    landed.append(swap(last, "gy", n_gy, 1))
    return sum(part.astype(jnp.float32) for part in [totals[0][0][0], *landed]).astype(jnp.bfloat16)


def solution(mesh):
    n_gx, n_gy = mesh.shape["gx"], mesh.shape["gy"]
    placed = (P(("groups", "gy"), "gx"), P("gx", "gy"), P("gx", "gy"), P("gy", "gx"))
    return jax.shard_map(
        functools.partial(on_device, n_gx, n_gy),
        mesh=mesh,
        in_specs=placed,
        out_specs=P(("groups", "gy"), "gx"),
        check_vma=False,
    )
```
